256 devices in a mesh: section: 4 (over y_lo, core), dp: 64 (over z, x, y_hi).
Axes of the slice: x: 4, y: 4 (y_hi: 2, y_lo: 2; y = y_hi * 2 + y_lo), z: 8, core: 2. Of those that a mesh axis runs over, the one named last changes fastest.
Arguments:
- token_ids: int32 [8192], P('dp'), may hold values from 0 to 64511, as said below
- embed_table: bfloat16 [64512, 8192], P('dp', 'section'), may hold values from -6 to 6
- subspace: bfloat16 [4, 8192, 256], P('section'), may hold values from -0.0625 to 0.0625
- adapter_in: bfloat16 [4, 8192, 128], P('section'), may hold values from -0.0625 to 0.0625
- adapter_out: bfloat16 [4, 128, 8192], P('section'), may hold values from -0.5 to 0.5
- norm_gain: float32 [4, 8192], P('section'), may hold values from 0.1 to 1.9
- coef_cotangent: bfloat16 [8192, 256], P('dp'), may hold values from -0.059814453 to 0.059814453
Outputs:
- sent_coefs: bfloat16 [4, 8192, 256], P('section', 'dp')
- grad_adapter_in: float32 [4, 8192, 128], P('section', 'dp')
- grad_adapter_out: float32 [4, 128, 8192], P('section', None, 'dp')
- grad_norm_gain: float32 [4, 8192], P('section', 'dp')
The draws below stay inside these ranges and needn't reach their ends.
Inputs may be any that keep to these rules, and one draw needn't show every extreme that they name: `token_ids`: an id i lies in table shard i // 1008. In each aligned block of 128 ids (the ids of one device) no shard is named by more than 4 ids; one shard is named by exactly 4 ids in every block, and in most blocks a second shard as well.
All inputs are finite; a program needn't handle non-finite values.
Results may differ from the reference program's by a relative error of at most 0.017.
Values may be sent and summed in bfloat16 or wider, within the bound.
No kernel may reach another device: no remote copies, remote signals or barrier semaphores. Data moves between devices by JAX's collectives and lax.ppermute only.
A program may use at most 128 MiB of HBM per device.

```python
import jax
import jax.numpy as jnp
from jax import lax

D = 8192
H = 128
R = 256
TOK_DEV = 128
VOC_DEV = 1008
SECTIONS = 4
TOKENS = 8192
VOCAB = 64512
CAP = 4


def draw_token_ids(key, part):
    key = jax.random.fold_in(key, 11)
    shards = TOKENS // TOK_DEV
    common_key, block_key = jax.random.split(key)
    common_owner = jax.random.randint(common_key, (), 0, shards)
    slot_owner = jnp.arange(shards * CAP, dtype=jnp.int32) // CAP

    def one_block(block_seed):
        first_key, second_key, third_key, fourth_key = jax.random.split(block_seed, 4)
        extra_owner = jax.random.randint(first_key, (), 0, shards)
        scores = jax.random.permutation(second_key, shards * CAP).astype(jnp.int32)
        scores = jnp.where(slot_owner == common_owner, scores - 2 * shards * CAP, scores)
        scores = jnp.where((slot_owner == extra_owner) & (slot_owner != common_owner), scores - shards * CAP, scores)
        order = jnp.argsort(scores, stable=True)
        owners = slot_owner[order][:TOK_DEV]
        owners = jax.random.permutation(third_key, owners)
        within = jax.random.randint(fourth_key, (TOK_DEV,), 0, VOC_DEV)
        return (owners * VOC_DEV + within).astype(jnp.int32)
    seeds = jax.random.split(block_key, shards)
    return jax.vmap(one_block)(seeds).reshape(TOKENS).astype(jnp.int32)


def block_scale(stream_key, shape, cuts, low, high):
    gain, own = 1.0, jax.random.fold_in(stream_key, 6)
    for dim, parts in cuts:
        steps = jnp.exp(jax.random.uniform(jax.random.fold_in(own, dim), (parts,), jnp.float32, low / len(cuts), high / len(cuts)))
        gain = gain * jnp.repeat(steps, shape[dim] // parts).reshape([-1 if axis == dim else 1 for axis in range(len(shape))])
    return gain


def scatter_about(own_key, extent, spread, bound, cuts=(), kind=jnp.bfloat16):
    array = jax.random.normal(own_key, extent, jnp.float32) * spread
    if len(cuts) > 0:
        array = block_scale(own_key, extent, cuts, -0.22, 0.18) * array
    return jnp.clip(array, min=-bound, max=bound).astype(kind)


def setup_inputs(seed: int = 0) -> dict:
    key_of = jax.random.split(jax.random.key(seed), 8)
    token_ids = draw_token_ids(jax.random.fold_in(key_of[7], 71), 0)
    embed_table = scatter_about(key_of[1], (VOCAB, D), 1.0, 6.0, ((0, 64), (1, 4)))
    subspace = scatter_about(key_of[2], (SECTIONS, D, R), D ** -0.5, 0.0625, ((0, 4),))
    adapter_in = scatter_about(key_of[3], (SECTIONS, D, H), D ** -0.5, 0.0625, ((0, 4),))
    adapter_out = scatter_about(key_of[4], (SECTIONS, H, D), H ** -0.5, 0.5, ((0, 4),))
    norm_gain = jnp.clip(1.0 + 0.18 * jax.random.normal(key_of[5], (SECTIONS, D), jnp.float32), 0.1, 1.9)
    coef_cotangent = scatter_about(key_of[6], (TOKENS, R), 0.01, 0.059814453, ((0, 64),))
    return {"token_ids": token_ids, "embed_table": embed_table, "subspace": subspace, "adapter_in": adapter_in, "adapter_out": adapter_out, "norm_gain": norm_gain, "coef_cotangent": coef_cotangent}


EPSILON = 1e-05

def contract_last(left, right):
    return lax.dot_general(left, right, (((1,), (1,)), ((), ())), preferred_element_type=jnp.float32)

def contract_first(left, right):
    return lax.dot_general(left, right, (((0,), (0,)), ((), ())), preferred_element_type=jnp.float32)

def contract_first_exact(left, right):
    return lax.dot_general(left.astype(jnp.float32), right.astype(jnp.float32), (((0,), (0,)), ((), ())), precision=lax.Precision.HIGHEST, preferred_element_type=jnp.float32)

def layer_pieces(hidden, scale, weight_in):
    inverse_rms = lax.rsqrt(lax.optimization_barrier(jnp.mean(hidden * hidden, axis=-1, keepdims=True)) + EPSILON)
    normal_hat = hidden * inverse_rms
    normed = (normal_hat * scale).astype(jnp.bfloat16)
    preact = jnp.dot(normed, weight_in, preferred_element_type=jnp.float32)
    return (inverse_rms, normal_hat, normed, preact)

def layer_forward(hidden, scale, weight_in, weight_out):
    inverse_rms, normal_hat, normed, preact = layer_pieces(hidden, scale, weight_in)
    active = jax.nn.silu(preact).astype(jnp.bfloat16)
    return hidden + jnp.dot(active, weight_out, preferred_element_type=jnp.float32)

def layer_backward(hidden, slope, scale, weight_in, weight_out):
    inverse_rms, normal_hat, normed, preact = layer_pieces(hidden, scale, weight_in)
    active = jax.nn.silu(preact).astype(jnp.bfloat16)
    slope_half = slope.astype(jnp.bfloat16)
    grad_branch = contract_last(slope_half, weight_out)
    sigmoid_value = jax.nn.sigmoid(preact)
    grad_preact = (grad_branch * sigmoid_value * (1.0 + preact * (1.0 - sigmoid_value))).astype(jnp.bfloat16)
    grad_normed = contract_last(grad_preact, weight_in)
    grad_hat = grad_normed * scale
    gain_term = lax.optimization_barrier(jnp.sum(grad_normed * normal_hat, axis=0))
    grad_hidden = slope + inverse_rms * (grad_hat - normal_hat * lax.optimization_barrier(jnp.mean(grad_hat * normal_hat, axis=-1, keepdims=True)))
    return (normed, active, grad_preact, gain_term, grad_hidden)

def reference(token_ids, embed_table, subspace, adapter_in, adapter_out, norm_gain, coef_cotangent):
    blocks = TOKENS // TOK_DEV
    id_blocks = token_ids.reshape(blocks, TOK_DEV)
    cot_blocks = coef_cotangent.reshape(blocks, TOK_DEV, R)

    def one_block(totals, inputs):
        block_ids, block_cot = inputs
        base_rows = jnp.take(embed_table, block_ids, axis=0).astype(jnp.float32)
        hidden = base_rows
        kept_inputs = []
        sent_list = []
        for section_index in range(SECTIONS):
            kept_inputs.append(hidden)
            output = layer_forward(hidden, norm_gain[section_index], adapter_in[section_index], adapter_out[section_index])
            sent = jnp.dot((output - base_rows).astype(jnp.bfloat16), subspace[section_index], preferred_element_type=jnp.float32).astype(jnp.bfloat16)
            sent_list.append(sent)
            hidden = base_rows + contract_last(sent, subspace[section_index])
        grads_in = [None] * SECTIONS
        grads_out = [None] * SECTIONS
        grads_gain = [None] * SECTIONS
        returning = block_cot
        for section_index in reversed(range(SECTIONS)):
            slope = contract_last(returning, subspace[section_index])
            normed, active, grad_preact, gain_term, grad_hidden = layer_backward(kept_inputs[section_index], slope, norm_gain[section_index], adapter_in[section_index], adapter_out[section_index])
            grads_in[section_index] = contract_first(normed, grad_preact)
            grads_out[section_index] = contract_first_exact(active, slope)
            grads_gain[section_index] = gain_term
            if section_index > 0:
                returning = jnp.dot(grad_hidden.astype(jnp.bfloat16), subspace[section_index - 1], preferred_element_type=jnp.float32).astype(jnp.bfloat16)
        new_totals = (totals[0] + jnp.stack(grads_in), totals[1] + jnp.stack(grads_out), totals[2] + jnp.stack(grads_gain))
        return (new_totals, jnp.stack(sent_list))
    start_totals = (jnp.zeros((SECTIONS, D, H), jnp.float32), jnp.zeros((SECTIONS, H, D), jnp.float32), jnp.zeros((SECTIONS, D), jnp.float32))
    totals, sent_all = lax.scan(one_block, start_totals, (id_blocks, cot_blocks))
    sent_coefs = jnp.transpose(sent_all, (1, 0, 2, 3)).reshape(SECTIONS, TOKENS, R)
    return (sent_coefs, totals[0], totals[1], totals[2])
```

```python
import jax
import jax.numpy as jnp
from jax import lax
from jax.experimental import pallas as pl
from jax.experimental.pallas import tpu as pltpu
from jax.sharding import Mesh, PartitionSpec as P

CAP = 4
EPSILON = 1e-05
F32, BF16 = jnp.float32, jnp.bfloat16
YL, CO, Z, X, YH = "yl", "co", "z", "x", "yh"
DP = (Z, X, YH)
SEC = (YL, CO)
XY = (X, YH)


def dot_nn(a, b):
    return lax.dot_general(a, b, (((1,), (0,)), ((), ())), preferred_element_type=F32)


def dot_nt(a, b):
    return lax.dot_general(a, b, (((1,), (1,)), ((), ())), preferred_element_type=F32)


def dot_tn(a, b):
    return lax.dot_general(a, b, (((0,), (0,)), ((), ())), preferred_element_type=F32)


def swap(x, axis):
    return lax.ppermute(x, axis, [(0, 1), (1, 0)])


def gather_peers(x):
    across = swap(x, YL)
    beside = swap(x, CO)
    return x, beside, across, swap(across, CO)


def full(shape):
    return pl.BlockSpec(shape, lambda *_: (0,) * len(shape))


def prep_kernel(basis, prev, gained, weight_out, mats, acc):
    step = pl.program_id(0)
    r, h = basis.shape[1], gained.shape[1]

    @pl.when(step == 0)
    def _():
        acc[...] = jnp.zeros_like(acc)

    own, before = basis[...], prev[...]
    acc[0:r, :] += dot_tn(before, own)
    acc[r : r + h, :] += dot_tn(gained[...], before)
    acc[r + h : r + 2 * h, :] += dot_nn(weight_out[...], own)
    acc[r + 2 * h : 2 * r + 2 * h, :] += dot_tn(own, own)

    @pl.when(step == pl.num_programs(0) - 1)
    def _():
        top = 2 * r + 2 * h
        high = acc[...].astype(BF16)
        mats[0:top, :] = high
        gram = acc[r + 2 * h : top, :]
        mats[top : top + r, :] = (gram - high[r + 2 * h : top, :].astype(F32)).astype(BF16)


def prep(basis, prev, gained, weight_out):
    d, r = basis.shape
    h = gained.shape[1]
    steps = 8
    rows = d // steps
    return pl.pallas_call(
        prep_kernel,
        grid=(steps,),
        in_specs=[
            pl.BlockSpec((rows, r), lambda k: (k, 0)),
            pl.BlockSpec((rows, r), lambda k: (k, 0)),
            pl.BlockSpec((rows, h), lambda k: (k, 0)),
            pl.BlockSpec((h, rows), lambda k: (0, k)),
        ],
        out_specs=full((3 * r + 2 * h, r)),
        out_shape=jax.ShapeDtypeStruct((3 * r + 2 * h, r), BF16),
        scratch_shapes=[pltpu.VMEM((2 * r + 2 * h, r), F32)],
        compiler_params=pltpu.CompilerParams(vmem_limit_bytes=24 * 2**20),
        cost_estimate=pl.CostEstimate(
            flops=2 * d * r * (2 * r + 2 * h), bytes_accessed=4 * d * (r + h), transcendentals=0
        ),
        name="prep",
    )(basis, prev, gained, weight_out)


def project_kernel(me, p0, p1, p2, p3, basis, gained, out, square):
    step = pl.program_id(0)
    r = basis.shape[1]
    for k, piece in enumerate((p0, p1, p2, p3)):

        @pl.when(step == k)
        def _(k=k, piece=piece):
            x = piece[...]
            xf = x.astype(F32)
            q = jnp.broadcast_to(jnp.sum(xf * xf, axis=1, keepdims=True), square.shape)
            a, b = dot_nn(x, basis[...]), dot_nn(x, gained[...])
            if k == 0:
                out[:, 0:r] = a
                out[:, r:] = b
                square[...] = q
            else:
                out[:, 0:r] += a
                out[:, r:] += b
                square[...] += q


def project(me, pieces, basis, gained):
    tokens, cols = pieces[0].shape
    r, h = basis.shape[1], gained.shape[1]
    return pl.pallas_call(
        project_kernel,
        grid_spec=pltpu.PrefetchScalarGridSpec(
            num_scalar_prefetch=1,
            grid=(4,),
            in_specs=[full((tokens, cols))] * 4
            + [
                pl.BlockSpec((cols, r), lambda k, me: (k ^ me[0], 0)),
                pl.BlockSpec((cols, h), lambda k, me: (k ^ me[0], 0)),
            ],
            out_specs=[full((tokens, r + h)), full((tokens, 128))],
        ),
        out_shape=[
            jax.ShapeDtypeStruct((tokens, r + h), F32),
            jax.ShapeDtypeStruct((tokens, 128), F32),
        ],
        compiler_params=pltpu.CompilerParams(vmem_limit_bytes=24 * 2**20),
        cost_estimate=pl.CostEstimate(
            flops=8 * tokens * cols * (r + h), bytes_accessed=8 * cols * (r + h + tokens), transcendentals=0
        ),
        name="project",
    )(me, *pieces, basis, gained)


def chain_kernel(width, me_ref, cot, square, q0, q1, q2, q3, m0, m1, m2, m3, sent, packed,
                 pq, mats, pres, acts, coefs, spans, invs, ins, ws):
    me = me_ref[0]
    r = cot.shape[1]
    h = q0.shape[1] - r
    for k, (q, m) in enumerate(((q0, m0), (q1, m1), (q2, m2), (q3, m3))):
        pq[k ^ me] = q[...]
        mats[k ^ me] = m[...]
    o_k, o_n, o_g, o_l = r, r + h, r + 2 * h, 2 * r + 2 * h
    squares = square[:, 0:1]
    coefs[0] = jnp.zeros_like(coefs[0])
    for s in range(4):
        base_in = pq[s, :, r:]
        if s == 0:
            inv = lax.rsqrt(squares * (1.0 / width) + EPSILON)
            pre = inv * base_in
        else:
            c = coefs[s]
            base_sub = pq[s - 1, :, 0:r]
            span = base_sub + dot_nn(c, mats[s - 1, o_g:o_l, :]) + dot_nn(c, mats[s - 1, o_l:, :])
            total = squares + jnp.sum(c.astype(F32) * (base_sub + span), axis=1, keepdims=True)
            inv = lax.rsqrt(jnp.maximum(total, 0.0) * (1.0 / width) + EPSILON)
            pre = inv * (base_in + dot_nt(c, mats[s, o_k:o_n, :]))
            spans[s] = span
        invs[s] = jnp.broadcast_to(inv, invs.shape[1:])
        pres[s] = pre
        act = (pre / (1.0 + jnp.exp(-pre))).astype(BF16)
        acts[s] = act
        new = dot_nn(act, mats[s, o_n:o_g, :])
        if s > 0:
            new = new + dot_nn(c, mats[s, 0:r, :])
        coefs[s + 1] = new.astype(BF16)
    arrived = cot[...]
    for s in (3, 2, 1, 0):
        ins[s] = arrived
        pre = pres[s]
        sg = 1.0 / (1.0 + jnp.exp(-pre))
        gp = dot_nt(arrived, mats[s, o_n:o_g, :]) * sg * (1.0 + pre * (1.0 - sg))
        inv = invs[s, :, 0:1]
        ws[s] = (gp * inv).astype(BF16)
        if s > 0:
            mean = jnp.sum(gp * pre, axis=1, keepdims=True) * (1.0 / width)
            back = dot_nn(gp.astype(BF16), mats[s, o_k:o_n, :]) - (inv * mean) * spans[s]
            arrived = (dot_nt(arrived, mats[s, 0:r, :]) + inv * back).astype(BF16)
    sent[...] = coefs[me + 1]
    row = (ws[me], acts[me], ins[me], coefs[me])
    for t in range(packed.shape[0]):
        at = 0
        for v in row:
            packed[t, :, at : at + v.shape[1]] = v
            at += v.shape[1]


def chain(me, cot, square, pq, mats, width, copies):
    tokens, r = cot.shape
    h = pq[0].shape[1] - r
    vmem = pl.BlockSpec(memory_space=pltpu.VMEM)
    return pl.pallas_call(
        lambda *refs: chain_kernel(width, *refs),
        in_specs=[pl.BlockSpec(memory_space=pltpu.SMEM)] + [vmem] * 10,
        out_specs=[vmem, vmem],
        out_shape=[
            jax.ShapeDtypeStruct((tokens, r), BF16),
            jax.ShapeDtypeStruct((copies, tokens, 2 * h + 2 * r), BF16),
        ],
        scratch_shapes=[
            pltpu.VMEM((4, tokens, r + h), F32),
            pltpu.VMEM((4,) + mats[0].shape, BF16),
            pltpu.VMEM((4, tokens, h), F32),
            pltpu.VMEM((4, tokens, h), BF16),
            pltpu.VMEM((5, tokens, r), BF16),
            pltpu.VMEM((4, tokens, r), F32),
            pltpu.VMEM((4, tokens, 128), F32),
            pltpu.VMEM((4, tokens, r), BF16),
            pltpu.VMEM((4, tokens, h), BF16),
        ],
        compiler_params=pltpu.CompilerParams(vmem_limit_bytes=32 * 2**20),
        cost_estimate=pl.CostEstimate(flops=4 * 10**9, bytes_accessed=6 * 2**20, transcendentals=10**6),
        name="chain",
    )(me, cot, square, *pq, *mats)


def share_kernel(me_ref, packed, t0, t1, t2, t3, rows_own, rows_prev, out):
    me = me_ref[0]
    r = rows_own.shape[2]
    h = (packed.shape[1] - 2 * r) // 2
    w = packed[:, 0:h]
    act = packed[:, h : 2 * h]
    arrived = packed[:, 2 * h : 2 * h + r]
    coef = packed[:, 2 * h + r :]
    v = dot_tn(act, arrived)
    u = dot_tn(w, coef)
    vh, uh = v.astype(BF16), u.astype(BF16)
    vl = (v - vh.astype(F32)).astype(BF16)
    wt = w.astype(F32).T.astype(BF16)
    for k, piece in enumerate((t0, t1, t2, t3)):
        c = k ^ me
        xs = dot_nn(wt, piece[...])
        n = xs.shape[1] // 2
        for e in range(2):
            z = 2 * c + e
            own = rows_own[z]
            out[z, 0:h, :] = (xs[:, e * n : (e + 1) * n] + dot_nt(uh, rows_prev[z])).astype(BF16)
            out[z, h:, :] = (dot_nt(vh, own) + dot_nt(vl, own)).astype(BF16)


def share(me, packed, pieces, rows_own, rows_prev):
    h = (packed.shape[1] - 2 * rows_own.shape[2]) // 2
    zs, n, _ = rows_own.shape
    vmem = pl.BlockSpec(memory_space=pltpu.VMEM)
    return pl.pallas_call(
        share_kernel,
        in_specs=[pl.BlockSpec(memory_space=pltpu.SMEM)] + [vmem] * 7,
        out_specs=vmem,
        out_shape=jax.ShapeDtypeStruct((zs, 2 * h, n), BF16),
        compiler_params=pltpu.CompilerParams(vmem_limit_bytes=32 * 2**20),
        cost_estimate=pl.CostEstimate(flops=2 * 10**9, bytes_accessed=6 * 2**20, transcendentals=0),
        name="share",
    )(me, packed, *pieces, rows_own, rows_prev)


def per_device(
    token_ids, embed_table, subspace, adapter_in, adapter_out, norm_gain, coef_cotangent
):
    tokens = token_ids.shape[0]
    shards = lax.axis_size(Z) * lax.axis_size(X) * lax.axis_size(YH)
    nz, nxy = lax.axis_size(Z), lax.axis_size(X) * lax.axis_size(YH)
    section = lax.axis_index(YL) * lax.axis_size(CO) + lax.axis_index(CO)
    me = jnp.reshape(section, (1,)).astype(jnp.int32)
    xy = lax.axis_index(X) * lax.axis_size(YH) + lax.axis_index(YH)
    dp = lax.axis_index(Z) * nxy + xy
    vocab, cols = embed_table.shape
    basis, weight_in, weight_out, gain = subspace[0], adapter_in[0], adapter_out[0], norm_gain[0]
    d, r = basis.shape
    h = weight_in.shape[1]
    block = d // shards

    prev = lax.ppermute(subspace, SEC, [(0, 1), (1, 2), (2, 3)])[0]

    owner = token_ids // vocab
    local_row = token_ids - owner * vocab
    matches = (owner[:, None] == jnp.arange(shards, dtype=jnp.int32)[None, :]).astype(jnp.int32)
    position = jnp.sum(jnp.cumsum(matches, axis=0) * matches, axis=1) - 1
    place = owner * CAP + position
    requests = jnp.zeros((shards * CAP,), jnp.int32).at[place].set(local_row).reshape(shards, CAP)
    asked = lax.all_to_all(requests, DP, split_axis=0, concat_axis=0, tiled=True).reshape(-1)
    pick = (asked[:, None] == jnp.arange(vocab, dtype=jnp.int32)[None, :]).astype(BF16)
    found = dot_nn(pick, embed_table).astype(BF16).reshape(shards, CAP, cols)
    answered = lax.all_to_all(found, DP, split_axis=0, concat_axis=0, tiled=True)
    put = (place[:, None] == jnp.arange(shards * CAP, dtype=jnp.int32)[None, :]).astype(BF16)
    part = dot_nn(put, answered.reshape(shards * CAP, cols)).astype(BF16)

    pieces = gather_peers(part)
    gained = (gain[:, None] * weight_in.astype(F32)).astype(BF16)
    pq, square = project(me, pieces, basis, gained)
    pqs = gather_peers(pq)
    mats = gather_peers(prep(basis, prev, gained, weight_out))

    turned = jnp.transpose(part.reshape(tokens, 2, nxy, block), (2, 0, 1, 3)).reshape(nxy, tokens, 2 * block)
    turned = lax.all_to_all(turned, XY, split_axis=0, concat_axis=0, tiled=True)
    turned = gather_peers(turned.reshape(nxy * tokens, 2 * block))

    sent, packed = chain(me, coef_cotangent, square, pqs, mats, d, nxy)
    packed = lax.all_to_all(packed, XY, split_axis=0, concat_axis=0, tiled=True)
    packed = packed.reshape(nxy * tokens, 2 * h + 2 * r)
    rows_own = lax.dynamic_index_in_dim(basis.reshape(nz, nxy, block, r), xy, 1, False)
    rows_prev = lax.dynamic_index_in_dim(prev.reshape(nz, nxy, block, r), xy, 1, False)
    shares = share(me, packed, turned, rows_own, rows_prev)
    shares = lax.all_to_all(shares, Z, split_axis=0, concat_axis=0, tiled=True)
    total = jnp.sum(shares.astype(F32), axis=0)
    plain = total[0:h].T
    gain_block = lax.dynamic_slice_in_dim(gain, dp * block, block, 0)
    in_block = lax.dynamic_slice_in_dim(weight_in, dp * block, block, 0)
    grad_in = gain_block[:, None] * plain
    grad_gain = jnp.sum(in_block.astype(F32) * plain, axis=1)
    return sent[None], grad_in[None], total[h:][None], grad_gain[None]


def solution(mesh):
    fine = Mesh(mesh.devices.reshape(2, 2, 8, 4, 2), (YL, CO, Z, X, YH))
    return jax.shard_map(
        per_device,
        mesh=fine,
        in_specs=(
            P(DP),
            P(DP, SEC),
            P(SEC, None, None),
            P(SEC, None, None),
            P(SEC, None, None),
            P(SEC, None),
            P(DP, None),
        ),
        out_specs=(
            P(SEC, DP, None),
            P(SEC, DP, None),
            P(SEC, None, DP),
            P(SEC, DP),
        ),
        check_vma=False,
    )
```

```python
import jax
import jax.numpy as jnp
from jax import lax
from jax.experimental import pallas as pl
from jax.experimental.pallas import tpu as pltpu
from jax.sharding import Mesh, PartitionSpec as P

CAP = 4
EPSILON = 1e-05
F32, BF16 = jnp.float32, jnp.bfloat16
YL, CO, ZH, ZL, X, YH = "yl", "co", "zh", "zl", "x", "yh"
DP = (ZH, ZL, X, YH)
SEC = (YL, CO)
GATHER = (ZL, X)
REDUCE = (ZH, YH)


def dot_nn(a, b):
    return lax.dot_general(a, b, (((1,), (0,)), ((), ())), preferred_element_type=F32)


def dot_nt(a, b):
    return lax.dot_general(a, b, (((1,), (1,)), ((), ())), preferred_element_type=F32)


def dot_tn(a, b):
    return lax.dot_general(a, b, (((0,), (0,)), ((), ())), preferred_element_type=F32)


def swap(x, axis):
    return lax.ppermute(x, axis, [(0, 1), (1, 0)])


def gather_peers(x):
    across = swap(x, YL)
    beside = swap(x, CO)
    return x, beside, across, swap(across, CO)


def full(shape):
    return pl.BlockSpec(shape, lambda *_: (0,) * len(shape))


def own_kernel(basis, weight_out, out, acc):
    step = pl.program_id(0)
    r, h = basis.shape[1], weight_out.shape[0]

    @pl.when(step == 0)
    def _():
        acc[...] = jnp.zeros_like(acc)

    own = basis[...]
    acc[0:h, :] += dot_nn(weight_out[...], own)
    acc[h:, :] += dot_tn(own, own)

    @pl.when(step == pl.num_programs(0) - 1)
    def _():
        high = acc[...].astype(BF16)
        out[0 : h + r, :] = high
        out[h + r :, :] = (acc[h:, :] - high[h:, :].astype(F32)).astype(BF16)


def own_products(basis, weight_out):
    d, r = basis.shape
    h = weight_out.shape[0]
    steps = 4
    rows = d // steps
    return pl.pallas_call(
        own_kernel,
        grid=(steps,),
        in_specs=[
            pl.BlockSpec((rows, r), lambda k: (k, 0)),
            pl.BlockSpec((h, rows), lambda k: (0, k)),
        ],
        out_specs=full((2 * r + h, r)),
        out_shape=jax.ShapeDtypeStruct((2 * r + h, r), BF16),
        scratch_shapes=[pltpu.VMEM((r + h, r), F32)],
        compiler_params=pltpu.CompilerParams(vmem_limit_bytes=24 * 2**20),
        cost_estimate=pl.CostEstimate(
            flops=2 * d * r * (r + h), bytes_accessed=2 * d * (r + h), transcendentals=0
        ),
        name="own_products",
    )(basis, weight_out)


def cross_kernel(at, basis, prev, gained, out):
    r, h = basis.shape[1], gained.shape[1]

    @pl.when(pl.program_id(0) == 0)
    def _():
        out[...] = jnp.zeros_like(out)

    before = prev[0]
    out[0:r, :] += dot_tn(before, basis[...])
    out[r:, :] += dot_tn(gained[...], before)


def cross_products(at, basis, prev, gained):
    r, h = basis.shape[1], gained.shape[1]
    blocks, rows, _ = prev.shape
    return pl.pallas_call(
        cross_kernel,
        grid_spec=pltpu.PrefetchScalarGridSpec(
            num_scalar_prefetch=1,
            grid=(blocks,),
            in_specs=[
                pl.BlockSpec((rows, r), lambda k, at: (k * 4 + at[0], 0)),
                pl.BlockSpec((1, rows, r), lambda k, at: (k, 0, 0)),
                pl.BlockSpec((rows, h), lambda k, at: (k * 4 + at[0], 0)),
            ],
            out_specs=full((r + h, r)),
        ),
        out_shape=jax.ShapeDtypeStruct((r + h, r), F32),
        compiler_params=pltpu.CompilerParams(vmem_limit_bytes=24 * 2**20),
        cost_estimate=pl.CostEstimate(
            flops=2 * blocks * rows * r * (r + h),
            bytes_accessed=2 * blocks * rows * (2 * r + h),
            transcendentals=0,
        ),
        name="cross_products",
    )(at, basis, prev, gained)


def sum_over_x(v):
    v = v + lax.ppermute(v, X, [(0, 1), (1, 0), (2, 3), (3, 2)])
    return v + lax.ppermute(v, X, [(0, 3), (3, 0), (1, 2), (2, 1)])


def column_of(row, n):
    return jnp.broadcast_to(row, (8, n)).T[:, 0:1]


def pick_kernel(asked, table, first, out):
    slots, vocab = asked.shape[1], table.shape[0]
    lanes = lax.broadcasted_iota(jnp.int32, (slots, vocab), 1)
    pick = (column_of(asked[...], slots) == lanes).astype(F32).astype(BF16)
    out[...] = dot_nn(pick, table[...]).astype(BF16)


def pick_rows(asked, table, first):
    slots = asked.shape[1]
    vocab, cols = table.shape
    steps = 4
    return pl.pallas_call(
        pick_kernel,
        grid=(steps,),
        in_specs=[
            full(asked.shape),
            pl.BlockSpec((vocab, cols // steps), lambda k: (0, k)),
            pl.BlockSpec(memory_space=pl.ANY),
        ],
        out_specs=pl.BlockSpec((slots, cols // steps), lambda k: (0, k)),
        out_shape=jax.ShapeDtypeStruct((slots, cols), BF16),
        compiler_params=pltpu.CompilerParams(vmem_limit_bytes=24 * 2**20),
        cost_estimate=pl.CostEstimate(
            flops=2 * slots * vocab * cols, bytes_accessed=2 * cols * (vocab + slots), transcendentals=0
        ),
        name="pick_rows",
    )(asked, table, first)


def place_kernel(place, answered, *refs):
    part, turned = refs[-2:]
    tokens, slots = part.shape[0], answered.shape[0]
    width = turned.shape[2]
    lanes = lax.broadcasted_iota(jnp.int32, (tokens, slots), 1)
    put = (column_of(place[...], tokens) == lanes).astype(F32).astype(BF16)
    for t in range(turned.shape[0]):
        rows = dot_nn(put, answered[:, t * width : (t + 1) * width]).astype(BF16)
        part[:, t * width : (t + 1) * width] = rows
        turned[t] = rows


def place_rows(place, answered, copies, firsts):
    tokens = place.shape[1]
    slots, cols = answered.shape
    vmem = pl.BlockSpec(memory_space=pltpu.VMEM)
    return pl.pallas_call(
        place_kernel,
        in_specs=[vmem, vmem] + [pl.BlockSpec(memory_space=pl.ANY)] * len(firsts),
        out_specs=[vmem, vmem],
        out_shape=[
            jax.ShapeDtypeStruct((tokens, cols), BF16),
            jax.ShapeDtypeStruct((copies, tokens, cols // copies), BF16),
        ],
        compiler_params=pltpu.CompilerParams(vmem_limit_bytes=16 * 2**20),
        cost_estimate=pl.CostEstimate(
            flops=2 * slots * tokens * cols, bytes_accessed=2 * cols * (slots + 2 * tokens), transcendentals=0
        ),
        name="place_rows",
    )(place, answered, *firsts)


def project_kernel(me, p0, p1, p2, p3, basis, gained, first, out, square):
    step = pl.program_id(0)
    r = basis.shape[1]
    for k, piece in enumerate((p0, p1, p2, p3)):

        @pl.when(step == k)
        def _(k=k, piece=piece):
            x = piece[...]
            xf = x.astype(F32)
            q = jnp.broadcast_to(jnp.sum(xf * xf, axis=1, keepdims=True), square.shape)
            a, b = dot_nn(x, basis[...]), dot_nn(x, gained[...])
            if k == 0:
                out[:, 0:r] = a
                out[:, r:] = b
                square[...] = q
            else:
                out[:, 0:r] += a
                out[:, r:] += b
                square[...] += q


def project(me, pieces, basis, gained, first):
    tokens, cols = pieces[0].shape
    r, h = basis.shape[1], gained.shape[1]
    return pl.pallas_call(
        project_kernel,
        grid_spec=pltpu.PrefetchScalarGridSpec(
            num_scalar_prefetch=1,
            grid=(4,),
            in_specs=[full((tokens, cols))] * 4
            + [
                pl.BlockSpec((cols, r), lambda k, me: (k ^ me[0], 0)),
                pl.BlockSpec((cols, h), lambda k, me: (k ^ me[0], 0)),
                pl.BlockSpec(memory_space=pl.ANY),
            ],
            out_specs=[full((tokens, r + h)), full((tokens, 128))],
        ),
        out_shape=[
            jax.ShapeDtypeStruct((tokens, r + h), F32),
            jax.ShapeDtypeStruct((tokens, 128), F32),
        ],
        compiler_params=pltpu.CompilerParams(vmem_limit_bytes=24 * 2**20),
        cost_estimate=pl.CostEstimate(
            flops=8 * tokens * cols * (r + h), bytes_accessed=8 * cols * (r + h + tokens), transcendentals=0
        ),
        name="project",
    )(me, *pieces, basis, gained, first)


def chain_kernel(width, me_ref, cot, square, q0, q1, q2, q3, g0, g1, g2, g3, m0, m1, m2, m3, sent, packed,
                 pq, owns, mats, pres, acts, coefs, spans, invs, ins, ws):
    me = me_ref[0]
    r = cot.shape[1]
    h = q0.shape[1] - r
    for k, (q, g, m) in enumerate(((q0, g0, m0), (q1, g1, m1), (q2, g2, m2), (q3, g3, m3))):
        pq[k ^ me] = q[...]
        owns[k ^ me] = g[...]
        mats[k ^ me] = m[...]
    squares = square[:, 0:1]
    coefs[0] = jnp.zeros_like(coefs[0])
    for s in range(4):
        base_in = pq[s, :, r:]
        if s == 0:
            inv = lax.rsqrt(squares * (1.0 / width) + EPSILON)
            pre = inv * base_in
        else:
            c = coefs[s]
            base_sub = pq[s - 1, :, 0:r]
            span = base_sub + dot_nn(c, owns[s - 1, h : h + r, :]) + dot_nn(c, owns[s - 1, h + r :, :])
            total = squares + jnp.sum(c.astype(F32) * (base_sub + span), axis=1, keepdims=True)
            inv = lax.rsqrt(jnp.maximum(total, 0.0) * (1.0 / width) + EPSILON)
            pre = inv * (base_in + dot_nt(c, mats[s, r:, :]))
            spans[s] = span
        invs[s] = jnp.broadcast_to(inv, invs.shape[1:])
        pres[s] = pre
        act = (pre / (1.0 + jnp.exp(-pre))).astype(BF16)
        acts[s] = act
        new = dot_nn(act, owns[s, 0:h, :])
        if s > 0:
            new = new + dot_nn(c, mats[s, 0:r, :])
        coefs[s + 1] = new.astype(BF16)
    arrived = cot[...]
    for s in (3, 2, 1, 0):
        ins[s] = arrived
        pre = pres[s]
        sg = 1.0 / (1.0 + jnp.exp(-pre))
        gp = dot_nt(arrived, owns[s, 0:h, :]) * sg * (1.0 + pre * (1.0 - sg))
        inv = invs[s, :, 0:1]
        ws[s] = (gp * inv).astype(BF16)
        if s > 0:
            mean = jnp.sum(gp * pre, axis=1, keepdims=True) * (1.0 / width)
            back = dot_nn(gp.astype(BF16), mats[s, r:, :]) - (inv * mean) * spans[s]
            arrived = (dot_nt(arrived, mats[s, 0:r, :]) + inv * back).astype(BF16)
    sent[...] = coefs[me + 1]
    row = (ws[me], acts[me], ins[me], coefs[me])
    for t in range(packed.shape[0]):
        at = 0
        for v in row:
            packed[t, :, at : at + v.shape[1]] = v
            at += v.shape[1]


def chain(me, cot, square, pq, owns, mats, width, copies):
    tokens, r = cot.shape
    h = pq[0].shape[1] - r
    vmem = pl.BlockSpec(memory_space=pltpu.VMEM)
    return pl.pallas_call(
        lambda *refs: chain_kernel(width, *refs),
        in_specs=[pl.BlockSpec(memory_space=pltpu.SMEM)] + [vmem] * 14,
        out_specs=[vmem, vmem],
        out_shape=[
            jax.ShapeDtypeStruct((tokens, r), BF16),
            jax.ShapeDtypeStruct((copies, tokens, 2 * h + 2 * r), BF16),
        ],
        scratch_shapes=[
            pltpu.VMEM((4, tokens, r + h), F32),
            pltpu.VMEM((4,) + owns[0].shape, BF16),
            pltpu.VMEM((4,) + mats[0].shape, BF16),
            pltpu.VMEM((4, tokens, h), F32),
            pltpu.VMEM((4, tokens, h), BF16),
            pltpu.VMEM((5, tokens, r), BF16),
            pltpu.VMEM((4, tokens, r), F32),
            pltpu.VMEM((4, tokens, 128), F32),
            pltpu.VMEM((4, tokens, r), BF16),
            pltpu.VMEM((4, tokens, h), BF16),
        ],
        compiler_params=pltpu.CompilerParams(vmem_limit_bytes=32 * 2**20),
        cost_estimate=pl.CostEstimate(flops=4 * 10**9, bytes_accessed=6 * 2**20, transcendentals=10**6),
        name="chain",
    )(me, cot, square, *pq, *owns, *mats)


def share_kernel(me_ref, packed, t0, t1, t2, t3, rows_own, rows_prev, out):
    me = me_ref[0]
    r = rows_own.shape[2]
    h = (packed.shape[1] - 2 * r) // 2
    w = packed[:, 0:h]
    act = packed[:, h : 2 * h]
    arrived = packed[:, 2 * h : 2 * h + r]
    coef = packed[:, 2 * h + r :]
    v = dot_tn(act, arrived)
    u = dot_tn(w, coef)
    vh, uh = v.astype(BF16), u.astype(BF16)
    vl = (v - vh.astype(F32)).astype(BF16)
    wt = w.astype(F32).T.astype(BF16)
    for k, piece in enumerate((t0, t1, t2, t3)):
        c = k ^ me
        xs = (dot_nn(wt, piece[...]) + dot_nt(uh, rows_prev[c])).astype(BF16)
        own = rows_own[c]
        os = (dot_nt(vh, own) + dot_nt(vl, own)).astype(BF16)
        n = xs.shape[1] // 2
        for e in range(2):
            out[2 * c + e, 0:h, :] = xs[:, e * n : (e + 1) * n]
            out[2 * c + e, h:, :] = os[:, e * n : (e + 1) * n]


def share(me, packed, pieces, rows_own, rows_prev):
    h = (packed.shape[1] - 2 * rows_own.shape[2]) // 2
    cs, n, _ = rows_own.shape
    vmem = pl.BlockSpec(memory_space=pltpu.VMEM)
    return pl.pallas_call(
        share_kernel,
        in_specs=[pl.BlockSpec(memory_space=pltpu.SMEM)] + [vmem] * 7,
        out_specs=vmem,
        out_shape=jax.ShapeDtypeStruct((2 * cs, 2 * h, n // 2), BF16),
        compiler_params=pltpu.CompilerParams(vmem_limit_bytes=32 * 2**20),
        cost_estimate=pl.CostEstimate(flops=2 * 10**9, bytes_accessed=6 * 2**20, transcendentals=0),
        name="share",
    )(me, packed, *pieces, rows_own, rows_prev)


def per_device(
    token_ids, embed_table, subspace, adapter_in, adapter_out, norm_gain, coef_cotangent
):
    tokens = token_ids.shape[0]
    zl, x = lax.axis_index(ZL), lax.axis_index(X)
    shards = lax.axis_size(DP)
    group = lax.axis_size(GATHER)
    section = lax.axis_index(SEC)
    me = jnp.reshape(section, (1,)).astype(jnp.int32)
    dp = lax.axis_index(DP)
    vocab, cols = embed_table.shape
    basis, weight_in, weight_out, gain = subspace[0], adapter_in[0], adapter_out[0], norm_gain[0]
    d, r = basis.shape
    h = weight_in.shape[1]
    block = d // shards

    rows_x = lax.dynamic_index_in_dim(basis.reshape(8, 4, 2 * block, r), x, 1, False)
    prev_x = lax.ppermute(rows_x, SEC, [(0, 1), (1, 2), (2, 3)])

    owner = token_ids // vocab
    local_row = token_ids - owner * vocab
    matches = (owner[:, None] == jnp.arange(shards, dtype=jnp.int32)[None, :]).astype(jnp.int32)
    position = jnp.sum(jnp.cumsum(matches, axis=0) * matches, axis=1) - 1
    place = owner * CAP + position
    requests = jnp.zeros((shards * CAP,), jnp.int32).at[place].set(local_row).reshape(shards, CAP)
    asked = lax.all_to_all(requests, DP, split_axis=0, concat_axis=0, tiled=True)
    found = pick_rows(asked.reshape(1, shards * CAP), embed_table, prev_x)
    answered = lax.all_to_all(
        found.reshape(shards, CAP, cols), DP, split_axis=0, concat_axis=0, tiled=True
    )

    gained = (gain[:, None] * weight_in.astype(F32)).astype(BF16)
    owns = gather_peers(own_products(basis, weight_out))
    crossed = sum_over_x(cross_products(jnp.reshape(x, (1,)), basis, prev_x, gained)).astype(BF16)
    rows_own = lax.dynamic_index_in_dim(rows_x.reshape(4, 2, 2 * block, r), zl, 1, False)
    rows_prev = lax.dynamic_index_in_dim(prev_x.reshape(4, 2, 2 * block, r), zl, 1, False)

    part, turned = place_rows(
        place.reshape(1, tokens),
        answered.reshape(shards * CAP, cols),
        group,
        (*owns, crossed, rows_own, rows_prev, gained),
    )
    pieces = gather_peers(part)
    turned = lax.all_to_all(turned, GATHER, split_axis=0, concat_axis=0, tiled=True)
    pq, square = project(me, pieces, basis, gained, turned)
    pqs = gather_peers(pq)
    mats = gather_peers(crossed)
    turned = gather_peers(turned.reshape(group * tokens, cols // group))

    sent, packed = chain(me, coef_cotangent, square, pqs, owns, mats, d, group)
    packed = lax.all_to_all(packed, GATHER, split_axis=0, concat_axis=0, tiled=True)
    packed = packed.reshape(group * tokens, 2 * h + 2 * r)
    shares = share(me, packed, turned, rows_own, rows_prev)
    shares = lax.all_to_all(shares, REDUCE, split_axis=0, concat_axis=0, tiled=True)
    total = jnp.sum(shares.astype(F32), axis=0)
    plain = total[0:h].T
    gain_block = lax.dynamic_slice_in_dim(gain, dp * block, block, 0)
    in_block = lax.dynamic_slice_in_dim(weight_in, dp * block, block, 0)
    grad_in = gain_block[:, None] * plain
    grad_gain = jnp.sum(in_block.astype(F32) * plain, axis=1)
    return sent[None], grad_in[None], total[h:][None], grad_gain[None]


def solution(mesh):
    fine = Mesh(mesh.devices.reshape(2, 2, 4, 2, 4, 2), (YL, CO, ZH, ZL, X, YH))
    return jax.shard_map(
        per_device,
        mesh=fine,
        in_specs=(
            P(DP),
            P(DP, SEC),
            P(SEC, None, None),
            P(SEC, None, None),
            P(SEC, None, None),
            P(SEC, None),
            P(DP, None),
        ),
        out_specs=(
            P(SEC, DP, None),
            P(SEC, DP, None),
            P(SEC, None, DP),
            P(SEC, DP),
        ),
        check_vma=False,
    )
```

```python
import functools

import jax
import jax.numpy as jnp
from jax import lax
from jax.experimental import pallas as pl
from jax.experimental.pallas import tpu as pltpu
from jax.sharding import Mesh, PartitionSpec as P

CAP = 4
EPSILON = 1e-05
GRANT = 63 * 2**20
F32, BF16 = jnp.float32, jnp.bfloat16
YL, CO, ZH, ZL, X, YH = "yl", "co", "zh", "zl", "x", "yh"
DP = (ZH, ZL, X, YH)
SEC = (YL, CO)
GATHER = (ZL, X)
REDUCE = (ZH, YH)


def dot_nn(a, b):
    return lax.dot_general(a, b, (((1,), (0,)), ((), ())), preferred_element_type=F32)


def dot_nt(a, b):
    return lax.dot_general(a, b, (((1,), (1,)), ((), ())), preferred_element_type=F32)


def dot_tn(a, b):
    return lax.dot_general(a, b, (((0,), (0,)), ((), ())), preferred_element_type=F32)


def swap(x, axis):
    return lax.ppermute(x, axis, [(0, 1), (1, 0)])


def gather_peers(x):
    across = swap(x, YL)
    beside = swap(x, CO)
    return x, beside, across, swap(across, CO)


def full(shape):
    return pl.BlockSpec(shape, lambda *_: (0,) * len(shape))


def weights_kernel(basis, weight_in, gain, weight_out, after, gained, own, acc):
    step = pl.program_id(0)
    h = weight_in.shape[1]

    @pl.when(step == 0)
    def _():
        acc[...] = jnp.zeros_like(acc)

    part = basis[...]
    gained[...] = scaled(weight_in[...], gain[...])
    acc[0:h, :] += dot_nn(weight_out[...], part)
    acc[h:, :] += dot_tn(part, part)

    @pl.when(step == pl.num_programs(0) - 1)
    def _():
        own[...] = acc[...].astype(BF16)


def weights(basis, weight_in, gain, weight_out, after):
    d, r = basis.shape
    h = weight_in.shape[1]
    steps = 4
    rows = d // steps
    return pl.pallas_call(
        weights_kernel,
        grid=(steps,),
        in_specs=[
            pl.BlockSpec((rows, r), lambda k: (k, 0)),
            pl.BlockSpec((rows, h), lambda k: (k, 0)),
            pl.BlockSpec((1, rows), lambda k: (0, k)),
            pl.BlockSpec((h, rows), lambda k: (0, k)),
            pl.BlockSpec(memory_space=pl.ANY),
        ],
        out_specs=[pl.BlockSpec((rows, h), lambda k: (k, 0)), full((r + h, r))],
        out_shape=[
            jax.ShapeDtypeStruct((d, h), BF16),
            jax.ShapeDtypeStruct((r + h, r), BF16),
        ],
        scratch_shapes=[pltpu.VMEM((r + h, r), F32)],
        compiler_params=pltpu.CompilerParams(vmem_limit_bytes=GRANT),
        cost_estimate=pl.CostEstimate(
            flops=2 * d * r * (r + h), bytes_accessed=4 * d * (r + h), transcendentals=0
        ),
        name="weights",
    )(basis, weight_in, gain, weight_out, after)


def scaled(rows, gain):
    column = jnp.broadcast_to(gain, (8, rows.shape[0])).T[:, 0:1]
    return (rows.astype(F32) * column).astype(BF16)


def cross_kernel(at, basis, weight_in, gain, prev, after, out, mine, ins, theirs, sems):
    blocks, rows, r = mine.shape
    copies = [
        start_all(
            [
                pltpu.make_async_copy(prev.at[k], theirs.at[k], sems.at[0, k]),
                pltpu.make_async_copy(basis.at[k, at[0]], mine.at[k], sems.at[1, k]),
                pltpu.make_async_copy(weight_in.at[k, at[0]], ins.at[k], sems.at[2, k]),
            ]
        )
        for k in range(blocks)
    ]
    first, second = 0.0, 0.0
    for k in range(blocks):
        start = pl.multiple_of((k * 4 + at[0]) * rows, rows)
        wait_all(copies[k])
        first = first + dot_tn(theirs[k], mine[k])
        second = second + dot_tn(theirs[k], scaled(ins[k], gain[:, pl.ds(start, rows)]))
    out[:, 0:r] = first.astype(BF16)
    out[:, r:] = second.astype(BF16)


def cross_products(at, basis, weight_in, gain, prev, after):
    blocks, rows, r = prev.shape
    h = weight_in.shape[1]
    hbm = pl.BlockSpec(memory_space=pl.ANY)
    return pl.pallas_call(
        cross_kernel,
        in_specs=[pl.BlockSpec(memory_space=pltpu.SMEM), hbm, hbm, full(gain.shape), hbm, hbm],
        out_specs=full((r, r + h)),
        out_shape=jax.ShapeDtypeStruct((r, r + h), BF16),
        scratch_shapes=[
            pltpu.VMEM((blocks, rows, r), BF16),
            pltpu.VMEM((blocks, rows, h), BF16),
            pltpu.VMEM((blocks, rows, r), BF16),
            pltpu.SemaphoreType.DMA((3, blocks)),
        ],
        compiler_params=pltpu.CompilerParams(vmem_limit_bytes=GRANT),
        cost_estimate=pl.CostEstimate(
            flops=2 * blocks * rows * r * (r + h),
            bytes_accessed=2 * blocks * rows * (2 * r + h),
            transcendentals=0,
        ),
        name="cross_products",
    )(at, basis.reshape(blocks, 4, rows, r), weight_in.reshape(blocks, 4, rows, h), gain, prev, after)


def sum_over_x(v):
    total = v.astype(F32)
    for k in (1, 2, 3):
        total = total + lax.ppermute(v, X, [(i, (i + k) % 4) for i in range(4)]).astype(F32)
    return total.astype(BF16)


def start_all(copies):
    for copy in copies:
        copy.start()
    return copies


def wait_all(copies):
    for copy in copies:
        copy.wait()


def one_hot(column, n):
    lanes = lax.broadcasted_iota(jnp.int32, (column.shape[0], n), 1)
    return (column == lanes).astype(F32)


def split_int(v):
    return (v // 128).astype(F32).astype(BF16), (v % 128).astype(F32).astype(BF16)


def request_kernel(vocab, at, ids, basis, place, requests, rows, sem):
    copy = pltpu.make_async_copy(basis.at[:, at[0]], rows, sem)
    copy.start()
    tokens, shards = ids.shape[1], requests.shape[0]
    column = jnp.broadcast_to(ids[...], (8, tokens)).T[:, 0:1]
    first = lax.broadcasted_iota(jnp.int32, (tokens, shards), 1) * vocab
    mine = (column >= first) & (column < first + vocab)
    matches = mine.astype(F32)
    local = jnp.sum(jnp.where(mine, column - first, 0), axis=1, keepdims=True)
    owner = jnp.sum(jnp.where(mine, first // vocab, 0), axis=1, keepdims=True)
    earlier = lax.broadcasted_iota(jnp.int32, (tokens, tokens), 0) > lax.broadcasted_iota(
        jnp.int32, (tokens, tokens), 1
    )
    half = matches.astype(BF16)
    before = dot_nn(earlier.astype(F32).astype(BF16), half)
    position = jnp.sum(matches * before, axis=1, keepdims=True).astype(jnp.int32)
    place[...] = owner * CAP + position
    slot = one_hot(position, 128)
    high, low = split_int(local)
    found = 128.0 * dot_tn(half, (slot * high.astype(F32)).astype(BF16))
    found = found + dot_tn(half, (slot * low.astype(F32)).astype(BF16))
    requests[...] = found[:, 0:CAP].astype(jnp.int32)
    copy.wait()


def request(at, ids, basis, vocab, shards):
    tokens = ids.shape[1]
    blocks, _, rows, r = basis.shape
    hbm = pl.BlockSpec(memory_space=pl.ANY)
    return pl.pallas_call(
        functools.partial(request_kernel, vocab),
        in_specs=[pl.BlockSpec(memory_space=pltpu.SMEM), full(ids.shape), hbm],
        out_specs=[full((tokens, 1)), full((shards, CAP)), full((blocks, rows, r))],
        out_shape=[
            jax.ShapeDtypeStruct((tokens, 1), jnp.int32),
            jax.ShapeDtypeStruct((shards, CAP), jnp.int32),
            jax.ShapeDtypeStruct((blocks, rows, r), BF16),
        ],
        scratch_shapes=[pltpu.SemaphoreType.DMA],
        compiler_params=pltpu.CompilerParams(vmem_limit_bytes=GRANT),
        cost_estimate=pl.CostEstimate(flops=10**7, bytes_accessed=2**21, transcendentals=0),
        name="request",
    )(at, ids, basis)


def pick_kernel(asked, table, *refs):
    out, hot, rows, found, in_sems, out_sems = refs[-6:]
    shards, cap = asked.shape
    slots, vocab = hot.shape
    steps, _, width = rows.shape
    ins = [
        pltpu.make_async_copy(table.at[:, pl.ds(k * width, width)], rows.at[k], in_sems.at[k])
        for k in range(steps)
    ]
    outs = [
        pltpu.make_async_copy(found.at[k], out.at[:, :, pl.ds(k * width, width)], out_sems.at[k])
        for k in range(steps)
    ]
    for copy in ins:
        copy.start()
    peer = lax.broadcasted_iota(jnp.int32, (slots, shards), 0) // cap
    peer = (peer == lax.broadcasted_iota(jnp.int32, (slots, shards), 1)).astype(F32).astype(BF16)
    high, low = split_int(asked[...])
    spread = 128.0 * dot_nn(peer, high) + dot_nn(peer, low)
    slot = lax.broadcasted_iota(jnp.int32, (slots, cap), 0) % cap
    keep = slot == lax.broadcasted_iota(jnp.int32, (slots, cap), 1)
    column = jnp.sum(jnp.where(keep, spread, 0.0), axis=1, keepdims=True)
    hot[...] = one_hot(column.astype(jnp.int32), vocab).astype(BF16)
    for k in range(steps):
        ins[k].wait()
        found[k] = dot_nn(hot[...], rows[k]).astype(BF16).reshape(shards, cap, width)
        outs[k].start()
    for copy in outs:
        copy.wait()


def pick_rows(asked, table, firsts):
    shards, cap = asked.shape
    vocab, cols = table.shape
    slots = shards * cap
    steps = 4
    width = cols // steps
    return pl.pallas_call(
        pick_kernel,
        in_specs=[full(asked.shape), pl.BlockSpec(memory_space=pl.ANY)]
        + [pl.BlockSpec(memory_space=pl.ANY)] * len(firsts),
        out_specs=pl.BlockSpec(memory_space=pl.ANY),
        out_shape=jax.ShapeDtypeStruct((shards, cap, cols), BF16),
        scratch_shapes=[
            pltpu.VMEM((slots, vocab), BF16),
            pltpu.VMEM((steps, vocab, width), BF16),
            pltpu.VMEM((steps, shards, cap, width), BF16),
            pltpu.SemaphoreType.DMA((steps,)),
            pltpu.SemaphoreType.DMA((steps,)),
        ],
        compiler_params=pltpu.CompilerParams(vmem_limit_bytes=GRANT),
        cost_estimate=pl.CostEstimate(
            flops=2 * slots * vocab * cols, bytes_accessed=2 * cols * (vocab + slots), transcendentals=0
        ),
        name="pick_rows",
    )(asked, table, *firsts)


def place_kernel(place, answered, *refs):
    part, turned = refs[-2:]
    tokens, slots = part.shape[0], answered.shape[0]
    width = turned.shape[2]
    put = one_hot(place[...], slots).astype(BF16)
    for t in range(turned.shape[0]):
        rows = dot_nn(put, answered[:, t * width : (t + 1) * width]).astype(BF16)
        part[:, t * width : (t + 1) * width] = rows
        turned[t] = rows


def place_rows(place, answered, copies, firsts):
    tokens = place.shape[0]
    slots, cols = answered.shape
    vmem = pl.BlockSpec(memory_space=pltpu.VMEM)
    return pl.pallas_call(
        place_kernel,
        in_specs=[vmem, vmem] + [pl.BlockSpec(memory_space=pl.ANY)] * len(firsts),
        out_specs=[vmem, vmem],
        out_shape=[
            jax.ShapeDtypeStruct((tokens, cols), BF16),
            jax.ShapeDtypeStruct((copies, tokens, cols // copies), BF16),
        ],
        compiler_params=pltpu.CompilerParams(vmem_limit_bytes=16 * 2**20),
        cost_estimate=pl.CostEstimate(
            flops=2 * slots * tokens * cols, bytes_accessed=2 * cols * (slots + 2 * tokens), transcendentals=0
        ),
        name="place_rows",
    )(place, answered, *firsts)


def project_kernel(me, p0, p1, p2, p3, basis, gained, first, second, out, square):
    step = pl.program_id(0)
    r = basis.shape[1]
    for k, piece in enumerate((p0, p1, p2, p3)):

        @pl.when(step == k)
        def _(k=k, piece=piece):
            x = piece[...]
            xf = x.astype(F32)
            q = jnp.broadcast_to(jnp.sum(xf * xf, axis=1, keepdims=True), square.shape)
            a, b = dot_nn(x, basis[...]), dot_nn(x, gained[...])
            if k == 0:
                out[:, 0:r] = a
                out[:, r:] = b
                square[...] = q
            else:
                out[:, 0:r] += a
                out[:, r:] += b
                square[...] += q


def project(me, pieces, basis, gained, first, second):
    tokens, cols = pieces[0].shape
    r, h = basis.shape[1], gained.shape[1]
    return pl.pallas_call(
        project_kernel,
        grid_spec=pltpu.PrefetchScalarGridSpec(
            num_scalar_prefetch=1,
            grid=(4,),
            in_specs=[full((tokens, cols))] * 4
            + [
                pl.BlockSpec((cols, r), lambda k, me: (k ^ me[0], 0)),
                pl.BlockSpec((cols, h), lambda k, me: (k ^ me[0], 0)),
                pl.BlockSpec(memory_space=pl.ANY),
                pl.BlockSpec(memory_space=pl.ANY),
            ],
            out_specs=[full((tokens, r + h)), full((tokens, 128))],
        ),
        out_shape=[
            jax.ShapeDtypeStruct((tokens, r + h), F32),
            jax.ShapeDtypeStruct((tokens, 128), F32),
        ],
        compiler_params=pltpu.CompilerParams(vmem_limit_bytes=24 * 2**20),
        cost_estimate=pl.CostEstimate(
            flops=8 * tokens * cols * (r + h), bytes_accessed=8 * cols * (r + h + tokens), transcendentals=0
        ),
        name="project",
    )(me, *pieces, basis, gained, first, second)


def chain_kernel(width, me_ref, cot, square, q0, q1, q2, q3, g0, g1, g2, g3, m0, m1, m2, m3, sent, packed,
                 pq, owns, mats, pres, acts, coefs, spans, invs, ins, ws):
    me = me_ref[0]
    r = cot.shape[1]
    h = q0.shape[1] - r
    for k, (q, g, m) in enumerate(((q0, g0, m0), (q1, g1, m1), (q2, g2, m2), (q3, g3, m3))):
        pq[k ^ me] = q[...]
        owns[k ^ me] = g[...]
        mats[k ^ me] = m[...]
    squares = square[:, 0:1]
    coefs[0] = jnp.zeros_like(coefs[0])
    for s in range(4):
        base_in = pq[s, :, r:]
        if s == 0:
            inv = lax.rsqrt(squares * (1.0 / width) + EPSILON)
            pre = inv * base_in
        else:
            c = coefs[s]
            base_sub = pq[s - 1, :, 0:r]
            span = base_sub + dot_nn(c, owns[s - 1, h:, :])
            total = squares + jnp.sum(c.astype(F32) * (base_sub + span), axis=1, keepdims=True)
            inv = lax.rsqrt(jnp.maximum(total, 0.0) * (1.0 / width) + EPSILON)
            pre = inv * (base_in + dot_nn(c, mats[s, :, r:]))
            spans[s] = span
        invs[s] = jnp.broadcast_to(inv, invs.shape[1:])
        pres[s] = pre
        act = (pre / (1.0 + jnp.exp(-pre))).astype(BF16)
        acts[s] = act
        new = dot_nn(act, owns[s, 0:h, :])
        if s > 0:
            new = new + dot_nn(c, mats[s, :, 0:r])
        coefs[s + 1] = new.astype(BF16)
    arrived = cot[...]
    for s in (3, 2, 1, 0):
        ins[s] = arrived
        pre = pres[s]
        sg = 1.0 / (1.0 + jnp.exp(-pre))
        gp = dot_nt(arrived, owns[s, 0:h, :]) * sg * (1.0 + pre * (1.0 - sg))
        inv = invs[s, :, 0:1]
        ws[s] = (gp * inv).astype(BF16)
        if s > 0:
            mean = jnp.sum(gp * pre, axis=1, keepdims=True) * (1.0 / width)
            back = dot_nt(gp.astype(BF16), mats[s, :, r:]) - (inv * mean) * spans[s]
            arrived = (dot_nt(arrived, mats[s, :, 0:r]) + inv * back).astype(BF16)
    sent[...] = coefs[me + 1]
    row = (ws[me], acts[me], ins[me], coefs[me])
    for t in range(packed.shape[0]):
        at = 0
        for v in row:
            packed[t, :, at : at + v.shape[1]] = v
            at += v.shape[1]


def chain(me, cot, square, pq, owns, mats, width, copies):
    tokens, r = cot.shape
    h = pq[0].shape[1] - r
    vmem = pl.BlockSpec(memory_space=pltpu.VMEM)
    return pl.pallas_call(
        functools.partial(chain_kernel, width),
        in_specs=[pl.BlockSpec(memory_space=pltpu.SMEM)] + [vmem] * 14,
        out_specs=[vmem, vmem],
        out_shape=[
            jax.ShapeDtypeStruct((tokens, r), BF16),
            jax.ShapeDtypeStruct((copies, tokens, 2 * h + 2 * r), BF16),
        ],
        scratch_shapes=[
            pltpu.VMEM((4, tokens, r + h), F32),
            pltpu.VMEM((4,) + owns[0].shape, BF16),
            pltpu.VMEM((4,) + mats[0].shape, BF16),
            pltpu.VMEM((4, tokens, h), F32),
            pltpu.VMEM((4, tokens, h), BF16),
            pltpu.VMEM((5, tokens, r), BF16),
            pltpu.VMEM((4, tokens, r), F32),
            pltpu.VMEM((4, tokens, 128), F32),
            pltpu.VMEM((4, tokens, r), BF16),
            pltpu.VMEM((4, tokens, h), BF16),
        ],
        compiler_params=pltpu.CompilerParams(vmem_limit_bytes=32 * 2**20),
        cost_estimate=pl.CostEstimate(flops=4 * 10**9, bytes_accessed=6 * 2**20, transcendentals=10**6),
        name="chain",
    )(me, cot, square, *pq, *owns, *mats)


def share_kernel(at, packed_in, t0, t1, t2, t3, basis, prev, out, packed, turned, rows_own, rows_prev, sems, t_sems, p_sems):
    me = at[0]
    r = rows_own.shape[2]
    h = (packed.shape[1] - 2 * r) // 2
    tokens = packed_in.shape[1]
    first = start_all(
        [
            pltpu.make_async_copy(packed_in.at[k], packed.at[pl.ds(k * tokens, tokens)], p_sems.at[k])
            for k in range(packed_in.shape[0])
        ]
    )
    rest = start_all(
        [
            pltpu.make_async_copy(prev.at[:, at[1]], rows_prev, sems.at[0]),
            pltpu.make_async_copy(basis.at[:, at[1], at[2]], rows_own, sems.at[1]),
        ]
    )
    pieces = start_all(
        [pltpu.make_async_copy(t, turned.at[k], t_sems.at[k]) for k, t in enumerate((t0, t1, t2, t3))]
    )
    wait_all(first)
    w = packed[:, 0:h]
    act = packed[:, h : 2 * h]
    arrived = packed[:, 2 * h : 2 * h + r]
    coef = packed[:, 2 * h + r :]
    v = dot_tn(act, arrived)
    wt = w.astype(F32).T.astype(BF16)
    uh = dot_nn(wt, coef).astype(BF16)
    vh = v.astype(BF16)
    vl = (v - vh.astype(F32)).astype(BF16)
    wait_all(rest)
    for k, piece in enumerate(pieces):
        c = k ^ me
        own = rows_own[c]
        os = (dot_nt(vh, own) + dot_nt(vl, own)).astype(BF16)
        low = dot_nt(uh, rows_prev[c])
        piece.wait()
        xs = (dot_nn(wt, turned[k]) + low).astype(BF16)
        n = xs.shape[1] // 2
        for e in range(2):
            out[2 * c + e, 0:h, :] = xs[:, e * n : (e + 1) * n]
            out[2 * c + e, h:, :] = os[:, e * n : (e + 1) * n]


def share(at, packed, pieces, basis, prev):
    cs, _, _, n, r = basis.shape
    group, tokens, wide = packed.shape
    h = (wide - 2 * r) // 2
    hbm = pl.BlockSpec(memory_space=pl.ANY)
    return pl.pallas_call(
        share_kernel,
        in_specs=[pl.BlockSpec(memory_space=pltpu.SMEM)] + [hbm] * 7,
        out_specs=full((2 * cs, 2 * h, n // 2)),
        out_shape=jax.ShapeDtypeStruct((2 * cs, 2 * h, n // 2), BF16),
        scratch_shapes=[
            pltpu.VMEM((group * tokens, wide), BF16),
            pltpu.VMEM((4,) + pieces[0].shape, BF16),
            pltpu.VMEM((cs, n, r), BF16),
            pltpu.VMEM((cs, n, r), BF16),
            pltpu.SemaphoreType.DMA((2,)),
            pltpu.SemaphoreType.DMA((4,)),
            pltpu.SemaphoreType.DMA((group,)),
        ],
        compiler_params=pltpu.CompilerParams(vmem_limit_bytes=GRANT),
        cost_estimate=pl.CostEstimate(flops=2 * 10**9, bytes_accessed=6 * 2**20, transcendentals=0),
        name="share",
    )(at, packed, *pieces, basis, prev)


def finish_kernel(arrived, weight_in, gain, grad_in, grad_out, grad_gain, shares, sem):
    h = shares.shape[1] // 2
    copy = pltpu.make_async_copy(arrived, shares, sem)
    copy.start()
    copy.wait()
    total = jnp.sum(shares[...].astype(F32), axis=0)
    plain = total[0:h]
    grad_out[...] = total[h:]
    grad_in[...] = (plain * gain[...]).T
    grad_gain[...] = jnp.sum(plain * weight_in[...].astype(F32).T, axis=0, keepdims=True)


def finish(shares, weight_in, gain):
    _, twice, n = shares.shape
    h = twice // 2
    return pl.pallas_call(
        finish_kernel,
        in_specs=[pl.BlockSpec(memory_space=pl.ANY), full((n, h)), full((1, n))],
        out_specs=[full((n, h)), full((h, n)), full((1, n))],
        out_shape=[
            jax.ShapeDtypeStruct((n, h), F32),
            jax.ShapeDtypeStruct((h, n), F32),
            jax.ShapeDtypeStruct((1, n), F32),
        ],
        scratch_shapes=[pltpu.VMEM(shares.shape, BF16), pltpu.SemaphoreType.DMA],
        compiler_params=pltpu.CompilerParams(vmem_limit_bytes=16 * 2**20),
        cost_estimate=pl.CostEstimate(flops=10**6, bytes_accessed=2**20, transcendentals=0),
        name="finish",
    )(shares, weight_in, gain)


def per_device(
    token_ids, embed_table, subspace, adapter_in, adapter_out, norm_gain, coef_cotangent
):
    tokens = token_ids.shape[0]
    zl, x = lax.axis_index(ZL), lax.axis_index(X)
    shards = lax.axis_size(DP)
    group = lax.axis_size(GATHER)
    section = lax.axis_index(SEC)
    me = jnp.reshape(section, (1,)).astype(jnp.int32)
    dp = lax.axis_index(DP)
    vocab, cols = embed_table.shape
    basis, weight_in, weight_out = subspace[0], adapter_in[0], adapter_out[0]
    d, r = basis.shape
    h = weight_in.shape[1]
    block = d // shards

    x_at = jnp.reshape(x, (1,)).astype(jnp.int32)
    place, requests, rows_x = request(
        x_at, token_ids.reshape(1, tokens), basis.reshape(8, 4, 2 * block, r), vocab, shards
    )
    prev_x = lax.ppermute(rows_x, SEC, [(0, 1), (1, 2), (2, 3)])
    asked = lax.all_to_all(requests, DP, split_axis=0, concat_axis=0, tiled=True)
    found = pick_rows(asked, embed_table, (prev_x,))
    answered = lax.all_to_all(found, DP, split_axis=0, concat_axis=0, tiled=True)

    crossed = cross_products(x_at, basis, weight_in, norm_gain, prev_x, found)
    gained, own = weights(basis, weight_in, norm_gain, weight_out, crossed)
    owns = gather_peers(own)
    mats = gather_peers(sum_over_x(crossed))

    part, turned = place_rows(
        place,
        answered.reshape(shards * CAP, cols),
        group,
        (*owns[1:], mats[2]),
    )
    pieces = gather_peers(part)
    turned = lax.all_to_all(turned, GATHER, split_axis=0, concat_axis=0, tiled=True)
    pq, square = project(me, pieces, basis, gained, turned, mats[2])
    pqs = gather_peers(pq)
    turned = gather_peers(turned.reshape(group * tokens, cols // group))

    sent, packed = chain(me, coef_cotangent, square, pqs, owns, mats, d, group)
    packed = lax.all_to_all(packed, GATHER, split_axis=0, concat_axis=0, tiled=True)
    at = jnp.stack([section, zl, x]).astype(jnp.int32)
    shares = share(
        at, packed, turned, basis.reshape(4, 2, 4, 2 * block, r), prev_x.reshape(4, 2, 2 * block, r)
    )
    shares = lax.all_to_all(shares, REDUCE, split_axis=0, concat_axis=0, tiled=True)
    in_block = lax.dynamic_slice_in_dim(weight_in, dp * block, block, 0)
    gain_block = lax.dynamic_slice_in_dim(norm_gain, dp * block, block, 1)
    grad_in, grad_out, grad_gain = finish(shares, in_block, gain_block)
    return sent[None], grad_in[None], grad_out[None], grad_gain


def solution(mesh):
    fine = Mesh(mesh.devices.reshape(2, 2, 4, 2, 4, 2), (YL, CO, ZH, ZL, X, YH))
    return jax.shard_map(
        per_device,
        mesh=fine,
        in_specs=(
            P(DP),
            P(DP, SEC),
            P(SEC, None, None),
            P(SEC, None, None),
            P(SEC, None, None),
            P(SEC, None),
            P(DP, None),
        ),
        out_specs=(
            P(SEC, DP, None),
            P(SEC, DP, None),
            P(SEC, None, DP),
            P(SEC, DP),
        ),
        check_vma=False,
    )
```

```python
import functools

import jax
import jax.numpy as jnp
from jax import lax
from jax.experimental import pallas as pl
from jax.experimental.pallas import tpu as pltpu
from jax.sharding import Mesh, PartitionSpec as P

CAP = 4
EPSILON = 1e-05
GRANT = 63 * 2**20
F32, BF16 = jnp.float32, jnp.bfloat16
YL, CO, ZH, ZL, X, YH = "yl", "co", "zh", "zl", "x", "yh"
DP = (ZH, ZL, X, YH)
SEC = (YL, CO)
GATHER = (ZL, X)
REDUCE = (ZH, YH)


def dot_nn(a, b):
    return lax.dot_general(a, b, (((1,), (0,)), ((), ())), preferred_element_type=F32)


def dot_nt(a, b):
    return lax.dot_general(a, b, (((1,), (1,)), ((), ())), preferred_element_type=F32)


def dot_tn(a, b):
    return lax.dot_general(a, b, (((0,), (0,)), ((), ())), preferred_element_type=F32)


def swap(x, axis):
    return lax.ppermute(x, axis, [(0, 1), (1, 0)])


def gather_peers(x):
    across = swap(x, YL)
    beside = swap(x, CO)
    return x, beside, across, swap(across, CO)


def full(shape):
    return pl.BlockSpec(shape, lambda *_: (0,) * len(shape))


def ordered(x, after):
    hbm = pl.BlockSpec(memory_space=pl.ANY)
    return pl.pallas_call(
        lambda *refs: None,
        in_specs=[hbm, hbm],
        out_specs=hbm,
        out_shape=jax.ShapeDtypeStruct(x.shape, x.dtype),
        input_output_aliases={0: 0},
        name="ordered",
    )(x, after)


def weights_kernel(basis, weight_in, gain, weight_out, *refs):
    gained, own, acc = refs[-3:]
    step = pl.program_id(0)
    h = weight_in.shape[1]

    @pl.when(step == 0)
    def _():
        acc[...] = jnp.zeros_like(acc)

    part = basis[...]
    gained[...] = scaled(weight_in[...], gain[...])
    acc[0:h, :] += dot_nn(weight_out[...], part)
    acc[h:, :] += dot_tn(part, part)

    @pl.when(step == pl.num_programs(0) - 1)
    def _():
        own[...] = acc[...].astype(BF16)


def weights(basis, weight_in, gain, weight_out, afters):
    d, r = basis.shape
    h = weight_in.shape[1]
    steps = 4
    rows = d // steps
    return pl.pallas_call(
        weights_kernel,
        grid=(steps,),
        in_specs=[
            pl.BlockSpec((rows, r), lambda k: (k, 0)),
            pl.BlockSpec((rows, h), lambda k: (k, 0)),
            pl.BlockSpec((1, rows), lambda k: (0, k)),
            pl.BlockSpec((h, rows), lambda k: (0, k)),
        ]
        + [pl.BlockSpec(memory_space=pl.ANY)] * len(afters),
        out_specs=[pl.BlockSpec((rows, h), lambda k: (k, 0)), full((r + h, r))],
        out_shape=[
            jax.ShapeDtypeStruct((d, h), BF16),
            jax.ShapeDtypeStruct((r + h, r), BF16),
        ],
        scratch_shapes=[pltpu.VMEM((r + h, r), F32)],
        compiler_params=pltpu.CompilerParams(vmem_limit_bytes=24 * 2**20),
        cost_estimate=pl.CostEstimate(
            flops=2 * d * r * (r + h), bytes_accessed=4 * d * (r + h), transcendentals=0
        ),
        name="weights",
    )(basis, weight_in, gain, weight_out, *afters)


def scaled(rows, gain):
    column = jnp.broadcast_to(gain, (8, rows.shape[0])).T[:, 0:1]
    return (rows.astype(F32) * column).astype(BF16)


def cross_kernel(at, basis, weight_in, gain, prev, after, out, mine, ins, theirs, sems):
    blocks, rows, r = theirs.shape
    wait_all(
        start_all(
            [
                pltpu.make_async_copy(prev, theirs, sems.at[0]),
                pltpu.make_async_copy(basis.at[:, at[0]], mine, sems.at[1]),
                pltpu.make_async_copy(weight_in.at[:, at[0]], ins, sems.at[2]),
            ]
        )
    )
    first, second = 0.0, 0.0
    for k in range(blocks):
        start = pl.multiple_of((k * 4 + at[0]) * rows, rows)
        first = first + dot_tn(theirs[k], mine[k])
        second = second + dot_tn(theirs[k], scaled(ins[k], gain[:, pl.ds(start, rows)]))
    out[:, 0:r] = first.astype(BF16)
    out[:, r:] = second.astype(BF16)


def cross_products(at, basis, weight_in, gain, prev, after):
    blocks, rows, r = prev.shape
    h = weight_in.shape[1]
    hbm = pl.BlockSpec(memory_space=pl.ANY)
    return pl.pallas_call(
        cross_kernel,
        in_specs=[pl.BlockSpec(memory_space=pltpu.SMEM), hbm, hbm, full(gain.shape), hbm, hbm],
        out_specs=full((r, r + h)),
        out_shape=jax.ShapeDtypeStruct((r, r + h), BF16),
        scratch_shapes=[
            pltpu.VMEM((blocks, rows, r), BF16),
            pltpu.VMEM((blocks, rows, h), BF16),
            pltpu.VMEM((blocks, rows, r), BF16),
            pltpu.SemaphoreType.DMA((3,)),
        ],
        compiler_params=pltpu.CompilerParams(vmem_limit_bytes=GRANT),
        cost_estimate=pl.CostEstimate(
            flops=2 * blocks * rows * r * (r + h),
            bytes_accessed=2 * blocks * rows * (2 * r + h),
            transcendentals=0,
        ),
        name="cross_products",
    )(at, basis.reshape(blocks, 4, rows, r), weight_in.reshape(blocks, 4, rows, h), gain, prev, after)


def sum_over_x(v):
    total = v.astype(F32)
    for k in (1, 2, 3):
        total = total + lax.ppermute(v, X, [(i, (i + k) % 4) for i in range(4)]).astype(F32)
    return total.astype(BF16)


def start_all(copies):
    for copy in copies:
        copy.start()
    return copies


def wait_all(copies):
    for copy in copies:
        copy.wait()


def one_hot(column, n):
    lanes = lax.broadcasted_iota(jnp.int32, (column.shape[0], n), 1)
    return (column == lanes).astype(F32)


def split_int(v):
    return (v // 128).astype(F32).astype(BF16), (v % 128).astype(F32).astype(BF16)


def request_kernel(vocab, at, ids, basis, place, requests, rows, sem):
    copy = pltpu.make_async_copy(basis.at[:, at[0]], rows, sem)
    copy.start()
    tokens, shards = ids.shape[1], requests.shape[0]
    column = jnp.broadcast_to(ids[...], (8, tokens)).T[:, 0:1]
    first = lax.broadcasted_iota(jnp.int32, (tokens, shards), 1) * vocab
    mine = (column >= first) & (column < first + vocab)
    matches = mine.astype(F32)
    local = jnp.sum(jnp.where(mine, column - first, 0), axis=1, keepdims=True)
    owner = jnp.sum(jnp.where(mine, first // vocab, 0), axis=1, keepdims=True)
    earlier = lax.broadcasted_iota(jnp.int32, (tokens, tokens), 0) > lax.broadcasted_iota(
        jnp.int32, (tokens, tokens), 1
    )
    half = matches.astype(BF16)
    before = dot_nn(earlier.astype(F32).astype(BF16), half)
    position = jnp.sum(matches * before, axis=1, keepdims=True).astype(jnp.int32)
    place[...] = owner * CAP + position
    slot = one_hot(position, 128)
    high, low = split_int(local)
    found = 128.0 * dot_tn(half, (slot * high.astype(F32)).astype(BF16))
    found = found + dot_tn(half, (slot * low.astype(F32)).astype(BF16))
    requests[...] = found[:, 0:CAP].astype(jnp.int32)
    copy.wait()


def request(at, ids, basis, vocab, shards):
    tokens = ids.shape[1]
    blocks, _, rows, r = basis.shape
    hbm = pl.BlockSpec(memory_space=pl.ANY)
    return pl.pallas_call(
        functools.partial(request_kernel, vocab),
        in_specs=[pl.BlockSpec(memory_space=pltpu.SMEM), full(ids.shape), hbm],
        out_specs=[full((tokens, 1)), full((shards, CAP)), full((blocks, rows, r))],
        out_shape=[
            jax.ShapeDtypeStruct((tokens, 1), jnp.int32),
            jax.ShapeDtypeStruct((shards, CAP), jnp.int32),
            jax.ShapeDtypeStruct((blocks, rows, r), BF16),
        ],
        scratch_shapes=[pltpu.SemaphoreType.DMA],
        compiler_params=pltpu.CompilerParams(vmem_limit_bytes=GRANT),
        cost_estimate=pl.CostEstimate(flops=10**7, bytes_accessed=2**21, transcendentals=0),
        name="request",
    )(at, ids, basis)


def pick_kernel(asked, table, *refs):
    out, hot, rows, found, in_sems, out_sems = refs[-6:]
    shards, cap = asked.shape
    slots, vocab = hot.shape
    steps, _, width = rows.shape
    ins = [
        pltpu.make_async_copy(table.at[:, pl.ds(k * width, width)], rows.at[k], in_sems.at[k])
        for k in range(steps)
    ]
    outs = [
        pltpu.make_async_copy(found.at[k], out.at[:, :, pl.ds(k * width, width)], out_sems.at[k])
        for k in range(steps)
    ]
    for copy in ins:
        copy.start()
    peer = lax.broadcasted_iota(jnp.int32, (slots, shards), 0) // cap
    peer = (peer == lax.broadcasted_iota(jnp.int32, (slots, shards), 1)).astype(F32).astype(BF16)
    high, low = split_int(asked[...])
    spread = 128.0 * dot_nn(peer, high) + dot_nn(peer, low)
    slot = lax.broadcasted_iota(jnp.int32, (slots, cap), 0) % cap
    keep = slot == lax.broadcasted_iota(jnp.int32, (slots, cap), 1)
    column = jnp.sum(jnp.where(keep, spread, 0.0), axis=1, keepdims=True)
    hot[...] = one_hot(column.astype(jnp.int32), vocab).astype(BF16)
    for k in range(steps):
        ins[k].wait()
        found[k] = dot_nn(hot[...], rows[k]).astype(BF16).reshape(shards, cap, width)
        outs[k].start()
    for copy in outs:
        copy.wait()


def pick_rows(asked, table, firsts):
    shards, cap = asked.shape
    vocab, cols = table.shape
    slots = shards * cap
    steps = 4
    width = cols // steps
    return pl.pallas_call(
        pick_kernel,
        in_specs=[full(asked.shape), pl.BlockSpec(memory_space=pl.ANY)]
        + [pl.BlockSpec(memory_space=pl.ANY)] * len(firsts),
        out_specs=pl.BlockSpec(memory_space=pl.ANY),
        out_shape=jax.ShapeDtypeStruct((shards, cap, cols), BF16),
        scratch_shapes=[
            pltpu.VMEM((slots, vocab), BF16),
            pltpu.VMEM((steps, vocab, width), BF16),
            pltpu.VMEM((steps, shards, cap, width), BF16),
            pltpu.SemaphoreType.DMA((steps,)),
            pltpu.SemaphoreType.DMA((steps,)),
        ],
        compiler_params=pltpu.CompilerParams(vmem_limit_bytes=GRANT),
        cost_estimate=pl.CostEstimate(
            flops=2 * slots * vocab * cols, bytes_accessed=2 * cols * (vocab + slots), transcendentals=0
        ),
        name="pick_rows",
    )(asked, table, *firsts)


def place_kernel(place, answered, *refs):
    part, turned = refs[-2:]
    tokens, slots = part.shape[0], answered.shape[0]
    width = turned.shape[2]
    put = one_hot(place[...], slots).astype(BF16)
    for t in range(turned.shape[0]):
        rows = dot_nn(put, answered[:, t * width : (t + 1) * width]).astype(BF16)
        part[:, t * width : (t + 1) * width] = rows
        turned[t] = rows


def place_rows(place, answered, copies, firsts):
    tokens = place.shape[0]
    slots, cols = answered.shape
    vmem = pl.BlockSpec(memory_space=pltpu.VMEM)
    return pl.pallas_call(
        place_kernel,
        in_specs=[vmem, vmem] + [pl.BlockSpec(memory_space=pl.ANY)] * len(firsts),
        out_specs=[vmem, vmem],
        out_shape=[
            jax.ShapeDtypeStruct((tokens, cols), BF16),
            jax.ShapeDtypeStruct((copies, tokens, cols // copies), BF16),
        ],
        compiler_params=pltpu.CompilerParams(vmem_limit_bytes=16 * 2**20),
        cost_estimate=pl.CostEstimate(
            flops=2 * slots * tokens * cols, bytes_accessed=2 * cols * (slots + 2 * tokens), transcendentals=0
        ),
        name="place_rows",
    )(place, answered, *firsts)


def project_kernel(me, p0, p1, p2, p3, basis, gained, first, second, out, square):
    step = pl.program_id(0)
    r = basis.shape[1]
    for k, piece in enumerate((p0, p1, p2, p3)):

        @pl.when(step == k)
        def _(k=k, piece=piece):
            x = piece[...]
            xf = x.astype(F32)
            q = jnp.broadcast_to(jnp.sum(xf * xf, axis=1, keepdims=True), square.shape)
            a, b = dot_nn(x, basis[...]), dot_nn(x, gained[...])
            if k == 0:
                out[:, 0:r] = a
                out[:, r:] = b
                square[...] = q
            else:
                out[:, 0:r] += a
                out[:, r:] += b
                square[...] += q


def project(me, pieces, basis, gained, first, second):
    tokens, cols = pieces[0].shape
    r, h = basis.shape[1], gained.shape[1]
    return pl.pallas_call(
        project_kernel,
        grid_spec=pltpu.PrefetchScalarGridSpec(
            num_scalar_prefetch=1,
            grid=(4,),
            in_specs=[full((tokens, cols))] * 4
            + [
                pl.BlockSpec((cols, r), lambda k, me: (k ^ me[0], 0)),
                pl.BlockSpec((cols, h), lambda k, me: (k ^ me[0], 0)),
                pl.BlockSpec(memory_space=pl.ANY),
                pl.BlockSpec(memory_space=pl.ANY),
            ],
            out_specs=[full((tokens, r + h)), full((tokens, 128))],
        ),
        out_shape=[
            jax.ShapeDtypeStruct((tokens, r + h), F32),
            jax.ShapeDtypeStruct((tokens, 128), F32),
        ],
        compiler_params=pltpu.CompilerParams(vmem_limit_bytes=24 * 2**20),
        cost_estimate=pl.CostEstimate(
            flops=8 * tokens * cols * (r + h), bytes_accessed=8 * cols * (r + h + tokens), transcendentals=0
        ),
        name="project",
    )(me, *pieces, basis, gained, first, second)


def chain_kernel(width, me_ref, cot, square, q0, q1, q2, q3, g0, g1, g2, g3, m0, m1, m2, m3, sent, packed,
                 pq, owns, mats, pres, acts, coefs, spans, invs, ins, ws):
    me = me_ref[0]
    r = cot.shape[1]
    h = q0.shape[1] - r
    for k, (q, g, m) in enumerate(((q0, g0, m0), (q1, g1, m1), (q2, g2, m2), (q3, g3, m3))):
        pq[k ^ me] = q[...]
        owns[k ^ me] = g[...]
        mats[k ^ me] = m[...]
    squares = square[:, 0:1]
    coefs[0] = jnp.zeros_like(coefs[0])
    for s in range(4):
        base_in = pq[s, :, r:]
        if s == 0:
            inv = lax.rsqrt(squares * (1.0 / width) + EPSILON)
            pre = inv * base_in
        else:
            c = coefs[s]
            base_sub = pq[s - 1, :, 0:r]
            span = base_sub + dot_nn(c, owns[s - 1, h:, :])
            total = squares + jnp.sum(c.astype(F32) * (base_sub + span), axis=1, keepdims=True)
            inv = lax.rsqrt(jnp.maximum(total, 0.0) * (1.0 / width) + EPSILON)
            pre = inv * (base_in + dot_nn(c, mats[s, :, r:]))
            spans[s] = span
        invs[s] = jnp.broadcast_to(inv, invs.shape[1:])
        pres[s] = pre
        act = (pre / (1.0 + jnp.exp(-pre))).astype(BF16)
        acts[s] = act
        new = dot_nn(act, owns[s, 0:h, :])
        if s > 0:
            new = new + dot_nn(c, mats[s, :, 0:r])
        coefs[s + 1] = new.astype(BF16)
    arrived = cot[...]
    for s in (3, 2, 1, 0):
        ins[s] = arrived
        pre = pres[s]
        sg = 1.0 / (1.0 + jnp.exp(-pre))
        gp = dot_nt(arrived, owns[s, 0:h, :]) * sg * (1.0 + pre * (1.0 - sg))
        inv = invs[s, :, 0:1]
        ws[s] = (gp * inv).astype(BF16)
        if s > 0:
            mean = jnp.sum(gp * pre, axis=1, keepdims=True) * (1.0 / width)
            back = dot_nt(gp.astype(BF16), mats[s, :, r:]) - (inv * mean) * spans[s]
            arrived = (dot_nt(arrived, mats[s, :, 0:r]) + inv * back).astype(BF16)
    sent[...] = coefs[me + 1]
    w = ws[me]
    row = (w, dot_tn(acts[me], ins[me]).astype(BF16), dot_tn(w, coefs[me]).astype(BF16))
    for t in range(packed.shape[0]):
        at = 0
        for v in row:
            packed[t, :, at : at + v.shape[1]] = v
            at += v.shape[1]


def chain(me, cot, square, pq, owns, mats, width, copies):
    tokens, r = cot.shape
    h = pq[0].shape[1] - r
    vmem = pl.BlockSpec(memory_space=pltpu.VMEM)
    return pl.pallas_call(
        functools.partial(chain_kernel, width),
        in_specs=[pl.BlockSpec(memory_space=pltpu.SMEM)] + [vmem] * 14,
        out_specs=[vmem, vmem],
        out_shape=[
            jax.ShapeDtypeStruct((tokens, r), BF16),
            jax.ShapeDtypeStruct((copies, tokens, h + 2 * r), BF16),
        ],
        scratch_shapes=[
            pltpu.VMEM((4, tokens, r + h), F32),
            pltpu.VMEM((4,) + owns[0].shape, BF16),
            pltpu.VMEM((4,) + mats[0].shape, BF16),
            pltpu.VMEM((4, tokens, h), F32),
            pltpu.VMEM((4, tokens, h), BF16),
            pltpu.VMEM((5, tokens, r), BF16),
            pltpu.VMEM((4, tokens, r), F32),
            pltpu.VMEM((4, tokens, 128), F32),
            pltpu.VMEM((4, tokens, r), BF16),
            pltpu.VMEM((4, tokens, h), BF16),
        ],
        compiler_params=pltpu.CompilerParams(vmem_limit_bytes=32 * 2**20),
        cost_estimate=pl.CostEstimate(flops=4 * 10**9, bytes_accessed=6 * 2**20, transcendentals=10**6),
        name="chain",
    )(me, cot, square, *pq, *owns, *mats)


def share_kernel(me_ref, packed, t0, t1, t2, t3, rows_own, rows_prev, out):
    me = me_ref[0]
    group, tokens, wide = packed.shape
    r = rows_own.shape[2]
    h = wide - 2 * r
    both = packed[0, :, h:].astype(F32)
    for g in range(1, group):
        both = both + packed[g, :, h:].astype(F32)
    v, uh = both[:, 0:r], both[:, r:].astype(BF16)
    vh = v.astype(BF16)
    vl = (v - vh.astype(F32)).astype(BF16)
    wt = jnp.concatenate([packed[g, :, 0:h].astype(F32).T.astype(BF16) for g in range(group)], axis=1)
    for k, piece in enumerate((t0, t1, t2, t3)):
        c = k ^ me
        xs = (dot_nn(wt, piece[...]) + dot_nt(uh, rows_prev[c])).astype(BF16)
        own = rows_own[c]
        os = (dot_nt(vh, own) + dot_nt(vl, own)).astype(BF16)
        n = xs.shape[1] // 2
        for e in range(2):
            out[2 * c + e, 0:h, :] = xs[:, e * n : (e + 1) * n]
            out[2 * c + e, h:, :] = os[:, e * n : (e + 1) * n]


def share(me, packed, pieces, rows_own, rows_prev):
    h = packed.shape[2] - 2 * rows_own.shape[2]
    cs, n, _ = rows_own.shape
    vmem = pl.BlockSpec(memory_space=pltpu.VMEM)
    return pl.pallas_call(
        share_kernel,
        in_specs=[pl.BlockSpec(memory_space=pltpu.SMEM)] + [vmem] * 7,
        out_specs=vmem,
        out_shape=jax.ShapeDtypeStruct((2 * cs, 2 * h, n // 2), BF16),
        compiler_params=pltpu.CompilerParams(vmem_limit_bytes=32 * 2**20),
        cost_estimate=pl.CostEstimate(flops=2 * 10**9, bytes_accessed=6 * 2**20, transcendentals=0),
        name="share",
    )(me, packed, *pieces, rows_own, rows_prev)


def finish_kernel(arrived, weight_in, gain, grad_in, grad_out, grad_gain, shares, sem):
    h = shares.shape[1] // 2
    copy = pltpu.make_async_copy(arrived, shares, sem)
    copy.start()
    copy.wait()
    total = jnp.sum(shares[...].astype(F32), axis=0)
    plain = total[0:h]
    grad_out[...] = total[h:]
    grad_in[...] = (plain * gain[...]).T
    grad_gain[...] = jnp.sum(plain * weight_in[...].astype(F32).T, axis=0, keepdims=True)


def finish(shares, weight_in, gain):
    _, twice, n = shares.shape
    h = twice // 2
    return pl.pallas_call(
        finish_kernel,
        in_specs=[pl.BlockSpec(memory_space=pl.ANY), full((n, h)), full((1, n))],
        out_specs=[full((n, h)), full((h, n)), full((1, n))],
        out_shape=[
            jax.ShapeDtypeStruct((n, h), F32),
            jax.ShapeDtypeStruct((h, n), F32),
            jax.ShapeDtypeStruct((1, n), F32),
        ],
        scratch_shapes=[pltpu.VMEM(shares.shape, BF16), pltpu.SemaphoreType.DMA],
        compiler_params=pltpu.CompilerParams(vmem_limit_bytes=16 * 2**20),
        cost_estimate=pl.CostEstimate(flops=10**6, bytes_accessed=2**20, transcendentals=0),
        name="finish",
    )(shares, weight_in, gain)


def per_device(
    token_ids, embed_table, subspace, adapter_in, adapter_out, norm_gain, coef_cotangent
):
    tokens = token_ids.shape[0]
    zl, x = lax.axis_index(ZL), lax.axis_index(X)
    shards = lax.axis_size(DP)
    group = lax.axis_size(GATHER)
    section = lax.axis_index(SEC)
    me = jnp.reshape(section, (1,)).astype(jnp.int32)
    dp = lax.axis_index(DP)
    vocab, cols = embed_table.shape
    basis, weight_in, weight_out = subspace[0], adapter_in[0], adapter_out[0]
    d, r = basis.shape
    h = weight_in.shape[1]
    block = d // shards

    x_at = jnp.reshape(x, (1,)).astype(jnp.int32)
    place, requests, rows_x = request(
        x_at, token_ids.reshape(1, tokens), basis.reshape(8, 4, 2 * block, r), vocab, shards
    )
    prev_x = lax.ppermute(rows_x, SEC, [(0, 1), (1, 2), (2, 3)])
    asked = lax.all_to_all(requests, DP, split_axis=0, concat_axis=0, tiled=True)
    found = pick_rows(asked, embed_table, (prev_x,))
    answered = lax.all_to_all(found, DP, split_axis=0, concat_axis=0, tiled=True)

    crossed = cross_products(x_at, basis, weight_in, norm_gain, prev_x, found)
    crossed = sum_over_x(crossed)
    mats = gather_peers(crossed)

    part, turned = place_rows(place, answered.reshape(shards * CAP, cols), group, (crossed,))
    gained, own = weights(basis, weight_in, norm_gain, weight_out, (part,))
    owns = gather_peers(own)
    turned = ordered(turned, mats[2])
    pieces = gather_peers(part)
    turned = lax.all_to_all(turned, GATHER, split_axis=0, concat_axis=0, tiled=True)
    pq, square = project(me, pieces, basis, gained, turned, mats[2])
    pqs = gather_peers(pq)
    turned = gather_peers(turned.reshape(group * tokens, cols // group))

    sent, packed = chain(me, coef_cotangent, square, pqs, owns, mats, d, group)
    packed = lax.all_to_all(packed, GATHER, split_axis=0, concat_axis=0, tiled=True)
    rows_own = lax.dynamic_index_in_dim(rows_x.reshape(4, 2, 2 * block, r), zl, 1, False)
    rows_prev = lax.dynamic_index_in_dim(prev_x.reshape(4, 2, 2 * block, r), zl, 1, False)
    shares = share(me, packed, turned, rows_own, rows_prev)
    shares = lax.all_to_all(shares, REDUCE, split_axis=0, concat_axis=0, tiled=True)
    in_block = lax.dynamic_slice_in_dim(weight_in, dp * block, block, 0)
    gain_block = lax.dynamic_slice_in_dim(norm_gain, dp * block, block, 1)
    grad_in, grad_out, grad_gain = finish(shares, in_block, gain_block)
    return sent[None], grad_in[None], grad_out[None], grad_gain


def solution(mesh):
    fine = Mesh(mesh.devices.reshape(2, 2, 4, 2, 4, 2), (YL, CO, ZH, ZL, X, YH))
    return jax.shard_map(
        per_device,
        mesh=fine,
        in_specs=(
            P(DP),
            P(DP, SEC),
            P(SEC, None, None),
            P(SEC, None, None),
            P(SEC, None, None),
            P(SEC, None),
            P(DP, None),
        ),
        out_specs=(
            P(SEC, DP, None),
            P(SEC, DP, None),
            P(SEC, None, DP),
            P(SEC, DP),
        ),
        check_vma=False,
    )
```

```python
import functools

import jax
import jax.numpy as jnp
from jax import lax
from jax.experimental import pallas as pl
from jax.experimental.pallas import tpu as pltpu
from jax.sharding import Mesh, PartitionSpec as P

CAP = 4
EPSILON = 1e-05
GRANT = 63 * 2**20
F32, BF16 = jnp.float32, jnp.bfloat16
YL, CO, ZH, ZL, X, YH = "yl", "co", "zh", "zl", "x", "yh"
DP = (ZH, ZL, X, YH)
SEC = (YL, CO)
GATHER = (ZL, X)
REDUCE = (ZH, YH)


def dot_nn(a, b):
    return lax.dot_general(a, b, (((1,), (0,)), ((), ())), preferred_element_type=F32)


def dot_nt(a, b):
    return lax.dot_general(a, b, (((1,), (1,)), ((), ())), preferred_element_type=F32)


def dot_tn(a, b):
    return lax.dot_general(a, b, (((0,), (0,)), ((), ())), preferred_element_type=F32)


def swap(x, axis):
    return lax.ppermute(x, axis, [(0, 1), (1, 0)])


def gather_peers(x):
    across = swap(x, YL)
    beside = swap(x, CO)
    return x, beside, across, swap(across, CO)


def full(shape):
    return pl.BlockSpec(shape, lambda *_: (0,) * len(shape))


def ordered(x, after):
    hbm = pl.BlockSpec(memory_space=pl.ANY)
    return pl.pallas_call(
        lambda *refs: None,
        in_specs=[hbm, hbm],
        out_specs=hbm,
        out_shape=jax.ShapeDtypeStruct(x.shape, x.dtype),
        input_output_aliases={0: 0},
        name="ordered",
    )(x, after)


def weights_kernel(basis, weight_in, gain, weight_out, *refs):
    gained, own, acc = refs[-3:]
    step = pl.program_id(0)
    h = weight_in.shape[1]

    @pl.when(step == 0)
    def _():
        acc[...] = jnp.zeros_like(acc)

    part = basis[...]
    gained[...] = scaled(weight_in[...], gain[...])
    acc[0:h, :] += dot_nn(weight_out[...], part)
    acc[h:, :] += dot_tn(part, part)

    @pl.when(step == pl.num_programs(0) - 1)
    def _():
        own[...] = acc[...].astype(BF16)


def weights(basis, weight_in, gain, weight_out, afters):
    d, r = basis.shape
    h = weight_in.shape[1]
    steps = 4
    rows = d // steps
    return pl.pallas_call(
        weights_kernel,
        grid=(steps,),
        in_specs=[
            pl.BlockSpec((rows, r), lambda k: (k, 0)),
            pl.BlockSpec((rows, h), lambda k: (k, 0)),
            pl.BlockSpec((1, rows), lambda k: (0, k)),
            pl.BlockSpec((h, rows), lambda k: (0, k)),
        ]
        + [pl.BlockSpec(memory_space=pl.ANY)] * len(afters),
        out_specs=[pl.BlockSpec((rows, h), lambda k: (k, 0)), full((r + h, r))],
        out_shape=[
            jax.ShapeDtypeStruct((d, h), BF16),
            jax.ShapeDtypeStruct((r + h, r), BF16),
        ],
        scratch_shapes=[pltpu.VMEM((r + h, r), F32)],
        compiler_params=pltpu.CompilerParams(vmem_limit_bytes=GRANT),
        cost_estimate=pl.CostEstimate(
            flops=2 * d * r * (r + h), bytes_accessed=4 * d * (r + h), transcendentals=0
        ),
        name="weights",
    )(basis, weight_in, gain, weight_out, *afters)


def scaled(rows, gain):
    column = jnp.broadcast_to(gain, (8, rows.shape[0])).T[:, 0:1]
    return (rows.astype(F32) * column).astype(BF16)


def cross_kernel(at, basis, weight_in, gain, prev, after, out, mine, ins, theirs, sems):
    blocks, rows, r = theirs.shape
    wait_all(
        start_all(
            [
                pltpu.make_async_copy(prev, theirs, sems.at[0]),
                pltpu.make_async_copy(basis.at[:, at[0]], mine, sems.at[1]),
                pltpu.make_async_copy(weight_in.at[:, at[0]], ins, sems.at[2]),
            ]
        )
    )
    first, second = 0.0, 0.0
    for k in range(blocks):
        start = pl.multiple_of((k * 4 + at[0]) * rows, rows)
        first = first + dot_tn(theirs[k], mine[k])
        second = second + dot_tn(theirs[k], scaled(ins[k], gain[:, pl.ds(start, rows)]))
    out[:, 0:r] = first.astype(BF16)
    out[:, r:] = second.astype(BF16)


def cross_products(at, basis, weight_in, gain, prev, after):
    blocks, rows, r = prev.shape
    h = weight_in.shape[1]
    hbm = pl.BlockSpec(memory_space=pl.ANY)
    return pl.pallas_call(
        cross_kernel,
        in_specs=[pl.BlockSpec(memory_space=pltpu.SMEM), hbm, hbm, full(gain.shape), hbm, hbm],
        out_specs=full((r, r + h)),
        out_shape=jax.ShapeDtypeStruct((r, r + h), BF16),
        scratch_shapes=[
            pltpu.VMEM((blocks, rows, r), BF16),
            pltpu.VMEM((blocks, rows, h), BF16),
            pltpu.VMEM((blocks, rows, r), BF16),
            pltpu.SemaphoreType.DMA((3,)),
        ],
        compiler_params=pltpu.CompilerParams(vmem_limit_bytes=GRANT),
        cost_estimate=pl.CostEstimate(
            flops=2 * blocks * rows * r * (r + h),
            bytes_accessed=2 * blocks * rows * (2 * r + h),
            transcendentals=0,
        ),
        name="cross_products",
    )(at, basis.reshape(blocks, 4, rows, r), weight_in.reshape(blocks, 4, rows, h), gain, prev, after)


def sum_over_x(v):
    total = v.astype(F32)
    for k in (1, 2, 3):
        total = total + lax.ppermute(v, X, [(i, (i + k) % 4) for i in range(4)]).astype(F32)
    return total.astype(BF16)


def start_all(copies):
    for copy in copies:
        copy.start()
    return copies


def wait_all(copies):
    for copy in copies:
        copy.wait()


def one_hot(column, n):
    lanes = lax.broadcasted_iota(jnp.int32, (column.shape[0], n), 1)
    return (column == lanes).astype(F32)


def split_int(v):
    return (v // 128).astype(F32).astype(BF16), (v % 128).astype(F32).astype(BF16)


def request_kernel(vocab, at, ids, basis, place, requests, rows, sem):
    copy = pltpu.make_async_copy(basis.at[:, at[0]], rows, sem)
    copy.start()
    tokens, shards = ids.shape[1], requests.shape[0]
    column = jnp.broadcast_to(ids[...], (8, tokens)).T[:, 0:1]
    first = lax.broadcasted_iota(jnp.int32, (tokens, shards), 1) * vocab
    mine = (column >= first) & (column < first + vocab)
    matches = mine.astype(F32)
    local = jnp.sum(jnp.where(mine, column - first, 0), axis=1, keepdims=True)
    owner = jnp.sum(jnp.where(mine, first // vocab, 0), axis=1, keepdims=True)
    earlier = lax.broadcasted_iota(jnp.int32, (tokens, tokens), 0) > lax.broadcasted_iota(
        jnp.int32, (tokens, tokens), 1
    )
    half = matches.astype(BF16)
    before = dot_nn(earlier.astype(F32).astype(BF16), half)
    position = jnp.sum(matches * before, axis=1, keepdims=True).astype(jnp.int32)
    place[...] = owner * CAP + position
    slot = one_hot(position, 128)
    high, low = split_int(local)
    found = 128.0 * dot_tn(half, (slot * high.astype(F32)).astype(BF16))
    found = found + dot_tn(half, (slot * low.astype(F32)).astype(BF16))
    requests[...] = found[:, 0:CAP].astype(jnp.int32)
    copy.wait()


def request(at, ids, basis, vocab, shards):
    tokens = ids.shape[1]
    blocks, _, rows, r = basis.shape
    hbm = pl.BlockSpec(memory_space=pl.ANY)
    return pl.pallas_call(
        functools.partial(request_kernel, vocab),
        in_specs=[pl.BlockSpec(memory_space=pltpu.SMEM), full(ids.shape), hbm],
        out_specs=[full((tokens, 1)), full((shards, CAP)), full((blocks, rows, r))],
        out_shape=[
            jax.ShapeDtypeStruct((tokens, 1), jnp.int32),
            jax.ShapeDtypeStruct((shards, CAP), jnp.int32),
            jax.ShapeDtypeStruct((blocks, rows, r), BF16),
        ],
        scratch_shapes=[pltpu.SemaphoreType.DMA],
        compiler_params=pltpu.CompilerParams(vmem_limit_bytes=GRANT),
        cost_estimate=pl.CostEstimate(flops=10**7, bytes_accessed=2**21, transcendentals=0),
        name="request",
    )(at, ids, basis)


def pick_kernel(asked, table, *refs):
    out, hot, rows, found, in_sems, out_sems = refs[-6:]
    shards, cap = asked.shape
    slots, vocab = hot.shape
    steps, _, width = rows.shape
    ins = [
        pltpu.make_async_copy(table.at[:, pl.ds(k * width, width)], rows.at[k], in_sems.at[k])
        for k in range(steps)
    ]
    outs = [
        pltpu.make_async_copy(found.at[k], out.at[:, :, pl.ds(k * width, width)], out_sems.at[k])
        for k in range(steps)
    ]
    for copy in ins:
        copy.start()
    peer = lax.broadcasted_iota(jnp.int32, (slots, shards), 0) // cap
    peer = (peer == lax.broadcasted_iota(jnp.int32, (slots, shards), 1)).astype(F32).astype(BF16)
    high, low = split_int(asked[...])
    spread = 128.0 * dot_nn(peer, high) + dot_nn(peer, low)
    slot = lax.broadcasted_iota(jnp.int32, (slots, cap), 0) % cap
    keep = slot == lax.broadcasted_iota(jnp.int32, (slots, cap), 1)
    column = jnp.sum(jnp.where(keep, spread, 0.0), axis=1, keepdims=True)
    hot[...] = one_hot(column.astype(jnp.int32), vocab).astype(BF16)
    for k in range(steps):
        ins[k].wait()
        found[k] = dot_nn(hot[...], rows[k]).astype(BF16).reshape(shards, cap, width)
        outs[k].start()
    for copy in outs:
        copy.wait()


def pick_rows(asked, table, firsts):
    shards, cap = asked.shape
    vocab, cols = table.shape
    slots = shards * cap
    steps = 4
    width = cols // steps
    return pl.pallas_call(
        pick_kernel,
        in_specs=[full(asked.shape), pl.BlockSpec(memory_space=pl.ANY)]
        + [pl.BlockSpec(memory_space=pl.ANY)] * len(firsts),
        out_specs=pl.BlockSpec(memory_space=pl.ANY),
        out_shape=jax.ShapeDtypeStruct((shards, cap, cols), BF16),
        scratch_shapes=[
            pltpu.VMEM((slots, vocab), BF16),
            pltpu.VMEM((steps, vocab, width), BF16),
            pltpu.VMEM((steps, shards, cap, width), BF16),
            pltpu.SemaphoreType.DMA((steps,)),
            pltpu.SemaphoreType.DMA((steps,)),
        ],
        compiler_params=pltpu.CompilerParams(vmem_limit_bytes=GRANT),
        cost_estimate=pl.CostEstimate(
            flops=2 * slots * vocab * cols, bytes_accessed=2 * cols * (vocab + slots), transcendentals=0
        ),
        name="pick_rows",
    )(asked, table, *firsts)


def place_kernel(place, answered, *refs):
    part, turned = refs[-2:]
    tokens, slots = part.shape[0], answered.shape[0]
    width = turned.shape[2]
    put = one_hot(place[...], slots).astype(BF16)
    for t in range(turned.shape[0]):
        rows = dot_nn(put, answered[:, t * width : (t + 1) * width]).astype(BF16)
        part[:, t * width : (t + 1) * width] = rows
        turned[t] = rows


def place_rows(place, answered, copies, firsts):
    tokens = place.shape[0]
    slots, cols = answered.shape
    vmem = pl.BlockSpec(memory_space=pltpu.VMEM)
    return pl.pallas_call(
        place_kernel,
        in_specs=[vmem, vmem] + [pl.BlockSpec(memory_space=pl.ANY)] * len(firsts),
        out_specs=[vmem, vmem],
        out_shape=[
            jax.ShapeDtypeStruct((tokens, cols), BF16),
            jax.ShapeDtypeStruct((copies, tokens, cols // copies), BF16),
        ],
        compiler_params=pltpu.CompilerParams(vmem_limit_bytes=16 * 2**20),
        cost_estimate=pl.CostEstimate(
            flops=2 * slots * tokens * cols, bytes_accessed=2 * cols * (slots + 2 * tokens), transcendentals=0
        ),
        name="place_rows",
    )(place, answered, *firsts)


def project_kernel(me, p0, p1, p2, p3, basis, gained, first, second, out, square):
    step = pl.program_id(0)
    r = basis.shape[1]
    for k, piece in enumerate((p0, p1, p2, p3)):

        @pl.when(step == k)
        def _(k=k, piece=piece):
            x = piece[...]
            xf = x.astype(F32)
            q = jnp.broadcast_to(jnp.sum(xf * xf, axis=1, keepdims=True), square.shape)
            a, b = dot_nn(x, basis[...]), dot_nn(x, gained[...])
            if k == 0:
                out[:, 0:r] = a
                out[:, r:] = b
                square[...] = q
            else:
                out[:, 0:r] += a
                out[:, r:] += b
                square[...] += q


def project(me, pieces, basis, gained, first, second):
    tokens, cols = pieces[0].shape
    r, h = basis.shape[1], gained.shape[1]
    return pl.pallas_call(
        project_kernel,
        grid_spec=pltpu.PrefetchScalarGridSpec(
            num_scalar_prefetch=1,
            grid=(4,),
            in_specs=[full((tokens, cols))] * 4
            + [
                pl.BlockSpec((cols, r), lambda k, me: (k ^ me[0], 0)),
                pl.BlockSpec((cols, h), lambda k, me: (k ^ me[0], 0)),
                pl.BlockSpec(memory_space=pl.ANY),
                pl.BlockSpec(memory_space=pl.ANY),
            ],
            out_specs=[full((tokens, r + h)), full((tokens, 128))],
        ),
        out_shape=[
            jax.ShapeDtypeStruct((tokens, r + h), F32),
            jax.ShapeDtypeStruct((tokens, 128), F32),
        ],
        compiler_params=pltpu.CompilerParams(vmem_limit_bytes=24 * 2**20),
        cost_estimate=pl.CostEstimate(
            flops=8 * tokens * cols * (r + h), bytes_accessed=8 * cols * (r + h + tokens), transcendentals=0
        ),
        name="project",
    )(me, *pieces, basis, gained, first, second)


def chain_kernel(width, me_ref, cot, square, q0, q1, q2, q3, g0, g1, g2, g3, m0, m1, m2, m3, sent, packed,
                 pq, owns, mats, pres, acts, coefs, spans, invs, ins, ws):
    me = me_ref[0]
    r = cot.shape[1]
    h = q0.shape[1] - r
    for k, (q, g, m) in enumerate(((q0, g0, m0), (q1, g1, m1), (q2, g2, m2), (q3, g3, m3))):
        pq[k ^ me] = q[...]
        owns[k ^ me] = g[...]
        mats[k ^ me] = m[...]
    squares = square[:, 0:1]
    coefs[0] = jnp.zeros_like(coefs[0])
    for s in range(4):
        base_in = pq[s, :, r:]
        if s == 0:
            inv = lax.rsqrt(squares * (1.0 / width) + EPSILON)
            pre = inv * base_in
        else:
            c = coefs[s]
            base_sub = pq[s - 1, :, 0:r]
            span = base_sub + dot_nn(c, owns[s - 1, h:, :])
            total = squares + jnp.sum(c.astype(F32) * (base_sub + span), axis=1, keepdims=True)
            inv = lax.rsqrt(jnp.maximum(total, 0.0) * (1.0 / width) + EPSILON)
            pre = inv * (base_in + dot_nn(c, mats[s, :, r:]))
            spans[s] = span
        invs[s] = jnp.broadcast_to(inv, invs.shape[1:])
        pres[s] = pre
        act = (pre / (1.0 + jnp.exp(-pre))).astype(BF16)
        acts[s] = act
        new = dot_nn(act, owns[s, 0:h, :])
        if s > 0:
            new = new + dot_nn(c, mats[s, :, 0:r])
        coefs[s + 1] = new.astype(BF16)
    arrived = cot[...]
    for s in (3, 2, 1, 0):
        ins[s] = arrived
        pre = pres[s]
        sg = 1.0 / (1.0 + jnp.exp(-pre))
        gp = dot_nt(arrived, owns[s, 0:h, :]) * sg * (1.0 + pre * (1.0 - sg))
        inv = invs[s, :, 0:1]
        ws[s] = (gp * inv).astype(BF16)
        if s > 0:
            mean = jnp.sum(gp * pre, axis=1, keepdims=True) * (1.0 / width)
            back = dot_nt(gp.astype(BF16), mats[s, :, r:]) - (inv * mean) * spans[s]
            arrived = (dot_nt(arrived, mats[s, :, 0:r]) + inv * back).astype(BF16)
    sent[...] = coefs[me + 1]
    w = ws[me]
    row = (w, dot_tn(acts[me], ins[me]).astype(BF16), dot_tn(w, coefs[me]).astype(BF16))
    for t in range(packed.shape[0]):
        at = 0
        for v in row:
            packed[t, :, at : at + v.shape[1]] = v
            at += v.shape[1]


def chain(me, cot, square, pq, owns, mats, width, copies):
    tokens, r = cot.shape
    h = pq[0].shape[1] - r
    vmem = pl.BlockSpec(memory_space=pltpu.VMEM)
    return pl.pallas_call(
        functools.partial(chain_kernel, width),
        in_specs=[pl.BlockSpec(memory_space=pltpu.SMEM)] + [vmem] * 14,
        out_specs=[vmem, vmem],
        out_shape=[
            jax.ShapeDtypeStruct((tokens, r), BF16),
            jax.ShapeDtypeStruct((copies, tokens, h + 2 * r), BF16),
        ],
        scratch_shapes=[
            pltpu.VMEM((4, tokens, r + h), F32),
            pltpu.VMEM((4,) + owns[0].shape, BF16),
            pltpu.VMEM((4,) + mats[0].shape, BF16),
            pltpu.VMEM((4, tokens, h), F32),
            pltpu.VMEM((4, tokens, h), BF16),
            pltpu.VMEM((5, tokens, r), BF16),
            pltpu.VMEM((4, tokens, r), F32),
            pltpu.VMEM((4, tokens, 128), F32),
            pltpu.VMEM((4, tokens, r), BF16),
            pltpu.VMEM((4, tokens, h), BF16),
        ],
        compiler_params=pltpu.CompilerParams(vmem_limit_bytes=32 * 2**20),
        cost_estimate=pl.CostEstimate(flops=4 * 10**9, bytes_accessed=6 * 2**20, transcendentals=10**6),
        name="chain",
    )(me, cot, square, *pq, *owns, *mats)


def share_kernel(me_ref, packed, t0, t1, t2, t3, rows_own, rows_prev, out):
    me = me_ref[0]
    group, tokens, wide = packed.shape
    r = rows_own.shape[2]
    h = wide - 2 * r
    both = packed[0, :, h:].astype(F32)
    for g in range(1, group):
        both = both + packed[g, :, h:].astype(F32)
    v, uh = both[:, 0:r], both[:, r:].astype(BF16)
    vh = v.astype(BF16)
    vl = (v - vh.astype(F32)).astype(BF16)
    wt = jnp.concatenate([packed[g, :, 0:h].astype(F32).T.astype(BF16) for g in range(group)], axis=1)
    for k, piece in enumerate((t0, t1, t2, t3)):
        c = k ^ me
        xs = (dot_nn(wt, piece[...]) + dot_nt(uh, rows_prev[c])).astype(BF16)
        own = rows_own[c]
        os = (dot_nt(vh, own) + dot_nt(vl, own)).astype(BF16)
        n = xs.shape[1] // 2
        for e in range(2):
            out[2 * c + e, 0:h, :] = xs[:, e * n : (e + 1) * n]
            out[2 * c + e, h:, :] = os[:, e * n : (e + 1) * n]


def share(me, packed, pieces, rows_own, rows_prev):
    h = packed.shape[2] - 2 * rows_own.shape[2]
    cs, n, _ = rows_own.shape
    vmem = pl.BlockSpec(memory_space=pltpu.VMEM)
    return pl.pallas_call(
        share_kernel,
        in_specs=[pl.BlockSpec(memory_space=pltpu.SMEM)] + [vmem] * 7,
        out_specs=vmem,
        out_shape=jax.ShapeDtypeStruct((2 * cs, 2 * h, n // 2), BF16),
        compiler_params=pltpu.CompilerParams(vmem_limit_bytes=32 * 2**20),
        cost_estimate=pl.CostEstimate(flops=2 * 10**9, bytes_accessed=6 * 2**20, transcendentals=0),
        name="share",
    )(me, packed, *pieces, rows_own, rows_prev)


def finish_kernel(arrived, weight_in, gain, grad_in, grad_out, grad_gain, shares, sem):
    h = shares.shape[1] // 2
    copy = pltpu.make_async_copy(arrived, shares, sem)
    copy.start()
    copy.wait()
    total = jnp.sum(shares[...].astype(F32), axis=0)
    plain = total[0:h]
    grad_out[...] = total[h:]
    grad_in[...] = (plain * gain[...]).T
    grad_gain[...] = jnp.sum(plain * weight_in[...].astype(F32).T, axis=0, keepdims=True)


def finish(shares, weight_in, gain):
    _, twice, n = shares.shape
    h = twice // 2
    return pl.pallas_call(
        finish_kernel,
        in_specs=[pl.BlockSpec(memory_space=pl.ANY), full((n, h)), full((1, n))],
        out_specs=[full((n, h)), full((h, n)), full((1, n))],
        out_shape=[
            jax.ShapeDtypeStruct((n, h), F32),
            jax.ShapeDtypeStruct((h, n), F32),
            jax.ShapeDtypeStruct((1, n), F32),
        ],
        scratch_shapes=[pltpu.VMEM(shares.shape, BF16), pltpu.SemaphoreType.DMA],
        compiler_params=pltpu.CompilerParams(vmem_limit_bytes=16 * 2**20),
        cost_estimate=pl.CostEstimate(flops=10**6, bytes_accessed=2**20, transcendentals=0),
        name="finish",
    )(shares, weight_in, gain)


def per_device(
    token_ids, embed_table, subspace, adapter_in, adapter_out, norm_gain, coef_cotangent
):
    tokens = token_ids.shape[0]
    zl, x = lax.axis_index(ZL), lax.axis_index(X)
    shards = lax.axis_size(DP)
    group = lax.axis_size(GATHER)
    section = lax.axis_index(SEC)
    me = jnp.reshape(section, (1,)).astype(jnp.int32)
    dp = lax.axis_index(DP)
    vocab, cols = embed_table.shape
    basis, weight_in, weight_out = subspace[0], adapter_in[0], adapter_out[0]
    d, r = basis.shape
    h = weight_in.shape[1]
    block = d // shards

    x_at = jnp.reshape(x, (1,)).astype(jnp.int32)
    place, requests, rows_x = request(
        x_at, token_ids.reshape(1, tokens), basis.reshape(8, 4, 2 * block, r), vocab, shards
    )
    prev_x = lax.ppermute(rows_x, SEC, [(0, 1), (1, 2), (2, 3)])
    asked = lax.all_to_all(requests, DP, split_axis=0, concat_axis=0, tiled=True)
    found = pick_rows(asked, embed_table, (prev_x,))
    answered = lax.all_to_all(found, DP, split_axis=0, concat_axis=0, tiled=True)

    crossed = cross_products(x_at, basis, weight_in, norm_gain, prev_x, found)
    gained, own = weights(basis, weight_in, norm_gain, weight_out, (crossed,))
    owns = gather_peers(own)
    crossed = sum_over_x(crossed)
    mats = gather_peers(crossed)

    part, turned = place_rows(place, answered.reshape(shards * CAP, cols), group, (crossed, gained))
    turned = ordered(turned, mats[2])
    pieces = gather_peers(part)
    turned = lax.all_to_all(turned, GATHER, split_axis=0, concat_axis=0, tiled=True)
    pq, square = project(me, pieces, basis, gained, turned, mats[2])
    pqs = gather_peers(pq)
    turned = gather_peers(turned.reshape(group * tokens, cols // group))

    sent, packed = chain(me, coef_cotangent, square, pqs, owns, mats, d, group)
    packed = lax.all_to_all(packed, GATHER, split_axis=0, concat_axis=0, tiled=True)
    rows_own = lax.dynamic_index_in_dim(rows_x.reshape(4, 2, 2 * block, r), zl, 1, False)
    rows_prev = lax.dynamic_index_in_dim(prev_x.reshape(4, 2, 2 * block, r), zl, 1, False)
    shares = share(me, packed, turned, rows_own, rows_prev)
    shares = lax.all_to_all(shares, REDUCE, split_axis=0, concat_axis=0, tiled=True)
    in_block = lax.dynamic_slice_in_dim(weight_in, dp * block, block, 0)
    gain_block = lax.dynamic_slice_in_dim(norm_gain, dp * block, block, 1)
    grad_in, grad_out, grad_gain = finish(shares, in_block, gain_block)
    return sent[None], grad_in[None], grad_out[None], grad_gain


def solution(mesh):
    fine = Mesh(mesh.devices.reshape(2, 2, 4, 2, 4, 2), (YL, CO, ZH, ZL, X, YH))
    return jax.shard_map(
        per_device,
        mesh=fine,
        in_specs=(
            P(DP),
            P(DP, SEC),
            P(SEC, None, None),
            P(SEC, None, None),
            P(SEC, None, None),
            P(SEC, None),
            P(DP, None),
        ),
        out_specs=(
            P(SEC, DP, None),
            P(SEC, DP, None),
            P(SEC, None, DP),
            P(SEC, DP),
        ),
        check_vma=False,
    )
```

```python
import functools

import jax
import jax.numpy as jnp
from jax import lax
from jax.experimental import pallas as pl
from jax.experimental.pallas import tpu as pltpu
from jax.sharding import Mesh, PartitionSpec as P

CAP = 4
EPSILON = 1e-05
GRANT = 63 * 2**20
F32, BF16 = jnp.float32, jnp.bfloat16
YL, CO, ZH, ZL, X, YH = "yl", "co", "zh", "zl", "x", "yh"
DP = (ZH, ZL, X, YH)
SEC = (YL, CO)
GATHER = (ZL, X)
REDUCE = (ZH, YH)


def dot_nn(a, b):
    return lax.dot_general(a, b, (((1,), (0,)), ((), ())), preferred_element_type=F32)


def dot_nt(a, b):
    return lax.dot_general(a, b, (((1,), (1,)), ((), ())), preferred_element_type=F32)


def dot_tn(a, b):
    return lax.dot_general(a, b, (((0,), (0,)), ((), ())), preferred_element_type=F32)


def swap(x, axis):
    return lax.ppermute(x, axis, [(0, 1), (1, 0)])


def gather_peers(x):
    across = swap(x, YL)
    beside = swap(x, CO)
    return x, beside, across, swap(across, CO)


def gather_direct(x):
    return x, swap(x, CO), swap(x, YL), lax.ppermute(x, SEC, [(0, 3), (1, 2), (2, 1), (3, 0)])


def full(shape):
    return pl.BlockSpec(shape, lambda *_: (0,) * len(shape))


def weights_kernel(basis, weight_in, gain, weight_out, *refs):
    gained, own, acc = refs[-3:]
    step = pl.program_id(0)
    h = weight_in.shape[1]

    @pl.when(step == 0)
    def _():
        acc[...] = jnp.zeros_like(acc)

    part = basis[...]
    gained[...] = scaled(weight_in[...], gain[...])
    acc[0:h, :] += dot_nn(weight_out[...], part)
    acc[h:, :] += dot_tn(part, part)

    @pl.when(step == pl.num_programs(0) - 1)
    def _():
        own[...] = acc[...].astype(BF16)


def weights(basis, weight_in, gain, weight_out, afters):
    d, r = basis.shape
    h = weight_in.shape[1]
    steps = 4
    rows = d // steps
    return pl.pallas_call(
        weights_kernel,
        grid=(steps,),
        in_specs=[
            pl.BlockSpec((rows, r), lambda k: (k, 0)),
            pl.BlockSpec((rows, h), lambda k: (k, 0)),
            pl.BlockSpec((1, rows), lambda k: (0, k)),
            pl.BlockSpec((h, rows), lambda k: (0, k)),
        ]
        + [pl.BlockSpec(memory_space=pl.ANY)] * len(afters),
        out_specs=[pl.BlockSpec((rows, h), lambda k: (k, 0)), full((r + h, r))],
        out_shape=[
            jax.ShapeDtypeStruct((d, h), BF16),
            jax.ShapeDtypeStruct((r + h, r), BF16),
        ],
        scratch_shapes=[pltpu.VMEM((r + h, r), F32)],
        compiler_params=pltpu.CompilerParams(vmem_limit_bytes=GRANT),
        cost_estimate=pl.CostEstimate(
            flops=2 * d * r * (r + h), bytes_accessed=4 * d * (r + h), transcendentals=0
        ),
        name="weights",
    )(basis, weight_in, gain, weight_out, *afters)


def scaled(rows, gain):
    column = jnp.broadcast_to(gain, (8, rows.shape[0])).T[:, 0:1]
    return (rows.astype(F32) * column).astype(BF16)


def cross_kernel(at, basis, weight_in, gain, prev, after, out, mine, ins, theirs, sems):
    blocks, rows, r = theirs.shape
    wait_all(
        start_all(
            [
                pltpu.make_async_copy(prev, theirs, sems.at[0]),
                pltpu.make_async_copy(basis.at[:, at[0]], mine, sems.at[1]),
                pltpu.make_async_copy(weight_in.at[:, at[0]], ins, sems.at[2]),
            ]
        )
    )
    first, second = 0.0, 0.0
    for k in range(blocks):
        start = pl.multiple_of((k * 4 + at[0]) * rows, rows)
        first = first + dot_tn(theirs[k], mine[k])
        second = second + dot_tn(theirs[k], scaled(ins[k], gain[:, pl.ds(start, rows)]))
    out[:, 0:r] = first.astype(BF16)
    out[:, r:] = second.astype(BF16)


def cross_products(at, basis, weight_in, gain, prev, after):
    blocks, rows, r = prev.shape
    h = weight_in.shape[1]
    hbm = pl.BlockSpec(memory_space=pl.ANY)
    return pl.pallas_call(
        cross_kernel,
        in_specs=[pl.BlockSpec(memory_space=pltpu.SMEM), hbm, hbm, full(gain.shape), hbm, hbm],
        out_specs=full((r, r + h)),
        out_shape=jax.ShapeDtypeStruct((r, r + h), BF16),
        scratch_shapes=[
            pltpu.VMEM((blocks, rows, r), BF16),
            pltpu.VMEM((blocks, rows, h), BF16),
            pltpu.VMEM((blocks, rows, r), BF16),
            pltpu.SemaphoreType.DMA((3,)),
        ],
        compiler_params=pltpu.CompilerParams(vmem_limit_bytes=GRANT),
        cost_estimate=pl.CostEstimate(
            flops=2 * blocks * rows * r * (r + h),
            bytes_accessed=2 * blocks * rows * (2 * r + h),
            transcendentals=0,
        ),
        name="cross_products",
    )(at, basis.reshape(blocks, 4, rows, r), weight_in.reshape(blocks, 4, rows, h), gain, prev, after)


def sum_over_x(v):
    total = v.astype(F32)
    for k in (1, 2, 3):
        total = total + lax.ppermute(v, X, [(i, (i + k) % 4) for i in range(4)]).astype(F32)
    return total.astype(BF16)


def start_all(copies):
    for copy in copies:
        copy.start()
    return copies


def wait_all(copies):
    for copy in copies:
        copy.wait()


def one_hot(column, n):
    lanes = lax.broadcasted_iota(jnp.int32, (column.shape[0], n), 1)
    return (column == lanes).astype(F32)


def split_int(v):
    return (v // 128).astype(F32).astype(BF16), (v % 128).astype(F32).astype(BF16)


def request_kernel(vocab, at, ids, basis, place, requests, rows, sem):
    copy = pltpu.make_async_copy(basis.at[:, at[0]], rows, sem)
    copy.start()
    tokens, shards = ids.shape[1], requests.shape[0]
    column = jnp.broadcast_to(ids[...], (8, tokens)).T[:, 0:1]
    first = lax.broadcasted_iota(jnp.int32, (tokens, shards), 1) * vocab
    mine = (column >= first) & (column < first + vocab)
    matches = mine.astype(F32)
    local = jnp.sum(jnp.where(mine, column - first, 0), axis=1, keepdims=True)
    owner = jnp.sum(jnp.where(mine, first // vocab, 0), axis=1, keepdims=True)
    earlier = lax.broadcasted_iota(jnp.int32, (tokens, tokens), 0) > lax.broadcasted_iota(
        jnp.int32, (tokens, tokens), 1
    )
    half = matches.astype(BF16)
    before = dot_nn(earlier.astype(F32).astype(BF16), half)
    position = jnp.sum(matches * before, axis=1, keepdims=True).astype(jnp.int32)
    place[...] = owner * CAP + position
    slot = one_hot(position, 128)
    high, low = split_int(local)
    found = 128.0 * dot_tn(half, (slot * high.astype(F32)).astype(BF16))
    found = found + dot_tn(half, (slot * low.astype(F32)).astype(BF16))
    requests[...] = found[:, 0:CAP].astype(jnp.int32)
    copy.wait()


def request(at, ids, basis, vocab, shards):
    tokens = ids.shape[1]
    blocks, _, rows, r = basis.shape
    hbm = pl.BlockSpec(memory_space=pl.ANY)
    return pl.pallas_call(
        functools.partial(request_kernel, vocab),
        in_specs=[pl.BlockSpec(memory_space=pltpu.SMEM), full(ids.shape), hbm],
        out_specs=[full((tokens, 1)), full((shards, CAP)), full((blocks, rows, r))],
        out_shape=[
            jax.ShapeDtypeStruct((tokens, 1), jnp.int32),
            jax.ShapeDtypeStruct((shards, CAP), jnp.int32),
            jax.ShapeDtypeStruct((blocks, rows, r), BF16),
        ],
        scratch_shapes=[pltpu.SemaphoreType.DMA],
        compiler_params=pltpu.CompilerParams(vmem_limit_bytes=GRANT),
        cost_estimate=pl.CostEstimate(flops=10**7, bytes_accessed=2**21, transcendentals=0),
        name="request",
    )(at, ids, basis)


def pick_kernel(asked, table, *refs):
    out, hot, rows, found, in_sems, out_sems = refs[-6:]
    shards, cap = asked.shape
    slots, vocab = hot.shape
    steps, _, width = rows.shape
    ins = [
        pltpu.make_async_copy(table.at[:, pl.ds(k * width, width)], rows.at[k], in_sems.at[k])
        for k in range(steps)
    ]
    outs = [
        pltpu.make_async_copy(found.at[k], out.at[:, :, pl.ds(k * width, width)], out_sems.at[k])
        for k in range(steps)
    ]
    for copy in ins:
        copy.start()
    peer = lax.broadcasted_iota(jnp.int32, (slots, shards), 0) // cap
    peer = (peer == lax.broadcasted_iota(jnp.int32, (slots, shards), 1)).astype(F32).astype(BF16)
    high, low = split_int(asked[...])
    spread = 128.0 * dot_nn(peer, high) + dot_nn(peer, low)
    slot = lax.broadcasted_iota(jnp.int32, (slots, cap), 0) % cap
    keep = slot == lax.broadcasted_iota(jnp.int32, (slots, cap), 1)
    column = jnp.sum(jnp.where(keep, spread, 0.0), axis=1, keepdims=True)
    hot[...] = one_hot(column.astype(jnp.int32), vocab).astype(BF16)
    for k in range(steps):
        ins[k].wait()
        found[k] = dot_nn(hot[...], rows[k]).astype(BF16).reshape(shards, cap, width)
        outs[k].start()
    for copy in outs:
        copy.wait()


def pick_rows(asked, table, firsts):
    shards, cap = asked.shape
    vocab, cols = table.shape
    slots = shards * cap
    steps = 4
    width = cols // steps
    return pl.pallas_call(
        pick_kernel,
        in_specs=[full(asked.shape), pl.BlockSpec(memory_space=pl.ANY)]
        + [pl.BlockSpec(memory_space=pl.ANY)] * len(firsts),
        out_specs=pl.BlockSpec(memory_space=pl.ANY),
        out_shape=jax.ShapeDtypeStruct((shards, cap, cols), BF16),
        scratch_shapes=[
            pltpu.VMEM((slots, vocab), BF16),
            pltpu.VMEM((steps, vocab, width), BF16),
            pltpu.VMEM((steps, shards, cap, width), BF16),
            pltpu.SemaphoreType.DMA((steps,)),
            pltpu.SemaphoreType.DMA((steps,)),
        ],
        compiler_params=pltpu.CompilerParams(vmem_limit_bytes=GRANT),
        cost_estimate=pl.CostEstimate(
            flops=2 * slots * vocab * cols, bytes_accessed=2 * cols * (vocab + slots), transcendentals=0
        ),
        name="pick_rows",
    )(asked, table, *firsts)


def place_kernel(place, answered, *refs):
    part, turned = refs[-2:]
    tokens, slots = part.shape[0], answered.shape[0]
    width = turned.shape[2]
    put = one_hot(place[...], slots).astype(BF16)
    for t in range(turned.shape[0]):
        rows = dot_nn(put, answered[:, t * width : (t + 1) * width]).astype(BF16)
        part[:, t * width : (t + 1) * width] = rows
        turned[t] = rows


def place_rows(place, answered, copies, firsts):
    tokens = place.shape[0]
    slots, cols = answered.shape
    vmem = pl.BlockSpec(memory_space=pltpu.VMEM)
    return pl.pallas_call(
        place_kernel,
        in_specs=[vmem, vmem] + [pl.BlockSpec(memory_space=pl.ANY)] * len(firsts),
        out_specs=[vmem, vmem],
        out_shape=[
            jax.ShapeDtypeStruct((tokens, cols), BF16),
            jax.ShapeDtypeStruct((copies, tokens, cols // copies), BF16),
        ],
        compiler_params=pltpu.CompilerParams(vmem_limit_bytes=16 * 2**20),
        cost_estimate=pl.CostEstimate(
            flops=2 * slots * tokens * cols, bytes_accessed=2 * cols * (slots + 2 * tokens), transcendentals=0
        ),
        name="place_rows",
    )(place, answered, *firsts)


def project_kernel(me, p0, p1, p2, p3, basis, gained, first, second, out, square, acc):
    step = pl.program_id(0)
    r = basis.shape[1]
    for k, piece in enumerate((p0, p1, p2, p3)):

        @pl.when(step == k)
        def _(k=k, piece=piece):
            x = piece[...]
            xf = x.astype(F32)
            q = jnp.broadcast_to(jnp.sum(xf * xf, axis=1, keepdims=True), square.shape)
            a, b = dot_nn(x, basis[...]), dot_nn(x, gained[...])
            if k == 0:
                acc[:, 0:r] = a
                acc[:, r:] = b
                square[...] = q
            else:
                acc[:, 0:r] += a
                acc[:, r:] += b
                square[...] += q

    @pl.when(step == 3)
    def _():
        out[...] = acc[...].astype(BF16)


def project(me, pieces, basis, gained, first, second):
    tokens, cols = pieces[0].shape
    r, h = basis.shape[1], gained.shape[1]
    return pl.pallas_call(
        project_kernel,
        grid_spec=pltpu.PrefetchScalarGridSpec(
            num_scalar_prefetch=1,
            grid=(4,),
            in_specs=[full((tokens, cols))] * 4
            + [
                pl.BlockSpec((cols, r), lambda k, me: (k ^ me[0], 0)),
                pl.BlockSpec((cols, h), lambda k, me: (k ^ me[0], 0)),
                pl.BlockSpec(memory_space=pl.ANY),
                pl.BlockSpec(memory_space=pl.ANY),
            ],
            out_specs=[full((tokens, r + h)), full((tokens, 128))],
            scratch_shapes=[pltpu.VMEM((tokens, r + h), F32)],
        ),
        out_shape=[
            jax.ShapeDtypeStruct((tokens, r + h), BF16),
            jax.ShapeDtypeStruct((tokens, 128), F32),
        ],
        compiler_params=pltpu.CompilerParams(vmem_limit_bytes=24 * 2**20),
        cost_estimate=pl.CostEstimate(
            flops=8 * tokens * cols * (r + h), bytes_accessed=8 * cols * (r + h + tokens), transcendentals=0
        ),
        name="project",
    )(me, *pieces, basis, gained, first, second)


def chain_kernel(width, me_ref, cot, square, q0, q1, q2, q3, g0, g1, g2, g3, m0, m1, m2, m3, sent, packed,
                 pq, owns, mats, pres, acts, coefs, spans, invs, ins, ws):
    me = me_ref[0]
    r = cot.shape[1]
    h = q0.shape[1] - r
    for k, (q, g, m) in enumerate(((q0, g0, m0), (q1, g1, m1), (q2, g2, m2), (q3, g3, m3))):
        pq[k ^ me] = q[...].astype(F32)
        owns[k ^ me] = g[...]
        mats[k ^ me] = m[...]
    squares = square[:, 0:1]
    coefs[0] = jnp.zeros_like(coefs[0])
    for s in range(4):
        base_in = pq[s, :, r:]
        if s == 0:
            inv = lax.rsqrt(squares * (1.0 / width) + EPSILON)
            pre = inv * base_in
        else:
            c = coefs[s]
            base_sub = pq[s - 1, :, 0:r]
            span = base_sub + dot_nn(c, owns[s - 1, h:, :])
            total = squares + jnp.sum(c.astype(F32) * (base_sub + span), axis=1, keepdims=True)
            inv = lax.rsqrt(jnp.maximum(total, 0.0) * (1.0 / width) + EPSILON)
            pre = inv * (base_in + dot_nn(c, mats[s, :, r:]))
            spans[s] = span
        invs[s] = jnp.broadcast_to(inv, invs.shape[1:])
        pres[s] = pre
        act = (pre / (1.0 + jnp.exp(-pre))).astype(BF16)
        acts[s] = act
        new = dot_nn(act, owns[s, 0:h, :])
        if s > 0:
            new = new + dot_nn(c, mats[s, :, 0:r])
        coefs[s + 1] = new.astype(BF16)
    arrived = cot[...]
    for s in (3, 2, 1, 0):
        ins[s] = arrived
        pre = pres[s]
        sg = 1.0 / (1.0 + jnp.exp(-pre))
        gp = dot_nt(arrived, owns[s, 0:h, :]) * sg * (1.0 + pre * (1.0 - sg))
        inv = invs[s, :, 0:1]
        ws[s] = (gp * inv).astype(BF16)
        if s > 0:
            mean = jnp.sum(gp * pre, axis=1, keepdims=True) * (1.0 / width)
            back = dot_nt(gp.astype(BF16), mats[s, :, r:]) - (inv * mean) * spans[s]
            arrived = (dot_nt(arrived, mats[s, :, 0:r]) + inv * back).astype(BF16)
    sent[...] = coefs[me + 1]
    w = ws[me]
    row = (w, dot_tn(acts[me], ins[me]).astype(BF16), dot_tn(w, coefs[me]).astype(BF16))
    for t in range(packed.shape[0]):
        at = 0
        for v in row:
            packed[t, :, at : at + v.shape[1]] = v
            at += v.shape[1]


def chain(me, cot, square, pq, owns, mats, width, copies):
    tokens, r = cot.shape
    h = pq[0].shape[1] - r
    vmem = pl.BlockSpec(memory_space=pltpu.VMEM)
    return pl.pallas_call(
        functools.partial(chain_kernel, width),
        in_specs=[pl.BlockSpec(memory_space=pltpu.SMEM)] + [vmem] * 14,
        out_specs=[vmem, vmem],
        out_shape=[
            jax.ShapeDtypeStruct((tokens, r), BF16),
            jax.ShapeDtypeStruct((copies, tokens, h + 2 * r), BF16),
        ],
        scratch_shapes=[
            pltpu.VMEM((4, tokens, r + h), F32),
            pltpu.VMEM((4,) + owns[0].shape, BF16),
            pltpu.VMEM((4,) + mats[0].shape, BF16),
            pltpu.VMEM((4, tokens, h), F32),
            pltpu.VMEM((4, tokens, h), BF16),
            pltpu.VMEM((5, tokens, r), BF16),
            pltpu.VMEM((4, tokens, r), F32),
            pltpu.VMEM((4, tokens, 128), F32),
            pltpu.VMEM((4, tokens, r), BF16),
            pltpu.VMEM((4, tokens, h), BF16),
        ],
        compiler_params=pltpu.CompilerParams(vmem_limit_bytes=32 * 2**20),
        cost_estimate=pl.CostEstimate(flops=4 * 10**9, bytes_accessed=6 * 2**20, transcendentals=10**6),
        name="chain",
    )(me, cot, square, *pq, *owns, *mats)


def share_kernel(me_ref, packed, t0, t1, t2, t3, rows_own, rows_prev, out):
    me = me_ref[0]
    group, tokens, wide = packed.shape
    r = rows_own.shape[2]
    h = wide - 2 * r
    both = packed[0, :, h:].astype(F32)
    for g in range(1, group):
        both = both + packed[g, :, h:].astype(F32)
    v, uh = both[:, 0:r], both[:, r:].astype(BF16)
    vh = v.astype(BF16)
    vl = (v - vh.astype(F32)).astype(BF16)
    wt = jnp.concatenate([packed[g, :, 0:h].astype(F32).T.astype(BF16) for g in range(group)], axis=1)
    for k, piece in enumerate((t0, t1, t2, t3)):
        c = k ^ me
        xs = (dot_nn(wt, piece[...]) + dot_nt(uh, rows_prev[c])).astype(BF16)
        own = rows_own[c]
        os = (dot_nt(vh, own) + dot_nt(vl, own)).astype(BF16)
        n = xs.shape[1] // 2
        for e in range(2):
            out[2 * c + e, 0:h, :] = xs[:, e * n : (e + 1) * n]
            out[2 * c + e, h:, :] = os[:, e * n : (e + 1) * n]


def share(me, packed, pieces, rows_own, rows_prev):
    h = packed.shape[2] - 2 * rows_own.shape[2]
    cs, n, _ = rows_own.shape
    vmem = pl.BlockSpec(memory_space=pltpu.VMEM)
    return pl.pallas_call(
        share_kernel,
        in_specs=[pl.BlockSpec(memory_space=pltpu.SMEM)] + [vmem] * 7,
        out_specs=vmem,
        out_shape=jax.ShapeDtypeStruct((2 * cs, 2 * h, n // 2), BF16),
        compiler_params=pltpu.CompilerParams(vmem_limit_bytes=32 * 2**20),
        cost_estimate=pl.CostEstimate(flops=2 * 10**9, bytes_accessed=6 * 2**20, transcendentals=0),
        name="share",
    )(me, packed, *pieces, rows_own, rows_prev)


def finish_kernel(arrived, weight_in, gain, grad_in, grad_out, grad_gain, shares, sem):
    h = shares.shape[1] // 2
    copy = pltpu.make_async_copy(arrived, shares, sem)
    copy.start()
    copy.wait()
    total = jnp.sum(shares[...].astype(F32), axis=0)
    plain = total[0:h]
    grad_out[...] = total[h:]
    grad_in[...] = (plain * gain[...]).T
    grad_gain[...] = jnp.sum(plain * weight_in[...].astype(F32).T, axis=0, keepdims=True)


def finish(shares, weight_in, gain):
    _, twice, n = shares.shape
    h = twice // 2
    return pl.pallas_call(
        finish_kernel,
        in_specs=[pl.BlockSpec(memory_space=pl.ANY), full((n, h)), full((1, n))],
        out_specs=[full((n, h)), full((h, n)), full((1, n))],
        out_shape=[
            jax.ShapeDtypeStruct((n, h), F32),
            jax.ShapeDtypeStruct((h, n), F32),
            jax.ShapeDtypeStruct((1, n), F32),
        ],
        scratch_shapes=[pltpu.VMEM(shares.shape, BF16), pltpu.SemaphoreType.DMA],
        compiler_params=pltpu.CompilerParams(vmem_limit_bytes=16 * 2**20),
        cost_estimate=pl.CostEstimate(flops=10**6, bytes_accessed=2**20, transcendentals=0),
        name="finish",
    )(shares, weight_in, gain)


def per_device(
    token_ids, embed_table, subspace, adapter_in, adapter_out, norm_gain, coef_cotangent
):
    tokens = token_ids.shape[0]
    zl, x = lax.axis_index(ZL), lax.axis_index(X)
    shards = lax.axis_size(DP)
    group = lax.axis_size(GATHER)
    section = lax.axis_index(SEC)
    me = jnp.reshape(section, (1,)).astype(jnp.int32)
    dp = lax.axis_index(DP)
    vocab, cols = embed_table.shape
    basis, weight_in, weight_out = subspace[0], adapter_in[0], adapter_out[0]
    d, r = basis.shape
    h = weight_in.shape[1]
    block = d // shards

    x_at = jnp.reshape(x, (1,)).astype(jnp.int32)
    place, requests, rows_x = request(
        x_at, token_ids.reshape(1, tokens), basis.reshape(8, 4, 2 * block, r), vocab, shards
    )
    prev_x = lax.ppermute(rows_x, SEC, [(0, 1), (1, 2), (2, 3)])
    asked = lax.all_to_all(requests, DP, split_axis=0, concat_axis=0, tiled=True)
    found = pick_rows(asked, embed_table, (prev_x,))
    answered = lax.all_to_all(found, DP, split_axis=0, concat_axis=0, tiled=True)

    crossed = cross_products(x_at, basis, weight_in, norm_gain, prev_x, found)
    gained, own = weights(basis, weight_in, norm_gain, weight_out, (crossed,))
    owns = gather_peers(own)
    crossed = sum_over_x(crossed)
    mats = gather_peers(crossed)

    part, turned = place_rows(place, answered.reshape(shards * CAP, cols), group, (*owns[1:], mats[2]))
    pieces = gather_peers(part)
    turned = lax.all_to_all(turned, GATHER, split_axis=0, concat_axis=0, tiled=True)
    pq, square = project(me, pieces, basis, gained, turned, mats[2])
    pqs = gather_direct(pq)
    turned = gather_peers(turned.reshape(group * tokens, cols // group))

    sent, packed = chain(me, coef_cotangent, square, pqs, owns, mats, d, group)
    packed = lax.all_to_all(packed, GATHER, split_axis=0, concat_axis=0, tiled=True)
    rows_own = lax.dynamic_index_in_dim(rows_x.reshape(4, 2, 2 * block, r), zl, 1, False)
    rows_prev = lax.dynamic_index_in_dim(prev_x.reshape(4, 2, 2 * block, r), zl, 1, False)
    shares = share(me, packed, turned, rows_own, rows_prev)
    shares = lax.all_to_all(shares, REDUCE, split_axis=0, concat_axis=0, tiled=True)
    in_block = lax.dynamic_slice_in_dim(weight_in, dp * block, block, 0)
    gain_block = lax.dynamic_slice_in_dim(norm_gain, dp * block, block, 1)
    grad_in, grad_out, grad_gain = finish(shares, in_block, gain_block)
    return sent[None], grad_in[None], grad_out[None], grad_gain


def solution(mesh):
    fine = Mesh(mesh.devices.reshape(2, 2, 4, 2, 4, 2), (YL, CO, ZH, ZL, X, YH))
    return jax.shard_map(
        per_device,
        mesh=fine,
        in_specs=(
            P(DP),
            P(DP, SEC),
            P(SEC, None, None),
            P(SEC, None, None),
            P(SEC, None, None),
            P(SEC, None),
            P(DP, None),
        ),
        out_specs=(
            P(SEC, DP, None),
            P(SEC, DP, None),
            P(SEC, None, DP),
            P(SEC, DP),
        ),
        check_vma=False,
    )
```

```python
import functools

import jax
import jax.numpy as jnp
from jax import lax
from jax.experimental import pallas as pl
from jax.experimental.pallas import tpu as pltpu
from jax.sharding import Mesh, PartitionSpec as P

CAP = 4
EPSILON = 1e-05
GRANT = 63 * 2**20
F32, BF16 = jnp.float32, jnp.bfloat16
YL, CO, ZH, ZL, X, YH = "yl", "co", "zh", "zl", "x", "yh"
DP = (ZH, ZL, X, YH)
SEC = (YL, CO)
GATHER = (ZL, X)
REDUCE = (ZH, YH)


def dot_nn(a, b):
    return lax.dot_general(a, b, (((1,), (0,)), ((), ())), preferred_element_type=F32)


def dot_nt(a, b):
    return lax.dot_general(a, b, (((1,), (1,)), ((), ())), preferred_element_type=F32)


def dot_tn(a, b):
    return lax.dot_general(a, b, (((0,), (0,)), ((), ())), preferred_element_type=F32)


def swap(x, axis):
    return lax.ppermute(x, axis, [(0, 1), (1, 0)])


def gather_peers(x):
    across = swap(x, YL)
    beside = swap(x, CO)
    return x, beside, across, swap(across, CO)


def full(shape):
    return pl.BlockSpec(shape, lambda *_: (0,) * len(shape))


def ordered(x, after):
    hbm = pl.BlockSpec(memory_space=pl.ANY)
    return pl.pallas_call(
        lambda *refs: None,
        in_specs=[hbm, hbm],
        out_specs=hbm,
        out_shape=jax.ShapeDtypeStruct(x.shape, x.dtype),
        input_output_aliases={0: 0},
        name="ordered",
    )(x, after)


def weights_kernel(basis, weight_in, gain, weight_out, *refs):
    gained, own, acc = refs[-3:]
    step = pl.program_id(0)
    h = weight_in.shape[1]

    @pl.when(step == 0)
    def _():
        acc[...] = jnp.zeros_like(acc)

    part = basis[...]
    gained[...] = scaled(weight_in[...], gain[...])
    acc[0:h, :] += dot_nn(weight_out[...], part)
    acc[h:, :] += dot_tn(part, part)

    @pl.when(step == pl.num_programs(0) - 1)
    def _():
        own[...] = acc[...].astype(BF16)


def weights(basis, weight_in, gain, weight_out, afters):
    d, r = basis.shape
    h = weight_in.shape[1]
    steps = 4
    rows = d // steps
    return pl.pallas_call(
        weights_kernel,
        grid=(steps,),
        in_specs=[
            pl.BlockSpec((rows, r), lambda k: (k, 0)),
            pl.BlockSpec((rows, h), lambda k: (k, 0)),
            pl.BlockSpec((1, rows), lambda k: (0, k)),
            pl.BlockSpec((h, rows), lambda k: (0, k)),
        ]
        + [pl.BlockSpec(memory_space=pl.ANY)] * len(afters),
        out_specs=[pl.BlockSpec((rows, h), lambda k: (k, 0)), full((r + h, r))],
        out_shape=[
            jax.ShapeDtypeStruct((d, h), BF16),
            jax.ShapeDtypeStruct((r + h, r), BF16),
        ],
        scratch_shapes=[pltpu.VMEM((r + h, r), F32)],
        compiler_params=pltpu.CompilerParams(vmem_limit_bytes=GRANT),
        cost_estimate=pl.CostEstimate(
            flops=2 * d * r * (r + h), bytes_accessed=4 * d * (r + h), transcendentals=0
        ),
        name="weights",
    )(basis, weight_in, gain, weight_out, *afters)


def scaled(rows, gain):
    column = jnp.broadcast_to(gain, (8, rows.shape[0])).T[:, 0:1]
    return (rows.astype(F32) * column).astype(BF16)


def cross_kernel(at, basis, weight_in, gain, prev, after, out, mine, ins, theirs, sems):
    blocks, rows, r = theirs.shape
    wait_all(
        start_all(
            [
                pltpu.make_async_copy(prev, theirs, sems.at[0]),
                pltpu.make_async_copy(basis.at[:, at[0]], mine, sems.at[1]),
                pltpu.make_async_copy(weight_in.at[:, at[0]], ins, sems.at[2]),
            ]
        )
    )
    first, second = 0.0, 0.0
    for k in range(blocks):
        start = pl.multiple_of((k * 4 + at[0]) * rows, rows)
        first = first + dot_tn(theirs[k], mine[k])
        second = second + dot_tn(theirs[k], scaled(ins[k], gain[:, pl.ds(start, rows)]))
    out[:, 0:r] = first.astype(BF16)
    out[:, r:] = second.astype(BF16)


def cross_products(at, basis, weight_in, gain, prev, after):
    blocks, rows, r = prev.shape
    h = weight_in.shape[1]
    hbm = pl.BlockSpec(memory_space=pl.ANY)
    return pl.pallas_call(
        cross_kernel,
        in_specs=[pl.BlockSpec(memory_space=pltpu.SMEM), hbm, hbm, full(gain.shape), hbm, hbm],
        out_specs=full((r, r + h)),
        out_shape=jax.ShapeDtypeStruct((r, r + h), BF16),
        scratch_shapes=[
            pltpu.VMEM((blocks, rows, r), BF16),
            pltpu.VMEM((blocks, rows, h), BF16),
            pltpu.VMEM((blocks, rows, r), BF16),
            pltpu.SemaphoreType.DMA((3,)),
        ],
        compiler_params=pltpu.CompilerParams(vmem_limit_bytes=GRANT),
        cost_estimate=pl.CostEstimate(
            flops=2 * blocks * rows * r * (r + h),
            bytes_accessed=2 * blocks * rows * (2 * r + h),
            transcendentals=0,
        ),
        name="cross_products",
    )(at, basis.reshape(blocks, 4, rows, r), weight_in.reshape(blocks, 4, rows, h), gain, prev, after)


def sum_kernel(a, b, c, d, after, out):
    total = a[...].astype(F32) + b[...].astype(F32) + c[...].astype(F32) + d[...].astype(F32)
    out[...] = total.astype(BF16)


def sum_over_x(v, after):
    parts = [v] + [lax.ppermute(v, X, [(i, (i + k) % 4) for i in range(4)]) for k in (1, 2, 3)]
    vmem = pl.BlockSpec(memory_space=pltpu.VMEM)
    return pl.pallas_call(
        sum_kernel,
        in_specs=[vmem] * 4 + [pl.BlockSpec(memory_space=pl.ANY)],
        out_specs=vmem,
        out_shape=jax.ShapeDtypeStruct(v.shape, BF16),
        compiler_params=pltpu.CompilerParams(vmem_limit_bytes=16 * 2**20),
        cost_estimate=pl.CostEstimate(flops=4 * v.size, bytes_accessed=10 * v.size, transcendentals=0),
        name="sum_over_x",
    )(*parts, after)


def start_all(copies):
    for copy in copies:
        copy.start()
    return copies


def wait_all(copies):
    for copy in copies:
        copy.wait()


def one_hot(column, n):
    lanes = lax.broadcasted_iota(jnp.int32, (column.shape[0], n), 1)
    return (column == lanes).astype(F32)


def split_int(v):
    return (v // 128).astype(F32).astype(BF16), (v % 128).astype(F32).astype(BF16)


def request_kernel(vocab, at, ids, basis, place, requests, rows, sem):
    copy = pltpu.make_async_copy(basis.at[:, at[0]], rows, sem)
    copy.start()
    tokens, shards = ids.shape[1], requests.shape[0]
    column = jnp.broadcast_to(ids[...], (8, tokens)).T[:, 0:1]
    first = lax.broadcasted_iota(jnp.int32, (tokens, shards), 1) * vocab
    mine = (column >= first) & (column < first + vocab)
    matches = mine.astype(F32)
    local = jnp.sum(jnp.where(mine, column - first, 0), axis=1, keepdims=True)
    owner = jnp.sum(jnp.where(mine, first // vocab, 0), axis=1, keepdims=True)
    earlier = lax.broadcasted_iota(jnp.int32, (tokens, tokens), 0) > lax.broadcasted_iota(
        jnp.int32, (tokens, tokens), 1
    )
    half = matches.astype(BF16)
    before = dot_nn(earlier.astype(F32).astype(BF16), half)
    position = jnp.sum(matches * before, axis=1, keepdims=True).astype(jnp.int32)
    place[...] = owner * CAP + position
    slot = one_hot(position, 128)
    high, low = split_int(local)
    found = 128.0 * dot_tn(half, (slot * high.astype(F32)).astype(BF16))
    found = found + dot_tn(half, (slot * low.astype(F32)).astype(BF16))
    requests[...] = found[:, 0:CAP].astype(jnp.int32)
    copy.wait()


def request(at, ids, basis, vocab, shards):
    tokens = ids.shape[1]
    blocks, _, rows, r = basis.shape
    hbm = pl.BlockSpec(memory_space=pl.ANY)
    return pl.pallas_call(
        functools.partial(request_kernel, vocab),
        in_specs=[pl.BlockSpec(memory_space=pltpu.SMEM), full(ids.shape), hbm],
        out_specs=[full((tokens, 1)), full((shards, CAP)), full((blocks, rows, r))],
        out_shape=[
            jax.ShapeDtypeStruct((tokens, 1), jnp.int32),
            jax.ShapeDtypeStruct((shards, CAP), jnp.int32),
            jax.ShapeDtypeStruct((blocks, rows, r), BF16),
        ],
        scratch_shapes=[pltpu.SemaphoreType.DMA],
        compiler_params=pltpu.CompilerParams(vmem_limit_bytes=GRANT),
        cost_estimate=pl.CostEstimate(flops=10**7, bytes_accessed=2**21, transcendentals=0),
        name="request",
    )(at, ids, basis)


def pick_kernel(asked, table, *refs):
    out, hot, rows, found, in_sems, out_sems = refs[-6:]
    shards, cap = asked.shape
    slots, vocab = hot.shape
    steps, _, width = rows.shape
    ins = [
        pltpu.make_async_copy(table.at[:, pl.ds(k * width, width)], rows.at[k], in_sems.at[k])
        for k in range(steps)
    ]
    outs = [
        pltpu.make_async_copy(found.at[k], out.at[:, :, pl.ds(k * width, width)], out_sems.at[k])
        for k in range(steps)
    ]
    for copy in ins:
        copy.start()
    peer = lax.broadcasted_iota(jnp.int32, (slots, shards), 0) // cap
    peer = (peer == lax.broadcasted_iota(jnp.int32, (slots, shards), 1)).astype(F32).astype(BF16)
    high, low = split_int(asked[...])
    spread = 128.0 * dot_nn(peer, high) + dot_nn(peer, low)
    slot = lax.broadcasted_iota(jnp.int32, (slots, cap), 0) % cap
    keep = slot == lax.broadcasted_iota(jnp.int32, (slots, cap), 1)
    column = jnp.sum(jnp.where(keep, spread, 0.0), axis=1, keepdims=True)
    hot[...] = one_hot(column.astype(jnp.int32), vocab).astype(BF16)
    for k in range(steps):
        ins[k].wait()
        found[k] = dot_nn(hot[...], rows[k]).astype(BF16).reshape(shards, cap, width)
        outs[k].start()
    for copy in outs:
        copy.wait()


def pick_rows(asked, table, firsts):
    shards, cap = asked.shape
    vocab, cols = table.shape
    slots = shards * cap
    steps = 4
    width = cols // steps
    return pl.pallas_call(
        pick_kernel,
        in_specs=[full(asked.shape), pl.BlockSpec(memory_space=pl.ANY)]
        + [pl.BlockSpec(memory_space=pl.ANY)] * len(firsts),
        out_specs=pl.BlockSpec(memory_space=pl.ANY),
        out_shape=jax.ShapeDtypeStruct((shards, cap, cols), BF16),
        scratch_shapes=[
            pltpu.VMEM((slots, vocab), BF16),
            pltpu.VMEM((steps, vocab, width), BF16),
            pltpu.VMEM((steps, shards, cap, width), BF16),
            pltpu.SemaphoreType.DMA((steps,)),
            pltpu.SemaphoreType.DMA((steps,)),
        ],
        compiler_params=pltpu.CompilerParams(vmem_limit_bytes=GRANT),
        cost_estimate=pl.CostEstimate(
            flops=2 * slots * vocab * cols, bytes_accessed=2 * cols * (vocab + slots), transcendentals=0
        ),
        name="pick_rows",
    )(asked, table, *firsts)


def place_kernel(place, answered, *refs):
    part, turned = refs[-2:]
    tokens, slots = part.shape[0], answered.shape[0]
    width = turned.shape[2]
    put = one_hot(place[...], slots).astype(BF16)
    for t in range(turned.shape[0]):
        rows = dot_nn(put, answered[:, t * width : (t + 1) * width]).astype(BF16)
        part[:, t * width : (t + 1) * width] = rows
        turned[t] = rows


def place_rows(place, answered, copies, firsts):
    tokens = place.shape[0]
    slots, cols = answered.shape
    vmem = pl.BlockSpec(memory_space=pltpu.VMEM)
    return pl.pallas_call(
        place_kernel,
        in_specs=[vmem, vmem] + [pl.BlockSpec(memory_space=pl.ANY)] * len(firsts),
        out_specs=[vmem, vmem],
        out_shape=[
            jax.ShapeDtypeStruct((tokens, cols), BF16),
            jax.ShapeDtypeStruct((copies, tokens, cols // copies), BF16),
        ],
        compiler_params=pltpu.CompilerParams(vmem_limit_bytes=16 * 2**20),
        cost_estimate=pl.CostEstimate(
            flops=2 * slots * tokens * cols, bytes_accessed=2 * cols * (slots + 2 * tokens), transcendentals=0
        ),
        name="place_rows",
    )(place, answered, *firsts)


def project_kernel(me, p0, p1, p2, p3, basis, gained, first, second, out, square):
    step = pl.program_id(0)
    r = basis.shape[1]
    for k, piece in enumerate((p0, p1, p2, p3)):

        @pl.when(step == k)
        def _(k=k, piece=piece):
            x = piece[...]
            xf = x.astype(F32)
            q = jnp.broadcast_to(jnp.sum(xf * xf, axis=1, keepdims=True), square.shape)
            a, b = dot_nn(x, basis[...]), dot_nn(x, gained[...])
            if k == 0:
                out[:, 0:r] = a
                out[:, r:] = b
                square[...] = q
            else:
                out[:, 0:r] += a
                out[:, r:] += b
                square[...] += q


def project(me, pieces, basis, gained, first, second):
    tokens, cols = pieces[0].shape
    r, h = basis.shape[1], gained.shape[1]
    return pl.pallas_call(
        project_kernel,
        grid_spec=pltpu.PrefetchScalarGridSpec(
            num_scalar_prefetch=1,
            grid=(4,),
            in_specs=[full((tokens, cols))] * 4
            + [
                pl.BlockSpec((cols, r), lambda k, me: (k ^ me[0], 0)),
                pl.BlockSpec((cols, h), lambda k, me: (k ^ me[0], 0)),
                pl.BlockSpec(memory_space=pl.ANY),
                pl.BlockSpec(memory_space=pl.ANY),
            ],
            out_specs=[full((tokens, r + h)), full((tokens, 128))],
        ),
        out_shape=[
            jax.ShapeDtypeStruct((tokens, r + h), F32),
            jax.ShapeDtypeStruct((tokens, 128), F32),
        ],
        compiler_params=pltpu.CompilerParams(vmem_limit_bytes=24 * 2**20),
        cost_estimate=pl.CostEstimate(
            flops=8 * tokens * cols * (r + h), bytes_accessed=8 * cols * (r + h + tokens), transcendentals=0
        ),
        name="project",
    )(me, *pieces, basis, gained, first, second)


def chain_kernel(width, me_ref, cot, square, q0, q1, q2, q3, g0, g1, g2, g3, m0, m1, m2, m3, sent, packed,
                 pq, owns, mats, pres, acts, coefs, spans, invs, ins, ws):
    me = me_ref[0]
    r = cot.shape[1]
    h = q0.shape[1] - r
    for k, (q, g, m) in enumerate(((q0, g0, m0), (q1, g1, m1), (q2, g2, m2), (q3, g3, m3))):
        pq[k ^ me] = q[...]
        owns[k ^ me] = g[...]
        mats[k ^ me] = m[...]
    squares = square[:, 0:1]
    coefs[0] = jnp.zeros_like(coefs[0])
    for s in range(4):
        base_in = pq[s, :, r:]
        if s == 0:
            inv = lax.rsqrt(squares * (1.0 / width) + EPSILON)
            pre = inv * base_in
        else:
            c = coefs[s]
            base_sub = pq[s - 1, :, 0:r]
            span = base_sub + dot_nn(c, owns[s - 1, h:, :])
            total = squares + jnp.sum(c.astype(F32) * (base_sub + span), axis=1, keepdims=True)
            inv = lax.rsqrt(jnp.maximum(total, 0.0) * (1.0 / width) + EPSILON)
            pre = inv * (base_in + dot_nn(c, mats[s, :, r:]))
            spans[s] = span
        invs[s] = jnp.broadcast_to(inv, invs.shape[1:])
        pres[s] = pre
        act = (pre / (1.0 + jnp.exp(-pre))).astype(BF16)
        acts[s] = act
        new = dot_nn(act, owns[s, 0:h, :])
        if s > 0:
            new = new + dot_nn(c, mats[s, :, 0:r])
        coefs[s + 1] = new.astype(BF16)
    arrived = cot[...]
    for s in (3, 2, 1, 0):
        ins[s] = arrived
        pre = pres[s]
        sg = 1.0 / (1.0 + jnp.exp(-pre))
        gp = dot_nt(arrived, owns[s, 0:h, :]) * sg * (1.0 + pre * (1.0 - sg))
        inv = invs[s, :, 0:1]
        ws[s] = (gp * inv).astype(BF16)
        if s > 0:
            mean = jnp.sum(gp * pre, axis=1, keepdims=True) * (1.0 / width)
            back = dot_nt(gp.astype(BF16), mats[s, :, r:]) - (inv * mean) * spans[s]
            arrived = (dot_nt(arrived, mats[s, :, 0:r]) + inv * back).astype(BF16)
    sent[...] = coefs[me + 1]
    w = ws[me]
    row = (w, dot_tn(acts[me], ins[me]).astype(BF16), dot_tn(w, coefs[me]).astype(BF16))
    for t in range(packed.shape[0]):
        at = 0
        for v in row:
            packed[t, :, at : at + v.shape[1]] = v
            at += v.shape[1]


def chain(me, cot, square, pq, owns, mats, width, copies):
    tokens, r = cot.shape
    h = pq[0].shape[1] - r
    vmem = pl.BlockSpec(memory_space=pltpu.VMEM)
    return pl.pallas_call(
        functools.partial(chain_kernel, width),
        in_specs=[pl.BlockSpec(memory_space=pltpu.SMEM)] + [vmem] * 14,
        out_specs=[vmem, vmem],
        out_shape=[
            jax.ShapeDtypeStruct((tokens, r), BF16),
            jax.ShapeDtypeStruct((copies, tokens, h + 2 * r), BF16),
        ],
        scratch_shapes=[
            pltpu.VMEM((4, tokens, r + h), F32),
            pltpu.VMEM((4,) + owns[0].shape, BF16),
            pltpu.VMEM((4,) + mats[0].shape, BF16),
            pltpu.VMEM((4, tokens, h), F32),
            pltpu.VMEM((4, tokens, h), BF16),
            pltpu.VMEM((5, tokens, r), BF16),
            pltpu.VMEM((4, tokens, r), F32),
            pltpu.VMEM((4, tokens, 128), F32),
            pltpu.VMEM((4, tokens, r), BF16),
            pltpu.VMEM((4, tokens, h), BF16),
        ],
        compiler_params=pltpu.CompilerParams(vmem_limit_bytes=32 * 2**20),
        cost_estimate=pl.CostEstimate(flops=4 * 10**9, bytes_accessed=6 * 2**20, transcendentals=10**6),
        name="chain",
    )(me, cot, square, *pq, *owns, *mats)


def share_kernel(me_ref, packed, t0, t1, t2, t3, rows_own, rows_prev, out):
    me = me_ref[0]
    group, tokens, wide = packed.shape
    r = rows_own.shape[2]
    h = wide - 2 * r
    both = packed[0, :, h:].astype(F32)
    for g in range(1, group):
        both = both + packed[g, :, h:].astype(F32)
    v, uh = both[:, 0:r], both[:, r:].astype(BF16)
    vh = v.astype(BF16)
    vl = (v - vh.astype(F32)).astype(BF16)
    wt = jnp.concatenate([packed[g, :, 0:h].astype(F32).T.astype(BF16) for g in range(group)], axis=1)
    for k, piece in enumerate((t0, t1, t2, t3)):
        c = k ^ me
        xs = (dot_nn(wt, piece[...]) + dot_nt(uh, rows_prev[c])).astype(BF16)
        own = rows_own[c]
        os = (dot_nt(vh, own) + dot_nt(vl, own)).astype(BF16)
        n = xs.shape[1] // 2
        for e in range(2):
            out[2 * c + e, 0:h, :] = xs[:, e * n : (e + 1) * n]
            out[2 * c + e, h:, :] = os[:, e * n : (e + 1) * n]


def share(me, packed, pieces, rows_own, rows_prev):
    h = packed.shape[2] - 2 * rows_own.shape[2]
    cs, n, _ = rows_own.shape
    vmem = pl.BlockSpec(memory_space=pltpu.VMEM)
    return pl.pallas_call(
        share_kernel,
        in_specs=[pl.BlockSpec(memory_space=pltpu.SMEM)] + [vmem] * 7,
        out_specs=vmem,
        out_shape=jax.ShapeDtypeStruct((2 * cs, 2 * h, n // 2), BF16),
        compiler_params=pltpu.CompilerParams(vmem_limit_bytes=32 * 2**20),
        cost_estimate=pl.CostEstimate(flops=2 * 10**9, bytes_accessed=6 * 2**20, transcendentals=0),
        name="share",
    )(me, packed, *pieces, rows_own, rows_prev)


def finish_kernel(arrived, weight_in, gain, grad_in, grad_out, grad_gain, shares, sem):
    h = shares.shape[1] // 2
    copy = pltpu.make_async_copy(arrived, shares, sem)
    copy.start()
    copy.wait()
    total = jnp.sum(shares[...].astype(F32), axis=0)
    plain = total[0:h]
    grad_out[...] = total[h:]
    grad_in[...] = (plain * gain[...]).T
    grad_gain[...] = jnp.sum(plain * weight_in[...].astype(F32).T, axis=0, keepdims=True)


def finish(shares, weight_in, gain):
    _, twice, n = shares.shape
    h = twice // 2
    return pl.pallas_call(
        finish_kernel,
        in_specs=[pl.BlockSpec(memory_space=pl.ANY), full((n, h)), full((1, n))],
        out_specs=[full((n, h)), full((h, n)), full((1, n))],
        out_shape=[
            jax.ShapeDtypeStruct((n, h), F32),
            jax.ShapeDtypeStruct((h, n), F32),
            jax.ShapeDtypeStruct((1, n), F32),
        ],
        scratch_shapes=[pltpu.VMEM(shares.shape, BF16), pltpu.SemaphoreType.DMA],
        compiler_params=pltpu.CompilerParams(vmem_limit_bytes=16 * 2**20),
        cost_estimate=pl.CostEstimate(flops=10**6, bytes_accessed=2**20, transcendentals=0),
        name="finish",
    )(shares, weight_in, gain)


def per_device(
    token_ids, embed_table, subspace, adapter_in, adapter_out, norm_gain, coef_cotangent
):
    tokens = token_ids.shape[0]
    zl, x = lax.axis_index(ZL), lax.axis_index(X)
    shards = lax.axis_size(DP)
    group = lax.axis_size(GATHER)
    section = lax.axis_index(SEC)
    me = jnp.reshape(section, (1,)).astype(jnp.int32)
    dp = lax.axis_index(DP)
    vocab, cols = embed_table.shape
    basis, weight_in, weight_out = subspace[0], adapter_in[0], adapter_out[0]
    d, r = basis.shape
    h = weight_in.shape[1]
    block = d // shards

    x_at = jnp.reshape(x, (1,)).astype(jnp.int32)
    place, requests, rows_x = request(
        x_at, token_ids.reshape(1, tokens), basis.reshape(8, 4, 2 * block, r), vocab, shards
    )
    prev_x = lax.ppermute(rows_x, SEC, [(0, 1), (1, 2), (2, 3)])
    asked = lax.all_to_all(requests, DP, split_axis=0, concat_axis=0, tiled=True)
    found = pick_rows(asked, embed_table, (prev_x,))
    answered = lax.all_to_all(found, DP, split_axis=0, concat_axis=0, tiled=True)

    crossed = cross_products(x_at, basis, weight_in, norm_gain, prev_x, found)
    gained, own = weights(basis, weight_in, norm_gain, weight_out, (crossed,))
    owns = gather_peers(own)
    crossed = sum_over_x(crossed, own)
    mats = gather_peers(crossed)

    part, turned = place_rows(place, answered.reshape(shards * CAP, cols), group, (crossed,))
    turned = ordered(turned, mats[2])
    pieces = gather_peers(part)
    turned = lax.all_to_all(turned, GATHER, split_axis=0, concat_axis=0, tiled=True)
    pq, square = project(me, pieces, basis, gained, turned, mats[2])
    pqs = gather_peers(pq)
    turned = gather_peers(turned.reshape(group * tokens, cols // group))

    sent, packed = chain(me, coef_cotangent, square, pqs, owns, mats, d, group)
    packed = lax.all_to_all(packed, GATHER, split_axis=0, concat_axis=0, tiled=True)
    rows_own = lax.dynamic_index_in_dim(rows_x.reshape(4, 2, 2 * block, r), zl, 1, False)
    rows_prev = lax.dynamic_index_in_dim(prev_x.reshape(4, 2, 2 * block, r), zl, 1, False)
    shares = share(me, packed, turned, rows_own, rows_prev)
    shares = lax.all_to_all(shares, REDUCE, split_axis=0, concat_axis=0, tiled=True)
    in_block = lax.dynamic_slice_in_dim(weight_in, dp * block, block, 0)
    gain_block = lax.dynamic_slice_in_dim(norm_gain, dp * block, block, 1)
    grad_in, grad_out, grad_gain = finish(shares, in_block, gain_block)
    return sent[None], grad_in[None], grad_out[None], grad_gain


def solution(mesh):
    fine = Mesh(mesh.devices.reshape(2, 2, 4, 2, 4, 2), (YL, CO, ZH, ZL, X, YH))
    return jax.shard_map(
        per_device,
        mesh=fine,
        in_specs=(
            P(DP),
            P(DP, SEC),
            P(SEC, None, None),
            P(SEC, None, None),
            P(SEC, None, None),
            P(SEC, None),
            P(DP, None),
        ),
        out_specs=(
            P(SEC, DP, None),
            P(SEC, DP, None),
            P(SEC, None, DP),
            P(SEC, DP),
        ),
        check_vma=False,
    )
```

```python
import functools

import jax
import jax.numpy as jnp
from jax import lax
from jax.experimental import pallas as pl
from jax.experimental.pallas import tpu as pltpu
from jax.sharding import Mesh, PartitionSpec as P

CAP = 4
EPSILON = 1e-05
GRANT = 63 * 2**20
F32, BF16 = jnp.float32, jnp.bfloat16
YL, CO, ZH, ZL, X, YH = "yl", "co", "zh", "zl", "x", "yh"
DP = (ZH, ZL, X, YH)
SEC = (YL, CO)
GATHER = (ZL, X)
REDUCE = (ZH, YH)


def dot_nn(a, b):
    return lax.dot_general(a, b, (((1,), (0,)), ((), ())), preferred_element_type=F32)


def dot_nt(a, b):
    return lax.dot_general(a, b, (((1,), (1,)), ((), ())), preferred_element_type=F32)


def dot_tn(a, b):
    return lax.dot_general(a, b, (((0,), (0,)), ((), ())), preferred_element_type=F32)


def swap(x, axis):
    return lax.ppermute(x, axis, [(0, 1), (1, 0)])


def gather_peers(x):
    across = swap(x, YL)
    beside = swap(x, CO)
    return x, beside, across, swap(across, CO)


def full(shape):
    return pl.BlockSpec(shape, lambda *_: (0,) * len(shape))


def ordered(x, after):
    hbm = pl.BlockSpec(memory_space=pl.ANY)
    return pl.pallas_call(
        lambda *refs: None,
        in_specs=[hbm, hbm],
        out_specs=hbm,
        out_shape=jax.ShapeDtypeStruct(x.shape, x.dtype),
        input_output_aliases={0: 0},
        name="ordered",
    )(x, after)


def weights_kernel(basis, weight_in, gain, weight_out, *refs):
    gained, own, acc = refs[-3:]
    step = pl.program_id(0)
    h = weight_in.shape[1]

    @pl.when(step == 0)
    def _():
        acc[...] = jnp.zeros_like(acc)

    part = basis[...]
    gained[...] = scaled(weight_in[...], gain[...])
    acc[0:h, :] += dot_nn(weight_out[...], part)
    acc[h:, :] += dot_tn(part, part)

    @pl.when(step == pl.num_programs(0) - 1)
    def _():
        own[...] = acc[...].astype(BF16)


def weights(basis, weight_in, gain, weight_out, afters):
    d, r = basis.shape
    h = weight_in.shape[1]
    steps = 4
    rows = d // steps
    return pl.pallas_call(
        weights_kernel,
        grid=(steps,),
        in_specs=[
            pl.BlockSpec((rows, r), lambda k: (k, 0)),
            pl.BlockSpec((rows, h), lambda k: (k, 0)),
            pl.BlockSpec((1, rows), lambda k: (0, k)),
            pl.BlockSpec((h, rows), lambda k: (0, k)),
        ]
        + [pl.BlockSpec(memory_space=pl.ANY)] * len(afters),
        out_specs=[pl.BlockSpec((rows, h), lambda k: (k, 0)), full((r + h, r))],
        out_shape=[
            jax.ShapeDtypeStruct((d, h), BF16),
            jax.ShapeDtypeStruct((r + h, r), BF16),
        ],
        scratch_shapes=[pltpu.VMEM((r + h, r), F32)],
        compiler_params=pltpu.CompilerParams(vmem_limit_bytes=GRANT),
        cost_estimate=pl.CostEstimate(
            flops=2 * d * r * (r + h), bytes_accessed=4 * d * (r + h), transcendentals=0
        ),
        name="weights",
    )(basis, weight_in, gain, weight_out, *afters)


def scaled(rows, gain):
    column = jnp.broadcast_to(gain, (8, rows.shape[0])).T[:, 0:1]
    return (rows.astype(F32) * column).astype(BF16)


def cross_kernel(at, basis, weight_in, gain, prev, after, out, mine, ins, theirs, sems):
    blocks, rows, r = theirs.shape
    wait_all(
        start_all(
            [
                pltpu.make_async_copy(prev, theirs, sems.at[0]),
                pltpu.make_async_copy(basis.at[:, at[0]], mine, sems.at[1]),
                pltpu.make_async_copy(weight_in.at[:, at[0]], ins, sems.at[2]),
            ]
        )
    )
    first, second = 0.0, 0.0
    for k in range(blocks):
        start = pl.multiple_of((k * 4 + at[0]) * rows, rows)
        first = first + dot_tn(theirs[k], mine[k])
        second = second + dot_tn(theirs[k], scaled(ins[k], gain[:, pl.ds(start, rows)]))
    out[:, 0:r] = first.astype(BF16)
    out[:, r:] = second.astype(BF16)


def cross_products(at, basis, weight_in, gain, prev, after):
    blocks, rows, r = prev.shape
    h = weight_in.shape[1]
    hbm = pl.BlockSpec(memory_space=pl.ANY)
    return pl.pallas_call(
        cross_kernel,
        in_specs=[pl.BlockSpec(memory_space=pltpu.SMEM), hbm, hbm, full(gain.shape), hbm, hbm],
        out_specs=full((r, r + h)),
        out_shape=jax.ShapeDtypeStruct((r, r + h), BF16),
        scratch_shapes=[
            pltpu.VMEM((blocks, rows, r), BF16),
            pltpu.VMEM((blocks, rows, h), BF16),
            pltpu.VMEM((blocks, rows, r), BF16),
            pltpu.SemaphoreType.DMA((3,)),
        ],
        compiler_params=pltpu.CompilerParams(vmem_limit_bytes=GRANT),
        cost_estimate=pl.CostEstimate(
            flops=2 * blocks * rows * r * (r + h),
            bytes_accessed=2 * blocks * rows * (2 * r + h),
            transcendentals=0,
        ),
        name="cross_products",
    )(at, basis.reshape(blocks, 4, rows, r), weight_in.reshape(blocks, 4, rows, h), gain, prev, after)


def sum_kernel(a, b, c, d, after, out):
    total = a[...].astype(F32) + b[...].astype(F32) + c[...].astype(F32) + d[...].astype(F32)
    out[...] = total.astype(BF16)


def sum_over_x(v, after):
    parts = [v] + [lax.ppermute(v, X, [(i, (i + k) % 4) for i in range(4)]) for k in (1, 2, 3)]
    return pl.pallas_call(
        sum_kernel,
        in_specs=[full(v.shape)] * 4 + [pl.BlockSpec(memory_space=pl.ANY)],
        out_specs=full(v.shape),
        out_shape=jax.ShapeDtypeStruct(v.shape, BF16),
        compiler_params=pltpu.CompilerParams(vmem_limit_bytes=GRANT),
        cost_estimate=pl.CostEstimate(flops=4 * v.size, bytes_accessed=10 * v.size, transcendentals=0),
        name="sum_over_x",
    )(*parts, after)


def start_all(copies):
    for copy in copies:
        copy.start()
    return copies


def wait_all(copies):
    for copy in copies:
        copy.wait()


def one_hot(column, n):
    lanes = lax.broadcasted_iota(jnp.int32, (column.shape[0], n), 1)
    return (column == lanes).astype(F32)


def split_int(v):
    return (v // 128).astype(F32).astype(BF16), (v % 128).astype(F32).astype(BF16)


def request_kernel(vocab, at, ids, basis, place, requests, rows, sem):
    copy = pltpu.make_async_copy(basis.at[:, at[0]], rows, sem)
    copy.start()
    tokens, shards = ids.shape[1], requests.shape[0]
    column = jnp.broadcast_to(ids[...], (8, tokens)).T[:, 0:1]
    first = lax.broadcasted_iota(jnp.int32, (tokens, shards), 1) * vocab
    mine = (column >= first) & (column < first + vocab)
    matches = mine.astype(F32)
    local = jnp.sum(jnp.where(mine, column - first, 0), axis=1, keepdims=True)
    owner = jnp.sum(jnp.where(mine, first // vocab, 0), axis=1, keepdims=True)
    earlier = lax.broadcasted_iota(jnp.int32, (tokens, tokens), 0) > lax.broadcasted_iota(
        jnp.int32, (tokens, tokens), 1
    )
    half = matches.astype(BF16)
    before = dot_nn(earlier.astype(F32).astype(BF16), half)
    position = jnp.sum(matches * before, axis=1, keepdims=True).astype(jnp.int32)
    place[...] = owner * CAP + position
    slot = one_hot(position, 128)
    high, low = split_int(local)
    found = 128.0 * dot_tn(half, (slot * high.astype(F32)).astype(BF16))
    found = found + dot_tn(half, (slot * low.astype(F32)).astype(BF16))
    requests[...] = found[:, 0:CAP].astype(jnp.int32)
    copy.wait()


def request(at, ids, basis, vocab, shards):
    tokens = ids.shape[1]
    blocks, _, rows, r = basis.shape
    hbm = pl.BlockSpec(memory_space=pl.ANY)
    return pl.pallas_call(
        functools.partial(request_kernel, vocab),
        in_specs=[pl.BlockSpec(memory_space=pltpu.SMEM), full(ids.shape), hbm],
        out_specs=[full((tokens, 1)), full((shards, CAP)), full((blocks, rows, r))],
        out_shape=[
            jax.ShapeDtypeStruct((tokens, 1), jnp.int32),
            jax.ShapeDtypeStruct((shards, CAP), jnp.int32),
            jax.ShapeDtypeStruct((blocks, rows, r), BF16),
        ],
        scratch_shapes=[pltpu.SemaphoreType.DMA],
        compiler_params=pltpu.CompilerParams(vmem_limit_bytes=GRANT),
        cost_estimate=pl.CostEstimate(flops=10**7, bytes_accessed=2**21, transcendentals=0),
        name="request",
    )(at, ids, basis)


def pick_kernel(asked, table, *refs):
    out, hot, rows, found, in_sems, out_sems = refs[-6:]
    shards, cap = asked.shape
    slots, vocab = hot.shape
    steps, _, width = rows.shape
    ins = [
        pltpu.make_async_copy(table.at[:, pl.ds(k * width, width)], rows.at[k], in_sems.at[k])
        for k in range(steps)
    ]
    outs = [
        pltpu.make_async_copy(found.at[k], out.at[:, :, pl.ds(k * width, width)], out_sems.at[k])
        for k in range(steps)
    ]
    for copy in ins:
        copy.start()
    peer = lax.broadcasted_iota(jnp.int32, (slots, shards), 0) // cap
    peer = (peer == lax.broadcasted_iota(jnp.int32, (slots, shards), 1)).astype(F32).astype(BF16)
    high, low = split_int(asked[...])
    spread = 128.0 * dot_nn(peer, high) + dot_nn(peer, low)
    slot = lax.broadcasted_iota(jnp.int32, (slots, cap), 0) % cap
    keep = slot == lax.broadcasted_iota(jnp.int32, (slots, cap), 1)
    column = jnp.sum(jnp.where(keep, spread, 0.0), axis=1, keepdims=True)
    hot[...] = one_hot(column.astype(jnp.int32), vocab).astype(BF16)
    for k in range(steps):
        ins[k].wait()
        found[k] = dot_nn(hot[...], rows[k]).astype(BF16).reshape(shards, cap, width)
        outs[k].start()
    for copy in outs:
        copy.wait()


def pick_rows(asked, table, firsts):
    shards, cap = asked.shape
    vocab, cols = table.shape
    slots = shards * cap
    steps = 4
    width = cols // steps
    return pl.pallas_call(
        pick_kernel,
        in_specs=[full(asked.shape), pl.BlockSpec(memory_space=pl.ANY)]
        + [pl.BlockSpec(memory_space=pl.ANY)] * len(firsts),
        out_specs=pl.BlockSpec(memory_space=pl.ANY),
        out_shape=jax.ShapeDtypeStruct((shards, cap, cols), BF16),
        scratch_shapes=[
            pltpu.VMEM((slots, vocab), BF16),
            pltpu.VMEM((steps, vocab, width), BF16),
            pltpu.VMEM((steps, shards, cap, width), BF16),
            pltpu.SemaphoreType.DMA((steps,)),
            pltpu.SemaphoreType.DMA((steps,)),
        ],
        compiler_params=pltpu.CompilerParams(vmem_limit_bytes=GRANT),
        cost_estimate=pl.CostEstimate(
            flops=2 * slots * vocab * cols, bytes_accessed=2 * cols * (vocab + slots), transcendentals=0
        ),
        name="pick_rows",
    )(asked, table, *firsts)


def place_kernel(place, answered, *refs):
    part, turned = refs[-2:]
    shards, cap, cols = answered.shape
    width = turned.shape[2]
    put = one_hot(place[...], shards * cap).astype(BF16)
    for t in range(turned.shape[0]):
        rows = answered[:, :, t * width : (t + 1) * width].reshape(shards * cap, width)
        rows = dot_nn(put, rows).astype(BF16)
        part[:, t * width : (t + 1) * width] = rows
        turned[t] = rows


def place_rows(place, answered, copies, firsts):
    tokens = place.shape[0]
    shards, cap, cols = answered.shape
    return pl.pallas_call(
        place_kernel,
        in_specs=[full(place.shape), full(answered.shape)] + [pl.BlockSpec(memory_space=pl.ANY)] * len(firsts),
        out_specs=[full((tokens, cols)), full((copies, tokens, cols // copies))],
        out_shape=[
            jax.ShapeDtypeStruct((tokens, cols), BF16),
            jax.ShapeDtypeStruct((copies, tokens, cols // copies), BF16),
        ],
        compiler_params=pltpu.CompilerParams(vmem_limit_bytes=GRANT),
        cost_estimate=pl.CostEstimate(
            flops=2 * shards * cap * tokens * cols,
            bytes_accessed=2 * cols * (shards * cap + 2 * tokens),
            transcendentals=0,
        ),
        name="place_rows",
    )(place, answered, *firsts)


def project_kernel(me, p0, p1, p2, p3, basis, gained, first, second, out, square):
    step = pl.program_id(0)
    r = basis.shape[1]
    for k, piece in enumerate((p0, p1, p2, p3)):

        @pl.when(step == k)
        def _(k=k, piece=piece):
            x = piece[...]
            xf = x.astype(F32)
            q = jnp.broadcast_to(jnp.sum(xf * xf, axis=1, keepdims=True), square.shape)
            a, b = dot_nn(x, basis[...]), dot_nn(x, gained[...])
            if k == 0:
                out[:, 0:r] = a
                out[:, r:] = b
                square[...] = q
            else:
                out[:, 0:r] += a
                out[:, r:] += b
                square[...] += q


def project(me, pieces, basis, gained, first, second):
    tokens, cols = pieces[0].shape
    r, h = basis.shape[1], gained.shape[1]
    return pl.pallas_call(
        project_kernel,
        grid_spec=pltpu.PrefetchScalarGridSpec(
            num_scalar_prefetch=1,
            grid=(4,),
            in_specs=[full((tokens, cols))] * 4
            + [
                pl.BlockSpec((cols, r), lambda k, me: (k ^ me[0], 0)),
                pl.BlockSpec((cols, h), lambda k, me: (k ^ me[0], 0)),
                pl.BlockSpec(memory_space=pl.ANY),
                pl.BlockSpec(memory_space=pl.ANY),
            ],
            out_specs=[full((tokens, r + h)), full((tokens, 128))],
        ),
        out_shape=[
            jax.ShapeDtypeStruct((tokens, r + h), F32),
            jax.ShapeDtypeStruct((tokens, 128), F32),
        ],
        compiler_params=pltpu.CompilerParams(vmem_limit_bytes=24 * 2**20),
        cost_estimate=pl.CostEstimate(
            flops=8 * tokens * cols * (r + h), bytes_accessed=8 * cols * (r + h + tokens), transcendentals=0
        ),
        name="project",
    )(me, *pieces, basis, gained, first, second)


def chain_kernel(width, me_ref, cot, square, q0, q1, q2, q3, g0, g1, g2, g3, m0, m1, m2, m3, sent, packed,
                 pq, owns, mats, pres, acts, coefs, spans, invs, ins, ws):
    me = me_ref[0]
    r = cot.shape[1]
    h = q0.shape[1] - r
    for k, (q, g, m) in enumerate(((q0, g0, m0), (q1, g1, m1), (q2, g2, m2), (q3, g3, m3))):
        pq[k ^ me] = q[...]
        owns[k ^ me] = g[...]
        mats[k ^ me] = m[...]
    squares = square[:, 0:1]
    coefs[0] = jnp.zeros_like(coefs[0])
    for s in range(4):
        base_in = pq[s, :, r:]
        if s == 0:
            inv = lax.rsqrt(squares * (1.0 / width) + EPSILON)
            pre = inv * base_in
        else:
            c = coefs[s]
            base_sub = pq[s - 1, :, 0:r]
            span = base_sub + dot_nn(c, owns[s - 1, h:, :])
            total = squares + jnp.sum(c.astype(F32) * (base_sub + span), axis=1, keepdims=True)
            inv = lax.rsqrt(jnp.maximum(total, 0.0) * (1.0 / width) + EPSILON)
            pre = inv * (base_in + dot_nn(c, mats[s, :, r:]))
            spans[s] = span
        invs[s] = jnp.broadcast_to(inv, invs.shape[1:])
        pres[s] = pre
        act = (pre / (1.0 + jnp.exp(-pre))).astype(BF16)
        acts[s] = act
        new = dot_nn(act, owns[s, 0:h, :])
        if s > 0:
            new = new + dot_nn(c, mats[s, :, 0:r])
        coefs[s + 1] = new.astype(BF16)
    arrived = cot[...]
    for s in (3, 2, 1, 0):
        ins[s] = arrived
        pre = pres[s]
        sg = 1.0 / (1.0 + jnp.exp(-pre))
        gp = dot_nt(arrived, owns[s, 0:h, :]) * sg * (1.0 + pre * (1.0 - sg))
        inv = invs[s, :, 0:1]
        ws[s] = (gp * inv).astype(BF16)
        if s > 0:
            mean = jnp.sum(gp * pre, axis=1, keepdims=True) * (1.0 / width)
            back = dot_nt(gp.astype(BF16), mats[s, :, r:]) - (inv * mean) * spans[s]
            arrived = (dot_nt(arrived, mats[s, :, 0:r]) + inv * back).astype(BF16)
    sent[...] = coefs[me + 1]
    w = ws[me]
    row = (w, dot_tn(acts[me], ins[me]).astype(BF16), dot_tn(w, coefs[me]).astype(BF16))
    for t in range(packed.shape[0]):
        at = 0
        for v in row:
            packed[t, :, at : at + v.shape[1]] = v
            at += v.shape[1]


def chain(me, cot, square, pq, owns, mats, width, copies):
    tokens, r = cot.shape
    h = pq[0].shape[1] - r
    vmem = pl.BlockSpec(memory_space=pltpu.VMEM)
    return pl.pallas_call(
        functools.partial(chain_kernel, width),
        in_specs=[pl.BlockSpec(memory_space=pltpu.SMEM)] + [vmem] * 14,
        out_specs=[vmem, vmem],
        out_shape=[
            jax.ShapeDtypeStruct((tokens, r), BF16),
            jax.ShapeDtypeStruct((copies, tokens, h + 2 * r), BF16),
        ],
        scratch_shapes=[
            pltpu.VMEM((4, tokens, r + h), F32),
            pltpu.VMEM((4,) + owns[0].shape, BF16),
            pltpu.VMEM((4,) + mats[0].shape, BF16),
            pltpu.VMEM((4, tokens, h), F32),
            pltpu.VMEM((4, tokens, h), BF16),
            pltpu.VMEM((5, tokens, r), BF16),
            pltpu.VMEM((4, tokens, r), F32),
            pltpu.VMEM((4, tokens, 128), F32),
            pltpu.VMEM((4, tokens, r), BF16),
            pltpu.VMEM((4, tokens, h), BF16),
        ],
        compiler_params=pltpu.CompilerParams(vmem_limit_bytes=32 * 2**20),
        cost_estimate=pl.CostEstimate(flops=4 * 10**9, bytes_accessed=6 * 2**20, transcendentals=10**6),
        name="chain",
    )(me, cot, square, *pq, *owns, *mats)


def share_kernel(me_ref, packed, t0, t1, t2, t3, rows_own, rows_prev, out):
    me = me_ref[0]
    group, tokens, wide = packed.shape
    r = rows_own.shape[2]
    h = wide - 2 * r
    both = packed[0, :, h:].astype(F32)
    for g in range(1, group):
        both = both + packed[g, :, h:].astype(F32)
    v, uh = both[:, 0:r], both[:, r:].astype(BF16)
    vh = v.astype(BF16)
    vl = (v - vh.astype(F32)).astype(BF16)
    wt = jnp.concatenate([packed[g, :, 0:h].astype(F32).T.astype(BF16) for g in range(group)], axis=1)
    for k, piece in enumerate((t0, t1, t2, t3)):
        c = k ^ me
        xs = (dot_nn(wt, piece[...]) + dot_nt(uh, rows_prev[c])).astype(BF16)
        own = rows_own[c]
        os = (dot_nt(vh, own) + dot_nt(vl, own)).astype(BF16)
        n = xs.shape[1] // 2
        for e in range(2):
            out[2 * c + e, 0:h, :] = xs[:, e * n : (e + 1) * n]
            out[2 * c + e, h:, :] = os[:, e * n : (e + 1) * n]


def share(me, packed, pieces, rows_own, rows_prev):
    h = packed.shape[2] - 2 * rows_own.shape[2]
    cs, n, _ = rows_own.shape
    vmem = pl.BlockSpec(memory_space=pltpu.VMEM)
    return pl.pallas_call(
        share_kernel,
        in_specs=[pl.BlockSpec(memory_space=pltpu.SMEM)] + [vmem] * 7,
        out_specs=vmem,
        out_shape=jax.ShapeDtypeStruct((2 * cs, 2 * h, n // 2), BF16),
        compiler_params=pltpu.CompilerParams(vmem_limit_bytes=32 * 2**20),
        cost_estimate=pl.CostEstimate(flops=2 * 10**9, bytes_accessed=6 * 2**20, transcendentals=0),
        name="share",
    )(me, packed, *pieces, rows_own, rows_prev)


def finish_kernel(arrived, weight_in, gain, grad_in, grad_out, grad_gain, shares, sem):
    h = shares.shape[1] // 2
    copy = pltpu.make_async_copy(arrived, shares, sem)
    copy.start()
    copy.wait()
    total = jnp.sum(shares[...].astype(F32), axis=0)
    plain = total[0:h]
    grad_out[...] = total[h:]
    grad_in[...] = (plain * gain[...]).T
    grad_gain[...] = jnp.sum(plain * weight_in[...].astype(F32).T, axis=0, keepdims=True)


def finish(shares, weight_in, gain):
    _, twice, n = shares.shape
    h = twice // 2
    return pl.pallas_call(
        finish_kernel,
        in_specs=[pl.BlockSpec(memory_space=pl.ANY), full((n, h)), full((1, n))],
        out_specs=[full((n, h)), full((h, n)), full((1, n))],
        out_shape=[
            jax.ShapeDtypeStruct((n, h), F32),
            jax.ShapeDtypeStruct((h, n), F32),
            jax.ShapeDtypeStruct((1, n), F32),
        ],
        scratch_shapes=[pltpu.VMEM(shares.shape, BF16), pltpu.SemaphoreType.DMA],
        compiler_params=pltpu.CompilerParams(vmem_limit_bytes=16 * 2**20),
        cost_estimate=pl.CostEstimate(flops=10**6, bytes_accessed=2**20, transcendentals=0),
        name="finish",
    )(shares, weight_in, gain)


def per_device(
    token_ids, embed_table, subspace, adapter_in, adapter_out, norm_gain, coef_cotangent
):
    tokens = token_ids.shape[0]
    zl, x = lax.axis_index(ZL), lax.axis_index(X)
    shards = lax.axis_size(DP)
    group = lax.axis_size(GATHER)
    section = lax.axis_index(SEC)
    me = jnp.reshape(section, (1,)).astype(jnp.int32)
    dp = lax.axis_index(DP)
    vocab, cols = embed_table.shape
    basis, weight_in, weight_out = subspace[0], adapter_in[0], adapter_out[0]
    d, r = basis.shape
    h = weight_in.shape[1]
    block = d // shards

    x_at = jnp.reshape(x, (1,)).astype(jnp.int32)
    place, requests, rows_x = request(
        x_at, token_ids.reshape(1, tokens), basis.reshape(8, 4, 2 * block, r), vocab, shards
    )
    prev_x = lax.ppermute(rows_x, SEC, [(0, 1), (1, 2), (2, 3)])
    asked = lax.all_to_all(requests, DP, split_axis=0, concat_axis=0, tiled=True)
    found = pick_rows(asked, embed_table, (prev_x,))
    answered = lax.all_to_all(found, DP, split_axis=0, concat_axis=0, tiled=True)

    crossed = cross_products(x_at, basis, weight_in, norm_gain, prev_x, found)
    gained, own = weights(basis, weight_in, norm_gain, weight_out, (crossed,))
    owns = gather_peers(own)
    crossed = sum_over_x(crossed, own)
    mats = gather_peers(crossed)

    part, turned = place_rows(place, answered, group, (crossed,))
    turned = ordered(turned, mats[2])
    pieces = gather_peers(part)
    turned = lax.all_to_all(turned, GATHER, split_axis=0, concat_axis=0, tiled=True)
    pq, square = project(me, pieces, basis, gained, turned, mats[2])
    pqs = gather_peers(pq)
    turned = gather_peers(turned.reshape(group * tokens, cols // group))

    sent, packed = chain(me, coef_cotangent, square, pqs, owns, mats, d, group)
    packed = lax.all_to_all(packed, GATHER, split_axis=0, concat_axis=0, tiled=True)
    rows_own = lax.dynamic_index_in_dim(rows_x.reshape(4, 2, 2 * block, r), zl, 1, False)
    rows_prev = lax.dynamic_index_in_dim(prev_x.reshape(4, 2, 2 * block, r), zl, 1, False)
    shares = share(me, packed, turned, rows_own, rows_prev)
    shares = lax.all_to_all(shares, REDUCE, split_axis=0, concat_axis=0, tiled=True)
    in_block = lax.dynamic_slice_in_dim(weight_in, dp * block, block, 0)
    gain_block = lax.dynamic_slice_in_dim(norm_gain, dp * block, block, 1)
    grad_in, grad_out, grad_gain = finish(shares, in_block, gain_block)
    return sent[None], grad_in[None], grad_out[None], grad_gain


def solution(mesh):
    fine = Mesh(mesh.devices.reshape(2, 2, 4, 2, 4, 2), (YL, CO, ZH, ZL, X, YH))
    return jax.shard_map(
        per_device,
        mesh=fine,
        in_specs=(
            P(DP),
            P(DP, SEC),
            P(SEC, None, None),
            P(SEC, None, None),
            P(SEC, None, None),
            P(SEC, None),
            P(DP, None),
        ),
        out_specs=(
            P(SEC, DP, None),
            P(SEC, DP, None),
            P(SEC, None, DP),
            P(SEC, DP),
        ),
        check_vma=False,
    )
```

```python
import functools

import jax
import jax.numpy as jnp
from jax import lax
from jax.experimental import pallas as pl
from jax.experimental.pallas import tpu as pltpu
from jax.sharding import Mesh, PartitionSpec as P

CAP = 4
EPSILON = 1e-05
GRANT = 63 * 2**20
F32, BF16 = jnp.float32, jnp.bfloat16
YL, CO, ZH, ZL, X, YH = "yl", "co", "zh", "zl", "x", "yh"
DP = (ZH, ZL, X, YH)
SEC = (YL, CO)
GATHER = (ZL, X)
REDUCE = (ZH, YH)


def dot_nn(a, b):
    return lax.dot_general(a, b, (((1,), (0,)), ((), ())), preferred_element_type=F32)


def dot_nt(a, b):
    return lax.dot_general(a, b, (((1,), (1,)), ((), ())), preferred_element_type=F32)


def dot_tn(a, b):
    return lax.dot_general(a, b, (((0,), (0,)), ((), ())), preferred_element_type=F32)


def swap(x, axis):
    return lax.ppermute(x, axis, [(0, 1), (1, 0)])


def gather_peers(x):
    across = swap(x, YL)
    beside = swap(x, CO)
    return x, beside, across, swap(across, CO)


def full(shape):
    return pl.BlockSpec(shape, lambda *_: (0,) * len(shape))


def ordered(x, after):
    hbm = pl.BlockSpec(memory_space=pl.ANY)
    return pl.pallas_call(
        lambda *refs: None,
        in_specs=[hbm, hbm],
        out_specs=hbm,
        out_shape=jax.ShapeDtypeStruct(x.shape, x.dtype),
        input_output_aliases={0: 0},
        name="ordered",
    )(x, after)


def weights_kernel(basis, weight_in, gain, weight_out, *refs):
    gained, own, acc = refs[-3:]
    step = pl.program_id(0)
    h = weight_in.shape[1]

    @pl.when(step == 0)
    def _():
        acc[...] = jnp.zeros_like(acc)

    part = basis[...]
    gained[...] = scaled(weight_in[...], gain[...])
    acc[0:h, :] += dot_nn(weight_out[...], part)
    acc[h:, :] += dot_tn(part, part)

    @pl.when(step == pl.num_programs(0) - 1)
    def _():
        own[...] = acc[...].astype(BF16)


def weights(basis, weight_in, gain, weight_out, afters):
    d, r = basis.shape
    h = weight_in.shape[1]
    steps = 4
    rows = d // steps
    return pl.pallas_call(
        weights_kernel,
        grid=(steps,),
        in_specs=[
            pl.BlockSpec((rows, r), lambda k: (k, 0)),
            pl.BlockSpec((rows, h), lambda k: (k, 0)),
            pl.BlockSpec((1, rows), lambda k: (0, k)),
            pl.BlockSpec((h, rows), lambda k: (0, k)),
        ]
        + [pl.BlockSpec(memory_space=pl.ANY)] * len(afters),
        out_specs=[pl.BlockSpec((rows, h), lambda k: (k, 0)), full((r + h, r))],
        out_shape=[
            jax.ShapeDtypeStruct((d, h), BF16),
            jax.ShapeDtypeStruct((r + h, r), BF16),
        ],
        scratch_shapes=[pltpu.VMEM((r + h, r), F32)],
        compiler_params=pltpu.CompilerParams(vmem_limit_bytes=GRANT),
        cost_estimate=pl.CostEstimate(
            flops=2 * d * r * (r + h), bytes_accessed=4 * d * (r + h), transcendentals=0
        ),
        name="weights",
    )(basis, weight_in, gain, weight_out, *afters)


def scaled(rows, gain):
    column = jnp.broadcast_to(gain, (8, rows.shape[0])).T[:, 0:1]
    return (rows.astype(F32) * column).astype(BF16)


def cross_kernel(at, basis, weight_in, gain, prev, after, out, mine, ins, theirs, sems):
    blocks, rows, r = theirs.shape
    wait_all(
        start_all(
            [
                pltpu.make_async_copy(prev, theirs, sems.at[0]),
                pltpu.make_async_copy(basis.at[:, at[0]], mine, sems.at[1]),
                pltpu.make_async_copy(weight_in.at[:, at[0]], ins, sems.at[2]),
            ]
        )
    )
    first, second = 0.0, 0.0
    for k in range(blocks):
        start = pl.multiple_of((k * 4 + at[0]) * rows, rows)
        first = first + dot_tn(theirs[k], mine[k])
        second = second + dot_tn(theirs[k], scaled(ins[k], gain[:, pl.ds(start, rows)]))
    out[:, 0:r] = first.astype(BF16)
    out[:, r:] = second.astype(BF16)


def cross_products(at, basis, weight_in, gain, prev, after):
    blocks, rows, r = prev.shape
    h = weight_in.shape[1]
    hbm = pl.BlockSpec(memory_space=pl.ANY)
    return pl.pallas_call(
        cross_kernel,
        in_specs=[pl.BlockSpec(memory_space=pltpu.SMEM), hbm, hbm, full(gain.shape), hbm, hbm],
        out_specs=full((r, r + h)),
        out_shape=jax.ShapeDtypeStruct((r, r + h), BF16),
        scratch_shapes=[
            pltpu.VMEM((blocks, rows, r), BF16),
            pltpu.VMEM((blocks, rows, h), BF16),
            pltpu.VMEM((blocks, rows, r), BF16),
            pltpu.SemaphoreType.DMA((3,)),
        ],
        compiler_params=pltpu.CompilerParams(vmem_limit_bytes=GRANT),
        cost_estimate=pl.CostEstimate(
            flops=2 * blocks * rows * r * (r + h),
            bytes_accessed=2 * blocks * rows * (2 * r + h),
            transcendentals=0,
        ),
        name="cross_products",
    )(at, basis.reshape(blocks, 4, rows, r), weight_in.reshape(blocks, 4, rows, h), gain, prev, after)


def sum_kernel(a, b, c, d, after, out):
    total = a[...].astype(F32) + b[...].astype(F32) + c[...].astype(F32) + d[...].astype(F32)
    out[...] = total.astype(BF16)


def sum_over_x(v, after):
    parts = [v] + [lax.ppermute(v, X, [(i, (i + k) % 4) for i in range(4)]) for k in (1, 2, 3)]
    return pl.pallas_call(
        sum_kernel,
        in_specs=[full(v.shape)] * 4 + [pl.BlockSpec(memory_space=pl.ANY)],
        out_specs=full(v.shape),
        out_shape=jax.ShapeDtypeStruct(v.shape, BF16),
        compiler_params=pltpu.CompilerParams(vmem_limit_bytes=GRANT),
        cost_estimate=pl.CostEstimate(flops=4 * v.size, bytes_accessed=10 * v.size, transcendentals=0),
        name="sum_over_x",
    )(*parts, after)


def start_all(copies):
    for copy in copies:
        copy.start()
    return copies


def wait_all(copies):
    for copy in copies:
        copy.wait()


def one_hot(column, n):
    lanes = lax.broadcasted_iota(jnp.int32, (column.shape[0], n), 1)
    return (column == lanes).astype(F32)


def split_int(v):
    return (v // 128).astype(F32).astype(BF16), (v % 128).astype(F32).astype(BF16)


def request_kernel(vocab, at, ids, basis, place, requests, rows, sem):
    copy = pltpu.make_async_copy(basis.at[:, at[0]], rows, sem)
    copy.start()
    tokens, shards = ids.shape[1], requests.shape[0]
    column = jnp.broadcast_to(ids[...], (8, tokens)).T[:, 0:1]
    first = lax.broadcasted_iota(jnp.int32, (tokens, shards), 1) * vocab
    mine = (column >= first) & (column < first + vocab)
    matches = mine.astype(F32)
    local = jnp.sum(jnp.where(mine, column - first, 0), axis=1, keepdims=True)
    owner = jnp.sum(jnp.where(mine, first // vocab, 0), axis=1, keepdims=True)
    earlier = lax.broadcasted_iota(jnp.int32, (tokens, tokens), 0) > lax.broadcasted_iota(
        jnp.int32, (tokens, tokens), 1
    )
    half = matches.astype(BF16)
    before = dot_nn(earlier.astype(F32).astype(BF16), half)
    position = jnp.sum(matches * before, axis=1, keepdims=True).astype(jnp.int32)
    place[...] = owner * CAP + position
    slot = one_hot(position, 128)
    high, low = split_int(local)
    found = 128.0 * dot_tn(half, (slot * high.astype(F32)).astype(BF16))
    found = found + dot_tn(half, (slot * low.astype(F32)).astype(BF16))
    requests[...] = found[:, 0:CAP].astype(jnp.int32)
    copy.wait()


def request(at, ids, basis, vocab, shards):
    tokens = ids.shape[1]
    blocks, _, rows, r = basis.shape
    hbm = pl.BlockSpec(memory_space=pl.ANY)
    return pl.pallas_call(
        functools.partial(request_kernel, vocab),
        in_specs=[pl.BlockSpec(memory_space=pltpu.SMEM), full(ids.shape), hbm],
        out_specs=[full((tokens, 1)), full((shards, CAP)), full((blocks, rows, r))],
        out_shape=[
            jax.ShapeDtypeStruct((tokens, 1), jnp.int32),
            jax.ShapeDtypeStruct((shards, CAP), jnp.int32),
            jax.ShapeDtypeStruct((blocks, rows, r), BF16),
        ],
        scratch_shapes=[pltpu.SemaphoreType.DMA],
        compiler_params=pltpu.CompilerParams(vmem_limit_bytes=GRANT),
        cost_estimate=pl.CostEstimate(flops=10**7, bytes_accessed=2**21, transcendentals=0),
        name="request",
    )(at, ids, basis)


def pick_kernel(asked, table, *refs):
    out, hot, rows, found, in_sems, out_sems = refs[-6:]
    shards, cap = asked.shape
    slots, vocab = hot.shape
    steps, _, width = rows.shape
    ins = [
        pltpu.make_async_copy(table.at[:, pl.ds(k * width, width)], rows.at[k], in_sems.at[k])
        for k in range(steps)
    ]
    outs = [
        pltpu.make_async_copy(found.at[k], out.at[:, :, pl.ds(k * width, width)], out_sems.at[k])
        for k in range(steps)
    ]
    for copy in ins:
        copy.start()
    peer = lax.broadcasted_iota(jnp.int32, (slots, shards), 0) // cap
    peer = (peer == lax.broadcasted_iota(jnp.int32, (slots, shards), 1)).astype(F32).astype(BF16)
    high, low = split_int(asked[...])
    spread = 128.0 * dot_nn(peer, high) + dot_nn(peer, low)
    slot = lax.broadcasted_iota(jnp.int32, (slots, cap), 0) % cap
    keep = slot == lax.broadcasted_iota(jnp.int32, (slots, cap), 1)
    column = jnp.sum(jnp.where(keep, spread, 0.0), axis=1, keepdims=True)
    hot[...] = one_hot(column.astype(jnp.int32), vocab).astype(BF16)
    for k in range(steps):
        ins[k].wait()
        found[k] = dot_nn(hot[...], rows[k]).astype(BF16).reshape(shards, cap, width)
        outs[k].start()
    for copy in outs:
        copy.wait()


def pick_rows(asked, table, firsts):
    shards, cap = asked.shape
    vocab, cols = table.shape
    slots = shards * cap
    steps = 4
    width = cols // steps
    return pl.pallas_call(
        pick_kernel,
        in_specs=[full(asked.shape), pl.BlockSpec(memory_space=pl.ANY)]
        + [pl.BlockSpec(memory_space=pl.ANY)] * len(firsts),
        out_specs=pl.BlockSpec(memory_space=pl.ANY),
        out_shape=jax.ShapeDtypeStruct((shards, cap, cols), BF16),
        scratch_shapes=[
            pltpu.VMEM((slots, vocab), BF16),
            pltpu.VMEM((steps, vocab, width), BF16),
            pltpu.VMEM((steps, shards, cap, width), BF16),
            pltpu.SemaphoreType.DMA((steps,)),
            pltpu.SemaphoreType.DMA((steps,)),
        ],
        compiler_params=pltpu.CompilerParams(vmem_limit_bytes=GRANT),
        cost_estimate=pl.CostEstimate(
            flops=2 * slots * vocab * cols, bytes_accessed=2 * cols * (vocab + slots), transcendentals=0
        ),
        name="pick_rows",
    )(asked, table, *firsts)


def place_kernel(place, answered, *refs):
    part, turned = refs[-2:]
    shards, cap, cols = answered.shape
    width = turned.shape[2]
    put = one_hot(place[...], shards * cap).astype(BF16)
    for t in range(turned.shape[0]):
        rows = answered[:, :, t * width : (t + 1) * width].reshape(shards * cap, width)
        rows = dot_nn(put, rows).astype(BF16)
        part[:, t * width : (t + 1) * width] = rows
        turned[t] = rows


def place_rows(place, answered, copies, firsts):
    tokens = place.shape[0]
    shards, cap, cols = answered.shape
    return pl.pallas_call(
        place_kernel,
        in_specs=[full(place.shape), full(answered.shape)] + [pl.BlockSpec(memory_space=pl.ANY)] * len(firsts),
        out_specs=[full((tokens, cols)), full((copies, tokens, cols // copies))],
        out_shape=[
            jax.ShapeDtypeStruct((tokens, cols), BF16),
            jax.ShapeDtypeStruct((copies, tokens, cols // copies), BF16),
        ],
        compiler_params=pltpu.CompilerParams(vmem_limit_bytes=GRANT),
        cost_estimate=pl.CostEstimate(
            flops=2 * shards * cap * tokens * cols,
            bytes_accessed=2 * cols * (shards * cap + 2 * tokens),
            transcendentals=0,
        ),
        name="place_rows",
    )(place, answered, *firsts)


def project_kernel(me, p0, p1, p2, p3, basis, gained, first, second, out, square):
    step = pl.program_id(0)
    r = basis.shape[1]
    for k, piece in enumerate((p0, p1, p2, p3)):

        @pl.when(step == k)
        def _(k=k, piece=piece):
            x = piece[...]
            xf = x.astype(F32)
            q = jnp.broadcast_to(jnp.sum(xf * xf, axis=1, keepdims=True), square.shape)
            a, b = dot_nn(x, basis[...]), dot_nn(x, gained[...])
            if k == 0:
                out[:, 0:r] = a
                out[:, r:] = b
                square[...] = q
            else:
                out[:, 0:r] += a
                out[:, r:] += b
                square[...] += q


def project(me, pieces, basis, gained, first, second):
    tokens, cols = pieces[0].shape
    r, h = basis.shape[1], gained.shape[1]
    return pl.pallas_call(
        project_kernel,
        grid_spec=pltpu.PrefetchScalarGridSpec(
            num_scalar_prefetch=1,
            grid=(4,),
            in_specs=[full((tokens, cols))] * 4
            + [
                pl.BlockSpec((cols, r), lambda k, me: (k ^ me[0], 0)),
                pl.BlockSpec((cols, h), lambda k, me: (k ^ me[0], 0)),
                pl.BlockSpec(memory_space=pl.ANY),
                pl.BlockSpec(memory_space=pl.ANY),
            ],
            out_specs=[full((tokens, r + h)), full((tokens, 128))],
        ),
        out_shape=[
            jax.ShapeDtypeStruct((tokens, r + h), F32),
            jax.ShapeDtypeStruct((tokens, 128), F32),
        ],
        compiler_params=pltpu.CompilerParams(vmem_limit_bytes=GRANT),
        cost_estimate=pl.CostEstimate(
            flops=8 * tokens * cols * (r + h), bytes_accessed=8 * cols * (r + h + tokens), transcendentals=0
        ),
        name="project",
    )(me, *pieces, basis, gained, first, second)


def chain_kernel(width, me_ref, cot, square, q0, q1, q2, q3, g0, g1, g2, g3, m0, m1, m2, m3, sent, packed,
                 pq, owns, mats, pres, acts, coefs, spans, invs, ins, ws):
    me = me_ref[0]
    r = cot.shape[1]
    h = q0.shape[1] - r
    for k, (q, g, m) in enumerate(((q0, g0, m0), (q1, g1, m1), (q2, g2, m2), (q3, g3, m3))):
        pq[k ^ me] = q[...]
        owns[k ^ me] = g[...]
        mats[k ^ me] = m[...]
    squares = square[:, 0:1]
    coefs[0] = jnp.zeros_like(coefs[0])
    for s in range(4):
        base_in = pq[s, :, r:]
        if s == 0:
            inv = lax.rsqrt(squares * (1.0 / width) + EPSILON)
            pre = inv * base_in
        else:
            c = coefs[s]
            base_sub = pq[s - 1, :, 0:r]
            span = base_sub + dot_nn(c, owns[s - 1, h:, :])
            total = squares + jnp.sum(c.astype(F32) * (base_sub + span), axis=1, keepdims=True)
            inv = lax.rsqrt(jnp.maximum(total, 0.0) * (1.0 / width) + EPSILON)
            pre = inv * (base_in + dot_nn(c, mats[s, :, r:]))
            spans[s] = span
        invs[s] = jnp.broadcast_to(inv, invs.shape[1:])
        pres[s] = pre
        act = (pre / (1.0 + jnp.exp(-pre))).astype(BF16)
        acts[s] = act
        new = dot_nn(act, owns[s, 0:h, :])
        if s > 0:
            new = new + dot_nn(c, mats[s, :, 0:r])
        coefs[s + 1] = new.astype(BF16)
    arrived = cot[...]
    for s in (3, 2, 1, 0):
        ins[s] = arrived
        pre = pres[s]
        sg = 1.0 / (1.0 + jnp.exp(-pre))
        gp = dot_nt(arrived, owns[s, 0:h, :]) * sg * (1.0 + pre * (1.0 - sg))
        inv = invs[s, :, 0:1]
        ws[s] = (gp * inv).astype(BF16)
        if s > 0:
            mean = jnp.sum(gp * pre, axis=1, keepdims=True) * (1.0 / width)
            back = dot_nt(gp.astype(BF16), mats[s, :, r:]) - (inv * mean) * spans[s]
            arrived = (dot_nt(arrived, mats[s, :, 0:r]) + inv * back).astype(BF16)
    sent[...] = coefs[me + 1]
    w = ws[me]
    row = (w, dot_tn(acts[me], ins[me]).astype(BF16), dot_tn(w, coefs[me]).astype(BF16))
    for t in range(packed.shape[0]):
        at = 0
        for v in row:
            packed[t, :, at : at + v.shape[1]] = v
            at += v.shape[1]


def chain(me, cot, square, pq, owns, mats, width, copies):
    tokens, r = cot.shape
    h = pq[0].shape[1] - r
    vmem = pl.BlockSpec(memory_space=pltpu.VMEM)
    return pl.pallas_call(
        functools.partial(chain_kernel, width),
        in_specs=[pl.BlockSpec(memory_space=pltpu.SMEM)] + [vmem] * 14,
        out_specs=[vmem, vmem],
        out_shape=[
            jax.ShapeDtypeStruct((tokens, r), BF16),
            jax.ShapeDtypeStruct((copies, tokens, h + 2 * r), BF16),
        ],
        scratch_shapes=[
            pltpu.VMEM((4, tokens, r + h), F32),
            pltpu.VMEM((4,) + owns[0].shape, BF16),
            pltpu.VMEM((4,) + mats[0].shape, BF16),
            pltpu.VMEM((4, tokens, h), F32),
            pltpu.VMEM((4, tokens, h), BF16),
            pltpu.VMEM((5, tokens, r), BF16),
            pltpu.VMEM((4, tokens, r), F32),
            pltpu.VMEM((4, tokens, 128), F32),
            pltpu.VMEM((4, tokens, r), BF16),
            pltpu.VMEM((4, tokens, h), BF16),
        ],
        compiler_params=pltpu.CompilerParams(vmem_limit_bytes=32 * 2**20),
        cost_estimate=pl.CostEstimate(flops=4 * 10**9, bytes_accessed=6 * 2**20, transcendentals=10**6),
        name="chain",
    )(me, cot, square, *pq, *owns, *mats)


def share_kernel(me_ref, packed, t0, t1, t2, t3, rows_own, rows_prev, out):
    me = me_ref[0]
    group, tokens, wide = packed.shape
    r = rows_own.shape[2]
    h = wide - 2 * r
    both = packed[0, :, h:].astype(F32)
    for g in range(1, group):
        both = both + packed[g, :, h:].astype(F32)
    v, uh = both[:, 0:r], both[:, r:].astype(BF16)
    vh = v.astype(BF16)
    vl = (v - vh.astype(F32)).astype(BF16)
    wt = jnp.concatenate([packed[g, :, 0:h].astype(F32).T.astype(BF16) for g in range(group)], axis=1)
    for k, piece in enumerate((t0, t1, t2, t3)):
        c = k ^ me
        xs = (dot_nn(wt, piece[...]) + dot_nt(uh, rows_prev[c])).astype(BF16)
        own = rows_own[c]
        os = (dot_nt(vh, own) + dot_nt(vl, own)).astype(BF16)
        n = xs.shape[1] // 2
        for e in range(2):
            out[2 * c + e, 0:h, :] = xs[:, e * n : (e + 1) * n]
            out[2 * c + e, h:, :] = os[:, e * n : (e + 1) * n]


def share(me, packed, pieces, rows_own, rows_prev):
    h = packed.shape[2] - 2 * rows_own.shape[2]
    cs, n, _ = rows_own.shape
    vmem = pl.BlockSpec(memory_space=pltpu.VMEM)
    return pl.pallas_call(
        share_kernel,
        in_specs=[pl.BlockSpec(memory_space=pltpu.SMEM)] + [vmem] * 7,
        out_specs=vmem,
        out_shape=jax.ShapeDtypeStruct((2 * cs, 2 * h, n // 2), BF16),
        compiler_params=pltpu.CompilerParams(vmem_limit_bytes=32 * 2**20),
        cost_estimate=pl.CostEstimate(flops=2 * 10**9, bytes_accessed=6 * 2**20, transcendentals=0),
        name="share",
    )(me, packed, *pieces, rows_own, rows_prev)


def finish_kernel(arrived, weight_in, gain, grad_in, grad_out, grad_gain, shares, sem):
    h = shares.shape[1] // 2
    copy = pltpu.make_async_copy(arrived, shares, sem)
    copy.start()
    copy.wait()
    total = jnp.sum(shares[...].astype(F32), axis=0)
    plain = total[0:h]
    grad_out[...] = total[h:]
    grad_in[...] = (plain * gain[...]).T
    grad_gain[...] = jnp.sum(plain * weight_in[...].astype(F32).T, axis=0, keepdims=True)


def finish(shares, weight_in, gain):
    _, twice, n = shares.shape
    h = twice // 2
    return pl.pallas_call(
        finish_kernel,
        in_specs=[pl.BlockSpec(memory_space=pl.ANY), full((n, h)), full((1, n))],
        out_specs=[full((n, h)), full((h, n)), full((1, n))],
        out_shape=[
            jax.ShapeDtypeStruct((n, h), F32),
            jax.ShapeDtypeStruct((h, n), F32),
            jax.ShapeDtypeStruct((1, n), F32),
        ],
        scratch_shapes=[pltpu.VMEM(shares.shape, BF16), pltpu.SemaphoreType.DMA],
        compiler_params=pltpu.CompilerParams(vmem_limit_bytes=16 * 2**20),
        cost_estimate=pl.CostEstimate(flops=10**6, bytes_accessed=2**20, transcendentals=0),
        name="finish",
    )(shares, weight_in, gain)


def per_device(
    token_ids, embed_table, subspace, adapter_in, adapter_out, norm_gain, coef_cotangent
):
    tokens = token_ids.shape[0]
    zl, x = lax.axis_index(ZL), lax.axis_index(X)
    shards = lax.axis_size(DP)
    group = lax.axis_size(GATHER)
    section = lax.axis_index(SEC)
    me = jnp.reshape(section, (1,)).astype(jnp.int32)
    dp = lax.axis_index(DP)
    vocab, cols = embed_table.shape
    basis, weight_in, weight_out = subspace[0], adapter_in[0], adapter_out[0]
    d, r = basis.shape
    h = weight_in.shape[1]
    block = d // shards

    x_at = jnp.reshape(x, (1,)).astype(jnp.int32)
    place, requests, rows_x = request(
        x_at, token_ids.reshape(1, tokens), basis.reshape(8, 4, 2 * block, r), vocab, shards
    )
    prev_x = lax.ppermute(rows_x, SEC, [(0, 1), (1, 2), (2, 3)])
    asked = lax.all_to_all(requests, DP, split_axis=0, concat_axis=0, tiled=True)
    found = pick_rows(asked, embed_table, (prev_x,))
    answered = lax.all_to_all(found, DP, split_axis=0, concat_axis=0, tiled=True)

    crossed = cross_products(x_at, basis, weight_in, norm_gain, prev_x, found)
    gained, own = weights(basis, weight_in, norm_gain, weight_out, (crossed,))
    owns = gather_peers(own)
    crossed = sum_over_x(crossed, own)
    mats = gather_peers(crossed)

    part, turned = place_rows(place, answered, group, (crossed,))
    turned = ordered(turned, mats[2])
    pieces = gather_peers(part)
    turned = lax.all_to_all(turned, GATHER, split_axis=0, concat_axis=0, tiled=True)
    pq, square = project(me, pieces, basis, gained, turned, mats[2])
    pqs = gather_peers(pq)
    turned = gather_peers(turned.reshape(group * tokens, cols // group))

    sent, packed = chain(me, coef_cotangent, square, pqs, owns, mats, d, group)
    packed = lax.all_to_all(packed, GATHER, split_axis=0, concat_axis=0, tiled=True)
    rows_own = lax.dynamic_index_in_dim(rows_x.reshape(4, 2, 2 * block, r), zl, 1, False)
    rows_prev = lax.dynamic_index_in_dim(prev_x.reshape(4, 2, 2 * block, r), zl, 1, False)
    shares = share(me, packed, turned, rows_own, rows_prev)
    shares = lax.all_to_all(shares, REDUCE, split_axis=0, concat_axis=0, tiled=True)
    in_block = lax.dynamic_slice_in_dim(weight_in, dp * block, block, 0)
    gain_block = lax.dynamic_slice_in_dim(norm_gain, dp * block, block, 1)
    grad_in, grad_out, grad_gain = finish(shares, in_block, gain_block)
    return sent[None], grad_in[None], grad_out[None], grad_gain


def solution(mesh):
    fine = Mesh(mesh.devices.reshape(2, 2, 4, 2, 4, 2), (YL, CO, ZH, ZL, X, YH))
    return jax.shard_map(
        per_device,
        mesh=fine,
        in_specs=(
            P(DP),
            P(DP, SEC),
            P(SEC, None, None),
            P(SEC, None, None),
            P(SEC, None, None),
            P(SEC, None),
            P(DP, None),
        ),
        out_specs=(
            P(SEC, DP, None),
            P(SEC, DP, None),
            P(SEC, None, DP),
            P(SEC, DP),
        ),
        check_vma=False,
    )
```
